32 devices in a mesh: head: 4 (over z), blk: 8 (over y, x, core).
Axes of the slice: x: 2, y: 2, z: 4, core: 2. Of those that a mesh axis runs over, the one named last changes fastest.
Arguments:
- inputs: bfloat16 [4096, 1024], P(('head', 'blk')), may hold values from -6 to 6
- attn_gain: bfloat16 [1024], P(('head', 'blk')), may hold values from 0.5 to 1.5
- attn_qkv: bfloat16 [1024, 3072], P(('head', 'blk')), may hold values from -0.1875 to 0.1875
- attn_out: bfloat16 [1024, 1024], P(('head', 'blk')), may hold values from -2 to 2
- memory_gain: bfloat16 [1024], P(('head', 'blk')), may hold values from 0.5 to 1.5
- memory_query: bfloat16 [1024, 4096], P(('head', 'blk')), may hold values from -0.1875 to 0.1875
- sub_keys: bfloat16 [2048, 512], P(('head', 'blk')), may hold values from -0.25 to 0.25
- memory_gate: bfloat16 [1024, 1024], P(('head', 'blk')), may hold values from -0.1875 to 0.1875
- memory_out: bfloat16 [1024, 1024], P(('head', 'blk')), may hold values from -0.375 to 0.375
- memory_values: bfloat16 [65536, 1024], P(('head', 'blk')), may hold values from -6 to 6
- doc_lengths: int32 [3], replicated, may hold values from 512 to 2048, as said below
- token_order: int32 [4096], replicated, may hold values from 0 to 4095, as said below
- memory_picks: int32 [4096, 4, 32, 2], P(('head', 'blk')), may hold values from 0 to 255, as said below
- cotangent: bfloat16 [4096, 1024], P(('head', 'blk')), may hold values from -6 to 6
Outputs:
- output: bfloat16 [4096, 1024], P(('head', 'blk'))
- grad_inputs: float32 [4096, 1024], P(('head', 'blk'))
- grad_attn_gain: float32 [1024], P(('head', 'blk'))
- grad_attn_qkv: float32 [1024, 3072], P(('head', 'blk'))
- grad_attn_out: float32 [1024, 1024], P(('head', 'blk'))
- grad_memory_gain: float32 [1024], P(('head', 'blk'))
- grad_memory_query: float32 [1024, 4096], P(('head', 'blk'))
- grad_sub_keys: float32 [2048, 512], P(('head', 'blk'))
- grad_memory_gate: float32 [1024, 1024], P(('head', 'blk'))
- grad_memory_out: float32 [1024, 1024], P(('head', 'blk'))
- grad_memory_values: float32 [65536, 1024], P(('head', 'blk'))
The draws below stay inside these ranges and needn't reach their ends.
Inputs may be any that keep to these rules, and one draw needn't show every extreme that they name: `doc_lengths`: the entries sum to 4096; each is 512 or more, and one is exactly 2048. `token_order`: A permutation of the tokens. Dealt slots lie in blocks of 128, one block a device in the order of head, then blk, and tokens lie likewise in blocks of 128 in order. The block of device (g, b) holds, for each device (g, b2) of the same head index in blk order, exactly 128 / 8 of the tokens of b2's block. `memory_picks`: each entry is a pair (first, second) naming value row first * 256 + second. The value rows lie in order in 32 equal slices of 2048, one a device in the order of head, then blk. Of the picks of the dealt slots of one device (aligned blocks of 128 slots) at most 1024 name rows of any one slice, and in every draw some slice receives exactly 1024 from every device.
All inputs are finite; a program needn't handle non-finite values.
Results may differ from the reference program's by a relative error of at most 0.035.
Values may be sent and summed in bfloat16 or wider, within the bound.
No kernel may reach another device: no remote copies, remote signals or barrier semaphores. Data moves between devices by JAX's collectives and lax.ppermute only.
A program may use at most 320 MiB of HBM per device.

```python
import jax
import jax.numpy as jnp
from jax import lax

D = 1024
NH = 16
HD = 64
MH = 4
QHALF = 512
NSUB = 256
KPICK = 32
TOK_DEV = 128
MINLEN = 512
NDEV = 32
TOKENS = 4096
LONGEST = 2048
NDOC = 3
VROWS = 65536
OWN_ROWS = 2048
N_HEAD = 4
N_BLK = 8


def permute_one(order_seed, owner_row):
    return jax.random.permutation(order_seed, owner_row)


def shuffle_rows(order_seed):
    return jax.random.permutation(order_seed, jnp.arange(TOK_DEV, dtype=jnp.int32))


def draw_doc_lengths(key, part):
    key = jax.random.fold_in(key, 5)
    spare = TOKENS - LONGEST - (NDOC - 1) * MINLEN
    cut_seed, place_seed = jax.random.split(key, 2)
    cuts = jnp.sort(jax.random.randint(cut_seed, (NDOC - 2,), 0, spare + 1))
    edges = jnp.concatenate([jnp.zeros((1,), jnp.int32), cuts.astype(jnp.int32), jnp.full((1,), spare, jnp.int32)])
    others = MINLEN + edges[1:] - edges[:-1]
    place = jax.random.randint(place_seed, (), 0, NDOC)
    slots = jnp.arange(NDOC, dtype=jnp.int32)
    lower = others[jnp.clip(slots, 0, NDOC - 2)]
    upper = others[jnp.clip(slots - 1, 0, NDOC - 2)]
    lengths = jnp.where(slots < place, lower, jnp.where(slots == place, LONGEST, upper))
    return lengths.astype(jnp.int32)


def draw_token_order(key, part):
    key = jax.random.fold_in(key, 9)
    share = TOK_DEV // N_BLK
    orders = jax.vmap(shuffle_rows)(jax.random.split(key, NDEV))
    anchor = jnp.arange(NDEV, dtype=jnp.int32)[:, None] * TOK_DEV + orders
    laid = anchor.reshape(N_HEAD, N_BLK, N_BLK, share)
    return jnp.transpose(laid, (0, 2, 1, 3)).reshape(TOKENS).astype(jnp.int32)


def draw_memory_picks(key, part):
    key = jax.random.fold_in(key, 7)
    per_device = TOK_DEV * MH * KPICK
    mean_load = per_device // NDEV
    first_seed, shift_seed, order_seed, within_seed = jax.random.split(key, 4)
    target = jax.random.randint(first_seed, (), 0, NDEV)
    shifts = jax.random.randint(shift_seed, (NDEV,), 0, NDEV // 4)
    relative = (jnp.arange(NDEV)[None, :] - target + shifts[:, None]) % NDEV
    loads = jnp.where(relative < NDEV // 4, 2 * mean_load, jnp.where(relative < NDEV // 2, mean_load, mean_load // 2))
    bounds = jnp.cumsum(loads, axis=1)
    places = jnp.arange(per_device)

    def owners_of(bound_row):
        return jnp.searchsorted(bound_row, places, side='right')
    owners = jax.vmap(owners_of)(bounds).astype(jnp.int32)
    shuffled = jax.vmap(permute_one)(jax.random.split(order_seed, NDEV), owners)
    within = jax.random.randint(within_seed, (NDEV, per_device), 0, OWN_ROWS)
    value_rows = (shuffled * OWN_ROWS + within).reshape(TOKENS, MH, KPICK)
    return jnp.stack([value_rows // NSUB, value_rows % NSUB], axis=-1).astype(jnp.int32)


def block_scale(stream_key, shape, cuts, least, top_value):
    def one(dim, blocks):
        draws = jax.random.uniform(jax.random.fold_in(jax.random.fold_in(stream_key, 6), dim), (blocks,), jnp.float32, least / len(cuts), top_value / len(cuts))
        return jnp.repeat(jnp.exp(draws), shape[dim] // blocks).reshape((-1,) + (1,) * (len(shape) - dim - 1))

    level = one(*cuts[0])
    for cut in cuts[1:]:
        level = level * one(*cut)
    return level


def bell_draw(key, extent, width, reach, shards=(), kind=jnp.bfloat16):
    entries = jax.random.normal(key, extent, jnp.float32) * width
    if len(shards) > 0:
        entries = block_scale(key, extent, shards, -0.22, 0.18) * entries
    return jnp.clip(entries, min=-reach, max=reach).astype(kind)


def setup_inputs(seed: int = 0) -> dict:
    keys = jax.random.split(jax.random.key(seed), 15)
    return {
        "inputs": bell_draw(keys[0], (TOKENS, D), 1.0, 6.0, ((0, 32),)),
        "attn_gain": jnp.clip(1.0 + 0.1 * jax.random.normal(keys[1], (D,), jnp.float32), 0.5, 1.5).astype(jnp.bfloat16),
        "attn_qkv": bell_draw(keys[2], (D, 3 * NH * HD), D ** -0.5, 0.1875, ((0, 32),)),
        "attn_out": bell_draw(keys[3], (NH * HD, D), (D // 128) ** -0.5, 2.0, ((0, 32),)),
        "memory_gain": jnp.clip(1.0 + 0.1 * jax.random.normal(keys[4], (D,), jnp.float32), 0.5, 1.5).astype(jnp.bfloat16),
        "memory_query": bell_draw(keys[5], (D, MH * 2 * QHALF), D ** -0.5, 0.1875, ((0, 32),)),
        "sub_keys": bell_draw(keys[6], (MH * 2 * NSUB, QHALF), QHALF ** -0.5, 0.25, ((0, 32),)),
        "memory_gate": bell_draw(keys[7], (D, D), D ** -0.5, 0.1875, ((0, 32),)),
        "memory_out": bell_draw(keys[8], (D, D), (D // 4) ** -0.5, 0.375, ((0, 32),)),
        "memory_values": bell_draw(keys[9], (VROWS, D), 1.0, 6.0, ((0, 32),)),
        "doc_lengths": draw_doc_lengths(jax.random.fold_in(keys[14], 71), 0),
        "token_order": draw_token_order(jax.random.fold_in(keys[14], 71), 0),
        "memory_picks": draw_memory_picks(jax.random.fold_in(keys[14], 71), 0),
        "cotangent": bell_draw(keys[13], (TOKENS, D), 1.0, 6.0, ((0, 32),)),
    }


@jax.custom_vjp
def low(v):
    return lax.optimization_barrier(v.astype(jnp.bfloat16)).astype(jnp.float32)

@jax.custom_vjp
def low_back(v):
    return v

def low_keep(v):
    return (low(v), None)

def low_pass(kept, grad):
    return (grad,)

def back_keep(v):
    return (v, None)

def back_low(kept, grad):
    return (low(grad),)
low.defvjp(low_keep, low_pass)
low_back.defvjp(back_keep, back_low)

def product(left, right):
    return jnp.dot(left, right, precision=lax.Precision.HIGHEST, preferred_element_type=jnp.float32)

def norm_scale(hidden):
    return lax.rsqrt(lax.optimization_barrier(jnp.mean(hidden * hidden, axis=-1, keepdims=True)) + 1e-06)

def softmax_last(scores):
    shifted = scores - lax.optimization_barrier(jnp.max(scores, axis=-1, keepdims=True))
    powers = jnp.exp(shifted)
    return powers / lax.optimization_barrier(jnp.sum(powers, axis=-1, keepdims=True))

def forward(inputs, attn_gain, attn_qkv, attn_out, memory_gain, memory_query, sub_keys, memory_gate, memory_out, memory_values, doc_lengths, memory_picks):
    tokens_all = inputs.shape[0]
    positions = jnp.arange(tokens_all, dtype=jnp.int32)
    doc_ends = jnp.cumsum(doc_lengths)
    documents = lax.optimization_barrier(jnp.sum((positions[:, None] >= doc_ends[None, :]).astype(jnp.int32), axis=1))
    normed_one = low(inputs * norm_scale(inputs) * attn_gain)
    projected = low_back(low(product(normed_one, attn_qkv))).reshape(tokens_all, 3, NH, HD)
    queries = projected[:, 0]
    keys_all = projected[:, 1]
    values_all = projected[:, 2]
    rows_block = min(512, tokens_all)
    blocks = tokens_all // rows_block

    def attend(pieces):
        query_block, place_block, doc_block = pieces
        scores = low_back(jnp.einsum('qhd,khd->hqk', query_block, keys_all, precision=lax.Precision.HIGHEST) * HD ** (-0.5))
        allowed = (positions[None, :] <= place_block[:, None]) & (documents[None, :] == doc_block[:, None])
        attn_probs = low(softmax_last(jnp.where(allowed[None], scores, -1e+30)))
        return jnp.einsum('hqk,khd->qhd', attn_probs, values_all, precision=lax.Precision.HIGHEST)
    attended = lax.map(jax.checkpoint(attend), (queries.reshape(blocks, rows_block, NH, HD), positions.reshape(blocks, rows_block), documents.reshape(blocks, rows_block)))
    attended = low_back(low(attended.reshape(tokens_all, NH * HD)))
    hidden_one = inputs + low_back(product(attended, attn_out))
    normed_two = low(hidden_one * norm_scale(hidden_one) * memory_gain)
    query_mem = low_back(low(product(normed_two, memory_query))).reshape(tokens_all, MH, 2, QHALF)
    key_table = sub_keys.reshape(MH, 2, NSUB, QHALF)
    sub_scores = low_back(jnp.einsum('thcd,hcnd->thcn', query_mem, key_table, precision=lax.Precision.HIGHEST))
    picked = jnp.take_along_axis(sub_scores[:, :, 0], memory_picks[:, :, :, 0], axis=2) + jnp.take_along_axis(sub_scores[:, :, 1], memory_picks[:, :, :, 1], axis=2)
    weights = low(softmax_last(picked))
    indices = memory_picks[:, :, :, 0] * NSUB + memory_picks[:, :, :, 1]

    def lookup(pieces):
        weight_block, index_block = pieces
        fetched = low_back(memory_values[index_block])
        return jnp.einsum('thk,thkd->td', weight_block, fetched, precision=lax.Precision.HIGHEST)
    memory = lax.map(jax.checkpoint(lookup), (weights.reshape(blocks, rows_block, MH, KPICK), indices.reshape(blocks, rows_block, MH, KPICK)))
    memory = low_back(memory.reshape(tokens_all, D))
    gate_pre = low_back(product(normed_two, memory_gate))
    mixed_low = low(memory * gate_pre * jax.nn.sigmoid(gate_pre))
    return hidden_one + product(mixed_low, memory_out)

def reference(inputs, attn_gain, attn_qkv, attn_out, memory_gain, memory_query, sub_keys, memory_gate, memory_out, memory_values, doc_lengths, token_order, memory_picks, cotangent):
    tokens_all = inputs.shape[0]
    inverse = jnp.zeros((tokens_all,), jnp.int32).at[token_order.astype(jnp.int32)].set(jnp.arange(tokens_all, dtype=jnp.int32))
    picks_of = memory_picks[inverse]

    def whole(inputs_f, attn_gain_f, attn_qkv_f, attn_out_f, memory_gain_f, memory_query_f, sub_keys_f, memory_gate_f, memory_out_f, memory_values_f):
        return forward(inputs_f, attn_gain_f, attn_qkv_f, attn_out_f, memory_gain_f, memory_query_f, sub_keys_f, memory_gate_f, memory_out_f, memory_values_f, doc_lengths, picks_of)
    result, backward = jax.vjp(whole, inputs.astype(jnp.float32), attn_gain.astype(jnp.float32), attn_qkv.astype(jnp.float32), attn_out.astype(jnp.float32), memory_gain.astype(jnp.float32), memory_query.astype(jnp.float32), sub_keys.astype(jnp.float32), memory_gate.astype(jnp.float32), memory_out.astype(jnp.float32), memory_values.astype(jnp.float32))
    grads = backward(cotangent.astype(jnp.float32))
    return (result.astype(jnp.bfloat16), grads[0], grads[1], grads[2], grads[3], grads[4], grads[5], grads[6], grads[7], grads[8], grads[9])
```

```python
import math

import jax
import jax.numpy as jnp
from jax import lax
from jax.experimental import pallas as pl
from jax.experimental.pallas import tpu as pltpu
from jax.sharding import Mesh
from jax.sharding import PartitionSpec as P

NH = 16
HD = 64
MH = 4
QHALF = 512
NSUB = 256
KPICK = 32
TP = 2 * MH

GROUP = ("head", "outer")
BLK = ("outer", "tp")
ALL = ("head", "outer", "tp")

epsilon = 1e-06
neg_big = -1e30
LANES = 128
bf16 = jnp.bfloat16
f32 = jnp.float32
NT = (((1,), (1,)), ((), ()))
TN = (((0,), (0,)), ((), ()))


def mm(left, right, dims=(((1,), (0,)), ((), ()))):
    return lax.dot_general(left, right, dims, preferred_element_type=f32)


def params(mib):
    return pltpu.CompilerParams(vmem_limit_bytes=mib * 1024 * 1024)


def head_rows(pair):
    lane = lax.broadcasted_iota(jnp.int32, pair.shape, 1)
    zero = jnp.zeros_like(pair)
    return (jnp.where(lane < HD, pair, zero), jnp.where(lane < HD, zero, pair))


def key_range(base, block_q, block_k, low_first_ref):
    step = pl.program_id(0)
    first = low_first_ref[step] // block_k
    last = (base + (step + 1) * block_q - 1) // block_k
    return step, first, last + 1


def attn_fwd_kernel(base, block_k, low_first_ref, q_ref, kv_ref, low_ref, att_ref, lse_ref):
    block_q = q_ref.shape[0]
    step, first, stop = key_range(base, block_q, block_k, low_first_ref)
    queries = head_rows(q_ref[...])
    low = low_ref[...]
    high = base + step * block_q + lax.broadcasted_iota(jnp.int32, (1, block_q), 1)

    def visit(turn, carried):
        start = pl.multiple_of(turn * block_k, block_k)
        keys = kv_ref[pl.ds(start, block_k), :LANES]
        values = kv_ref[pl.ds(start, block_k), LANES:]
        place = start + lax.broadcasted_iota(jnp.int32, (block_k, block_q), 0)
        allowed = (place >= low) & (place <= high)
        out = []
        for head in range(2):
            run_max, run_sum, run_acc = carried[head]
            scores = jnp.where(allowed, mm(keys, queries[head], NT), neg_big)
            new_max = jnp.maximum(run_max, jnp.max(scores, axis=0, keepdims=True))
            powers = jnp.exp(scores - new_max)
            rescale = jnp.exp(run_max - new_max)
            run_sum = run_sum * rescale + jnp.sum(powers, axis=0, keepdims=True)
            run_acc = run_acc * rescale + mm(values, powers.astype(bf16), TN)
            out.append((new_max, run_sum, run_acc))
        return tuple(out)

    fresh = (
        jnp.full((1, block_q), neg_big, f32),
        jnp.zeros((1, block_q), f32),
        jnp.zeros((LANES, block_q), f32),
    )
    done = lax.fori_loop(first, stop, visit, (fresh, fresh))
    att_ref[:HD, :] = done[0][2][:HD] / done[0][1]
    att_ref[HD:, :] = done[1][2][HD:] / done[1][1]
    lse_ref[0:1, :] = done[0][0] + jnp.log(done[0][1])
    lse_ref[1:2, :] = done[1][0] + jnp.log(done[1][1])


def attn_fwd(base, low_first, low, queries, keys_values):
    rows = queries.shape[0]
    block_q, block_k = 256, 512
    return pl.pallas_call(
        lambda *refs: attn_fwd_kernel(base, block_k, *refs),
        grid_spec=pltpu.PrefetchScalarGridSpec(
            num_scalar_prefetch=1,
            grid=(rows // block_q,),
            in_specs=[
                pl.BlockSpec((block_q, LANES), lambda i, s: (i, 0)),
                pl.BlockSpec(keys_values.shape, lambda i, s: (0, 0)),
                pl.BlockSpec((1, block_q), lambda i, s: (0, i)),
            ],
            out_specs=[
                pl.BlockSpec((LANES, block_q), lambda i, s: (0, i)),
                pl.BlockSpec((2, block_q), lambda i, s: (0, i)),
            ],
        ),
        out_shape=[
            jax.ShapeDtypeStruct((LANES, rows), f32),
            jax.ShapeDtypeStruct((2, rows), f32),
        ],
        compiler_params=params(32),
        name="attn_fwd",
    )(low_first[::block_q], queries, keys_values, low[None, :])


def attn_bwd_kernel(
    base,
    block_k,
    low_first_ref,
    q_ref,
    kv_ref,
    low_ref,
    lse_ref,
    att_ref,
    grad_ref,
    dq_ref,
    dk_ref,
    dv_ref,
):
    block_q = q_ref.shape[0]
    step, first, stop = key_range(base, block_q, block_k, low_first_ref)

    @pl.when(step == 0)
    def clear():
        dk_ref[...] = jnp.zeros_like(dk_ref)
        dv_ref[...] = jnp.zeros_like(dv_ref)

    queries = head_rows(q_ref[...])
    grads = head_rows(grad_ref[...])
    grad_turned = jnp.transpose(grad_ref[...].astype(f32)) * att_ref[...]
    deltas = (
        jnp.sum(grad_turned[:HD], axis=0, keepdims=True),
        jnp.sum(grad_turned[HD:], axis=0, keepdims=True),
    )
    low = low_ref[...]
    high = base + step * block_q + lax.broadcasted_iota(jnp.int32, (1, block_q), 1)

    def visit(turn, carried):
        start = pl.multiple_of(turn * block_k, block_k)
        keys = kv_ref[pl.ds(start, block_k), :LANES]
        values = kv_ref[pl.ds(start, block_k), LANES:]
        place = start + lax.broadcasted_iota(jnp.int32, (block_k, block_q), 0)
        allowed = (place >= low) & (place <= high)
        out = []
        grad_key = dk_ref[pl.ds(start, block_k), :]
        grad_value = dv_ref[pl.ds(start, block_k), :]
        for head in range(2):
            scores = mm(keys, queries[head], NT)
            probs = jnp.where(allowed, jnp.exp(scores - lse_ref[head : head + 1, :]), 0.0)
            grad_probs = mm(values, grads[head], NT)
            grad_scores = (probs * (grad_probs - deltas[head])).astype(bf16)
            grad_key = grad_key + mm(grad_scores, queries[head])
            grad_value = grad_value + mm(probs.astype(bf16), grads[head])
            out.append(carried[head] + mm(keys, grad_scores, TN))
        dk_ref[pl.ds(start, block_k), :] = grad_key
        dv_ref[pl.ds(start, block_k), :] = grad_value
        return tuple(out)

    fresh = jnp.zeros((LANES, block_q), f32)
    done = lax.fori_loop(first, stop, visit, (fresh, fresh))
    dq_ref[:HD, :] = done[0][:HD]
    dq_ref[HD:, :] = done[1][HD:]


def attn_bwd(base, low_first, low, queries, keys_values, lse, att, grads):
    rows = queries.shape[0]
    block_q, block_k = 256, 512
    span = keys_values.shape[0]
    return pl.pallas_call(
        lambda *refs: attn_bwd_kernel(base, block_k, *refs),
        grid_spec=pltpu.PrefetchScalarGridSpec(
            num_scalar_prefetch=1,
            grid=(rows // block_q,),
            in_specs=[
                pl.BlockSpec((block_q, LANES), lambda i, s: (i, 0)),
                pl.BlockSpec(keys_values.shape, lambda i, s: (0, 0)),
                pl.BlockSpec((1, block_q), lambda i, s: (0, i)),
                pl.BlockSpec((2, block_q), lambda i, s: (0, i)),
                pl.BlockSpec((LANES, block_q), lambda i, s: (0, i)),
                pl.BlockSpec((block_q, LANES), lambda i, s: (i, 0)),
            ],
            out_specs=[
                pl.BlockSpec((LANES, block_q), lambda i, s: (0, i)),
                pl.BlockSpec((span, LANES), lambda i, s: (0, 0)),
                pl.BlockSpec((span, LANES), lambda i, s: (0, 0)),
            ],
        ),
        out_shape=[
            jax.ShapeDtypeStruct((LANES, rows), f32),
            jax.ShapeDtypeStruct((span, LANES), f32),
            jax.ShapeDtypeStruct((span, LANES), f32),
        ],
        compiler_params=params(48),
        name="attn_bwd",
    )(low_first[::block_q], queries, keys_values, low[None, :], lse, att, grads)


def hits(count, row):
    return lax.broadcasted_iota(jnp.int32, (count, row.shape[1]), 0) == row


def one_hot(count, row):
    return jnp.where(hits(count, row), 1.0, 0.0).astype(bf16)


def bucket_kernel(high_ref, low_ref, load_ref, out_ref):
    loads = load_ref.shape[0]
    chunks = high_ref.shape[0]
    total = jnp.zeros(out_ref.shape, f32)
    for chunk in range(chunks):
        high = one_hot(out_ref.shape[0], high_ref[chunk : chunk + 1, :])
        mask = hits(LANES, low_ref[chunk : chunk + 1, :])
        parts = [
            jnp.where(mask, load_ref[load, chunk : chunk + 1, :], 0.0).astype(bf16)
            for load in range(loads)
        ]
        total = total + mm(high, jnp.concatenate(parts, axis=0), NT)
    out_ref[...] = total


def to_buckets(high, low, loads, places):
    return pl.pallas_call(
        bucket_kernel,
        out_shape=jax.ShapeDtypeStruct((places // LANES, loads.shape[0] * LANES), f32),
        compiler_params=params(32),
        name="to_buckets",
    )(high, low, loads)


def unbucket_kernel(high_ref, low_ref, main_ref, rest_ref, out_ref):
    count = main_ref.shape[1]
    for chunk in range(high_ref.shape[0]):
        high = one_hot(count, high_ref[chunk : chunk + 1, :])
        found = mm(main_ref[...], high) + mm(rest_ref[...], high)
        mask = hits(LANES, low_ref[chunk : chunk + 1, :])
        out_ref[chunk : chunk + 1, :] = jnp.sum(
            jnp.where(mask, found, 0.0), axis=0, keepdims=True
        )


def from_buckets(high, low, table):
    turned = jnp.transpose(table)
    main = turned.astype(bf16)
    rest = (turned - main.astype(f32)).astype(bf16)
    return pl.pallas_call(
        unbucket_kernel,
        out_shape=jax.ShapeDtypeStruct(high.shape, f32),
        compiler_params=params(32),
        name="from_buckets",
    )(high, low, main, rest)


def place_rows(rows, subs, token_row, first_row):
    tokens = one_hot(rows, token_row)
    return jnp.concatenate(
        [tokens * jnp.where(first_row == first, 1.0, 0.0).astype(bf16) for first in range(subs)],
        axis=0,
    )


def spread_kernel(rows, subs, token_ref, first_ref, second_ref, weight_ref, out_ref):
    left = place_rows(rows, subs, token_ref[0], first_ref[0])
    right = jnp.where(hits(NSUB, second_ref[0]), weight_ref[0], 0.0).astype(bf16)
    table = mm(left, right, NT).astype(bf16)
    for first in range(subs):
        out_ref[:, first * NSUB : (first + 1) * NSUB] = table[first * rows : (first + 1) * rows]


def spread_weights(rows, subs, token, first, second, weight):
    devices, unused, capacity = token.shape
    row = pl.BlockSpec((1, 1, capacity), lambda i: (i, 0, 0))
    return pl.pallas_call(
        lambda *refs: spread_kernel(rows, subs, *refs),
        grid=(devices,),
        in_specs=[row, row, row, row],
        out_specs=pl.BlockSpec((rows, subs * NSUB), lambda i: (i, 0)),
        out_shape=jax.ShapeDtypeStruct((devices * rows, subs * NSUB), bf16),
        compiler_params=params(48),
        name="spread_weights",
    )(token, first, second, weight)


def dots_kernel(rows, subs, token_ref, first_ref, second_ref, grad_ref, value_ref, out_ref):
    pair = token_ref.shape[0]
    found = []
    for first in range(subs):
        found.append(
            mm(value_ref[first * NSUB : (first + 1) * NSUB, :], grad_ref[...], NT).astype(bf16)
        )
    for block in range(pair):
        left = place_rows(rows, subs, token_ref[block], first_ref[block])
        table = jnp.concatenate(
            [part[:, block * rows : (block + 1) * rows] for part in found], axis=1
        )
        spread = mm(table, left)
        out_ref[block] = jnp.sum(
            jnp.where(hits(NSUB, second_ref[block]), spread, 0.0), axis=0, keepdims=True
        )


def row_dots(rows, subs, token, first, second, grads, values):
    devices, unused, capacity = token.shape
    pair = 2
    row = pl.BlockSpec((pair, 1, capacity), lambda i: (i, 0, 0))
    return pl.pallas_call(
        lambda *refs: dots_kernel(rows, subs, *refs),
        grid=(devices // pair,),
        in_specs=[
            row,
            row,
            row,
            pl.BlockSpec((pair * rows, grads.shape[1]), lambda i: (i, 0)),
            pl.BlockSpec(values.shape, lambda i: (0, 0)),
        ],
        out_specs=row,
        out_shape=jax.ShapeDtypeStruct(token.shape, f32),
        compiler_params=params(48),
        name="row_dots",
    )(token, first, second, grads, values)


def swap(array, axes):
    return lax.all_to_all(array, axes, split_axis=0, concat_axis=0, tiled=True)


def gather(array, axes):
    return lax.all_gather(array, axes, axis=0, tiled=True)


def sum_back(partial, rows):
    pieces = swap(partial.astype(bf16).reshape(TP, rows, -1), "tp")
    return jnp.sum(pieces.astype(f32), axis=0)


def norm_scale(hidden):
    return lax.rsqrt(jnp.mean(hidden * hidden, axis=-1, keepdims=True) + epsilon)


def norm_back(hidden, scale, weighted):
    coupled = jnp.mean(hidden * weighted, axis=-1, keepdims=True)
    return scale * weighted - hidden * (scale * scale * scale) * coupled


def body(
    inputs,
    attn_gain,
    attn_qkv,
    attn_out,
    memory_gain,
    memory_query,
    sub_keys,
    memory_gate,
    memory_out,
    memory_values,
    doc_lengths,
    token_order,
    memory_picks,
    cotangent,
):
    rows, width = inputs.shape
    outer = lax.axis_size("outer")
    heads = lax.axis_size("head")
    groups = heads * outer
    blocks = outer * TP
    devices = groups * TP
    share = rows // blocks
    span = TP * rows
    tokens = token_order.shape[0]
    head_index = lax.axis_index("head")
    outer_index = lax.axis_index("outer")
    group_index = head_index * outer + outer_index
    rows_w = attn_qkv.shape[0]
    own_rows = memory_values.shape[0]
    subs = own_rows // NSUB
    picks = MH * KPICK
    capacity = 2 * rows * picks // devices
    back = min(groups - 1, -(-(tokens // 2 - 1) // span))
    base = back * span

    gain_one = attn_gain.astype(f32)[:, None]
    gain_two = memory_gain.astype(f32)[:, None]
    scaled_qkv = (attn_qkv.astype(f32) * gain_one).astype(bf16)
    scaled_query = (memory_query.astype(f32) * gain_two).astype(bf16)
    scaled_gate = (memory_gate.astype(f32) * gain_two).astype(bf16)

    def columns(piece):
        return jnp.moveaxis(piece, 1, 0).reshape(TP, rows_w, -1)

    qkv_cut = jnp.transpose(scaled_qkv.reshape(rows_w, 3, TP, LANES), (2, 0, 1, 3))
    weight_qkv = gather(swap(qkv_cut.reshape(TP, rows_w, 3 * LANES), "tp").reshape(TP * rows_w, -1), GROUP)
    rest_cut = jnp.concatenate(
        [columns(scaled_query.reshape(rows_w, TP, -1)), columns(scaled_gate.reshape(rows_w, TP, -1))],
        axis=2,
    )
    weight_rest = gather(swap(rest_cut, "tp").reshape(TP * rows_w, -1), GROUP)
    to_turned = [
        (groups * part + group, group * TP + part) for group in range(groups) for part in range(TP)
    ]
    from_turned = [(there, here) for here, there in to_turned]
    row_cut = jnp.stack([attn_out, memory_out, sub_keys.reshape(rows_w, width)])
    row_all = lax.all_gather(lax.ppermute(row_cut, ALL, to_turned), GROUP, axis=1, tiled=True)
    weight_attn = row_all[0]
    weight_mixed = row_all[1]
    key_table = row_all[2].reshape(NSUB, QHALF)

    by_half = jnp.transpose(
        memory_picks.reshape(outer, TP * share, MH, KPICK, 2), (0, 2, 4, 1, 3)
    ).reshape(blocks, TP * share, KPICK)
    half_index = swap(by_half, BLK).reshape(span, KPICK)
    first_pick = memory_picks[:, :, :, 0].reshape(rows, picks)
    second_pick = memory_picks[:, :, :, 1].reshape(rows, picks)
    owner = first_pick // subs
    device_range = jnp.arange(devices, dtype=jnp.int32)
    owned = (owner[None] == device_range[:, None, None]).astype(bf16)
    before = (
        jnp.arange(picks, dtype=jnp.int32)[:, None] < jnp.arange(picks, dtype=jnp.int32)[None, :]
    ).astype(bf16)
    before_rows = (
        jnp.arange(rows, dtype=jnp.int32)[:, None] < jnp.arange(rows, dtype=jnp.int32)[None, :]
    ).astype(bf16)
    in_row = jnp.einsum("dtk,kj->dtj", owned, before, preferred_element_type=f32)
    row_counts = jnp.sum(owned.astype(f32), axis=2)
    of_rows = jnp.dot(row_counts.astype(bf16), before_rows, preferred_element_type=f32)
    rank = jnp.sum(owned.astype(f32) * (in_row + of_rows[:, :, None]), axis=0).astype(jnp.int32)
    target = owner * capacity + rank
    chunked = (-1, 1024)
    target_high = (target // LANES).reshape(chunked)
    target_low = (target % LANES).reshape(chunked)
    places = devices * capacity
    entry_loads = jnp.stack(
        [
            jnp.broadcast_to(jnp.arange(rows, dtype=jnp.int32)[:, None], (rows, picks)),
            first_pick % subs,
            second_pick,
        ]
    ).astype(f32).reshape(3, -1, 1024)
    entries = to_buckets(target_high, target_low, entry_loads, places)
    entries = jnp.transpose(entries.reshape(devices, capacity // LANES, 3, LANES), (0, 2, 1, 3))
    entries = swap(entries.reshape(devices, 3, capacity).astype(jnp.int32), ALL)
    entry_token = entries[:, 0:1]
    entry_first = entries[:, 1:2]
    entry_second = entries[:, 2:3]

    laid = token_order.reshape(heads, blocks, outer, TP * share)
    mine = lax.dynamic_index_in_dim(laid, head_index, 0, keepdims=False)
    mine = lax.dynamic_index_in_dim(mine, outer_index, 1, keepdims=False)
    local = mine.reshape(span) - group_index * span
    deal = (local[:, None] == jnp.arange(span, dtype=jnp.int32)[None, :]).astype(bf16)

    def dealt(array):
        return mm(deal, array).astype(bf16)

    def undealt(array):
        return mm(deal, array, TN).astype(bf16)

    group_inputs = gather(inputs, "tp")
    group_wide = group_inputs.astype(f32)
    normed_one = (group_wide * norm_scale(group_wide)).astype(bf16)
    projected = mm(normed_one, weight_qkv).astype(bf16)
    queries = projected[:, :LANES] * jnp.asarray(1.0 / math.sqrt(HD), bf16)
    own_kv = projected[:, LANES:]
    keys_values = jnp.concatenate(
        [
            lax.ppermute(own_kv, GROUP, [(at, at + away) for at in range(groups - away)])
            for away in range(back, 0, -1)
        ]
        + [own_kv],
        axis=0,
    )
    positions = group_index * span + jnp.arange(span, dtype=jnp.int32)
    doc_ends = jnp.cumsum(doc_lengths)
    doc_start = jnp.max(
        jnp.where(positions[:, None] >= doc_ends[None, :], doc_ends[None, :], 0), axis=1
    )
    low = doc_start - (group_index - back) * span
    attended, lse = attn_fwd(base, low, low, queries, keys_values)
    attended_low = attended.astype(bf16)
    inputs_wide = inputs.astype(f32)
    hidden_one = inputs_wide + sum_back(mm(attended_low, weight_attn, TN), rows)
    scale_two = norm_scale(hidden_one)
    normed_two = dealt(gather((hidden_one * scale_two).astype(bf16), "tp"))
    dealt_cot = dealt(gather(cotangent, "tp"))

    pre = mm(normed_two, weight_rest)
    query_mem = pre[:, :QHALF].astype(bf16)
    gate_pre = pre[:, QHALF:]
    gate_sig = jax.nn.sigmoid(gate_pre)
    grad_mixed = mm(dealt_cot, weight_mixed, NT)
    grad_memory = (grad_mixed * gate_pre * gate_sig).astype(bf16)
    every_grad = gather(grad_memory, ALL).reshape(
        heads, outer, TP, blocks, TP * share, LANES
    )
    every_grad = jnp.transpose(every_grad, (0, 3, 1, 4, 2, 5)).reshape(devices * rows, width)

    sub_scores = mm(query_mem, key_table, NT)
    sub_range = jnp.arange(NSUB, dtype=jnp.int32)
    half_hit = half_index[:, :, None] == sub_range
    picked_half = jnp.sum(jnp.where(half_hit, sub_scores[:, None, :], 0.0), axis=2)
    picked = swap(picked_half.reshape(blocks, TP * share, KPICK), BLK)
    picked = jnp.transpose(
        picked.reshape(outer, MH, 2, TP * share, KPICK), (0, 3, 1, 2, 4)
    ).reshape(rows, MH, 2, KPICK)
    picked = picked[:, :, 0] + picked[:, :, 1]
    picked_exp = jnp.exp(picked - jnp.max(picked, axis=2, keepdims=True))
    pick_weights = picked_exp / jnp.sum(picked_exp, axis=2, keepdims=True)
    weight_loads = pick_weights.reshape(1, -1, 1024)
    sent_weights = to_buckets(target_high, target_low, weight_loads, places)
    entry_weight = swap(sent_weights.astype(bf16).reshape(devices, 1, capacity), ALL).astype(f32)

    spread = spread_weights(rows, subs, entry_token, entry_first, entry_second, entry_weight)
    partial = mm(spread, memory_values).astype(bf16)
    partial = jnp.transpose(
        partial.reshape(heads, blocks, outer, TP * share, TP, LANES), (0, 2, 4, 1, 3, 5)
    ).reshape(devices * span, LANES)
    memory = lax.psum_scatter(partial, ALL, scatter_dimension=0, tiled=True).astype(f32)
    mixed_low = (memory * gate_pre * gate_sig).astype(bf16)
    grad_gate = (grad_mixed * memory * gate_sig * (1.0 + gate_pre * (1.0 - gate_sig))).astype(bf16)
    output = (hidden_one + sum_back(mm(undealt(mixed_low), weight_mixed), rows)).astype(bf16)
    grad_mixed_rows = mm(mixed_low, dealt_cot, TN)

    entry_dots = row_dots(
        rows, subs, entry_token, entry_first, entry_second, every_grad, memory_values
    )
    returned = swap(entry_dots, ALL).reshape(places // LANES, LANES)
    grad_pick = from_buckets(target_high, target_low, returned).reshape(rows, MH, KPICK)
    grad_picked = pick_weights * (
        grad_pick - jnp.sum(pick_weights * grad_pick, axis=2, keepdims=True)
    )
    to_half = jnp.transpose(grad_picked.reshape(outer, TP * share, MH, KPICK), (0, 2, 1, 3))
    to_half = jnp.broadcast_to(
        to_half[:, :, None], (outer, MH, 2, TP * share, KPICK)
    ).reshape(blocks, TP * share, KPICK)
    grad_half = swap(to_half, BLK).reshape(span, KPICK)
    grad_sub = jnp.sum(jnp.where(half_hit, grad_half[:, :, None], 0.0), axis=1).astype(bf16)
    grad_query = mm(grad_sub, key_table).astype(bf16)
    grad_table = mm(grad_sub, query_mem, TN).reshape(LANES, width)
    grad_values = mm(spread, every_grad, TN)
    grad_pre = jnp.concatenate([grad_query, grad_gate], axis=1)
    grad_rest_cut = mm(normed_two, grad_pre, TN)
    weighted_two = sum_back(mm(undealt(grad_pre), weight_rest, NT), rows)
    grad_hidden = cotangent.astype(f32) + norm_back(hidden_one, scale_two, weighted_two)

    grad_branch = gather(grad_hidden.astype(bf16), "tp")
    grad_attn_rows = mm(attended_low, grad_branch)
    grad_attended = mm(grad_branch, weight_attn, NT).astype(bf16)
    grad_q, grad_k, grad_v = attn_bwd(
        base, low, low, queries, keys_values, lse, attended, grad_attended
    )
    grad_kv = jnp.concatenate([grad_k, grad_v], axis=1)
    own_grad_kv = grad_kv[base:]
    for away in range(1, back + 1):
        piece = grad_kv[base - away * span : base - (away - 1) * span].astype(bf16)
        own_grad_kv = own_grad_kv + lax.ppermute(
            piece, GROUP, [(at + away, at) for at in range(groups - away)]
        ).astype(f32)
    grad_projected = jnp.concatenate(
        [jnp.transpose(grad_q) * (1.0 / math.sqrt(HD)), own_grad_kv], axis=1
    ).astype(bf16)
    grad_qkv_cut = mm(normed_one, grad_projected, TN)
    weighted_one = sum_back(mm(grad_projected, weight_qkv, NT), rows)
    grad_inputs = grad_hidden + norm_back(inputs_wide, norm_scale(inputs_wide), weighted_one)

    def columns_home(cut):
        summed = lax.psum_scatter(cut, GROUP, scatter_dimension=0, tiled=True)
        return jnp.moveaxis(swap(summed.reshape(TP, rows_w, -1), "tp"), 0, 1)

    row_grads = jnp.stack([grad_attn_rows, grad_mixed_rows, grad_table], axis=1)
    row_home = lax.ppermute(
        lax.psum_scatter(row_grads, GROUP, scatter_dimension=0, tiled=True), ALL, from_turned
    )
    rest_home = columns_home(grad_rest_cut)
    query_home = rest_home[:, :, :QHALF].reshape(rows_w, -1)
    gate_home = rest_home[:, :, QHALF:].reshape(rows_w, -1)
    qkv_home = jnp.transpose(
        columns_home(grad_qkv_cut).reshape(rows_w, TP, 3, LANES), (0, 2, 1, 3)
    ).reshape(rows_w, -1)
    grad_attn_gain = jnp.sum(qkv_home * attn_qkv.astype(f32), axis=1)
    grad_memory_gain = jnp.sum(query_home * memory_query.astype(f32), axis=1) + jnp.sum(
        gate_home * memory_gate.astype(f32), axis=1
    )
    return (
        output,
        grad_inputs,
        grad_attn_gain,
        qkv_home * gain_one,
        row_home[:, 0],
        grad_memory_gain,
        query_home * gain_two,
        row_home[:, 2].reshape(sub_keys.shape),
        gate_home * gain_two,
        row_home[:, 1],
        grad_values,
    )


def solution(mesh):
    heads, blocks = mesh.devices.shape
    cut_mesh = Mesh(mesh.devices.reshape(heads, blocks // TP, TP), ALL)
    matrix = P(ALL, None)
    in_specs = (
        matrix,
        P(ALL),
        matrix,
        matrix,
        P(ALL),
        matrix,
        matrix,
        matrix,
        matrix,
        matrix,
        P(),
        P(),
        P(ALL, None, None, None),
        matrix,
    )
    out_specs = (
        matrix,
        matrix,
        P(ALL),
        matrix,
        matrix,
        P(ALL),
        matrix,
        matrix,
        matrix,
        matrix,
        matrix,
    )
    return jax.shard_map(
        body, mesh=cut_mesh, in_specs=in_specs, out_specs=out_specs, check_vma=False
    )
```

```python
import math

import jax
import jax.numpy as jnp
from jax import lax
from jax.experimental import pallas as pl
from jax.experimental.pallas import tpu as pltpu
from jax.sharding import Mesh
from jax.sharding import PartitionSpec as P

NH = 16
HD = 64
MH = 4
QHALF = 512
NSUB = 256
KPICK = 32
TP = 2 * MH

GROUP = ("head", "outer")
BLK = ("outer", "tp")
ALL = ("head", "outer", "tp")

epsilon = 1e-06
neg_big = -1e30
LANES = 128
bf16 = jnp.bfloat16
f32 = jnp.float32
NN = (((1,), (0,)), ((), ()))
NT = (((1,), (1,)), ((), ()))
TN = (((0,), (0,)), ((), ()))


def mm(left, right, dims=NN):
    return lax.dot_general(left, right, dims, preferred_element_type=f32)


def params(mib):
    return pltpu.CompilerParams(vmem_limit_bytes=mib * 1024 * 1024)


def lasting(microseconds):
    return pl.CostEstimate(
        flops=0, bytes_accessed=int(microseconds * 3.5e6), transcendentals=0
    )


def head_rows(pair):
    lane = lax.broadcasted_iota(jnp.int32, pair.shape, 1)
    zero = jnp.zeros_like(pair)
    return (jnp.where(lane < HD, pair, zero), jnp.where(lane < HD, zero, pair))


def turned_block(step, here, block, rows):
    return jnp.bitwise_xor(step, here * rows // block)


def turned_iota(shape, axis, here, rows):
    place = lax.broadcasted_iota(jnp.int32, shape, axis)
    return jnp.bitwise_xor(place, lax.rem(here * rows, shape[axis]))


def key_blocks(step, base, block_q, block_k, low_first_ref):
    return (
        low_first_ref[step] // block_k,
        (base + (step + 1) * block_q - 1) // block_k + 1,
    )


def key_start(turn, span, here, block_k, rows):
    per_group = span // block_k
    group = turn // per_group
    within = turned_block(lax.rem(turn, per_group), here, block_k, rows)
    return pl.multiple_of(group * span + within * block_k, block_k)


def attn_fwd_kernel(
    base, span, rows, block_k, low_first_ref, here_ref, q_ref, kv_ref, low_ref, att_ref, lse_ref, out_ref
):
    block_q = q_ref.shape[0]
    step = pl.program_id(0)
    here = here_ref[0]
    first, stop = key_blocks(step, base, block_q, block_k, low_first_ref)
    queries = head_rows(q_ref[...])
    low = low_ref[...]
    high = base + step * block_q + turned_iota((1, block_q), 1, here, rows)
    inner = turned_iota((block_k, block_q), 0, here, rows)

    def visit(turn, carried):
        start = key_start(turn, span, here, block_k, rows)
        keys = kv_ref[pl.ds(start, block_k), :LANES]
        values = kv_ref[pl.ds(start, block_k), LANES:]
        place = turn * block_k + inner
        allowed = (place >= low) & (place <= high)
        out = []
        for head in range(2):
            run_max, run_sum, run_acc = carried[head]
            scores = jnp.where(allowed, mm(keys, queries[head], NT), neg_big)
            new_max = jnp.maximum(run_max, jnp.max(scores, axis=0, keepdims=True))
            powers = jnp.exp(scores - new_max)
            rescale = jnp.exp(run_max - new_max)
            run_sum = run_sum * rescale + jnp.sum(powers, axis=0, keepdims=True)
            run_acc = run_acc * rescale + mm(values, powers.astype(bf16), TN)
            out.append((new_max, run_sum, run_acc))
        return tuple(out)

    fresh = (
        jnp.full((1, block_q), neg_big, f32),
        jnp.zeros((1, block_q), f32),
        jnp.zeros((LANES, block_q), f32),
    )
    done = lax.fori_loop(first, stop, visit, (fresh, fresh))
    att_ref[:HD, :] = done[0][2][:HD] / done[0][1]
    att_ref[HD:, :] = done[1][2][HD:] / done[1][1]
    out_ref[...] = jnp.transpose(att_ref[...]).astype(bf16)
    lse_ref[0:1, :] = done[0][0] + jnp.log(done[0][1])
    lse_ref[1:2, :] = done[1][0] + jnp.log(done[1][1])


def attn_specs(block_q, rows, span):
    def turn(i, here):
        return turned_block(i, here[0], block_q, rows)

    return (
        pl.BlockSpec((block_q, LANES), lambda i, s, here: (turn(i, here), 0)),
        pl.BlockSpec((1, block_q), lambda i, s, here: (0, turn(i, here))),
        pl.BlockSpec((2, block_q), lambda i, s, here: (0, turn(i, here))),
        pl.BlockSpec((LANES, block_q), lambda i, s, here: (0, turn(i, here))),
    )


def attn_fwd(base, rows, low_first, here, low, queries, keys_values):
    span = queries.shape[0]
    block_q, block_k = 256, 512
    by_row, one_lane, two_lane, by_lane = attn_specs(block_q, rows, span)
    return pl.pallas_call(
        lambda *refs: attn_fwd_kernel(base, span, rows, block_k, *refs),
        grid_spec=pltpu.PrefetchScalarGridSpec(
            num_scalar_prefetch=2,
            grid=(span // block_q,),
            in_specs=[
                by_row,
                pl.BlockSpec(keys_values.shape, lambda i, s, here: (0, 0)),
                one_lane,
            ],
            out_specs=[by_lane, two_lane, by_row],
        ),
        out_shape=[
            jax.ShapeDtypeStruct((LANES, span), f32),
            jax.ShapeDtypeStruct((2, span), f32),
            jax.ShapeDtypeStruct((span, LANES), bf16),
        ],
        compiler_params=params(32),
        cost_estimate=lasting(keys_values.shape[0] / 250),
        name="attn_fwd",
    )(low_first[::block_q], here, queries, keys_values, low[None, :])


def attn_bwd_kernel(
    base,
    span,
    rows,
    block_k,
    low_first_ref,
    here_ref,
    q_ref,
    kv_ref,
    low_ref,
    lse_ref,
    att_ref,
    grad_ref,
    dq_ref,
    *refs,
):
    dk_ref, dv_ref = refs[-2:]
    block_q = q_ref.shape[0]
    step = pl.program_id(0)
    here = here_ref[0]
    first, stop = key_blocks(step, base, block_q, block_k, low_first_ref)

    @pl.when(step == 0)
    def clear():
        dk_ref[...] = jnp.zeros_like(dk_ref)
        dv_ref[...] = jnp.zeros_like(dv_ref)

    queries = head_rows(q_ref[...])
    grads = head_rows(grad_ref[...])
    grad_turned = jnp.transpose(grad_ref[...].astype(f32)) * att_ref[...]
    deltas = (
        jnp.sum(grad_turned[:HD], axis=0, keepdims=True),
        jnp.sum(grad_turned[HD:], axis=0, keepdims=True),
    )
    low = low_ref[...]
    high = base + step * block_q + turned_iota((1, block_q), 1, here, rows)
    inner = turned_iota((block_k, block_q), 0, here, rows)

    def visit(turn, carried):
        start = key_start(turn, span, here, block_k, rows)
        keys = kv_ref[pl.ds(start, block_k), :LANES]
        values = kv_ref[pl.ds(start, block_k), LANES:]
        place = turn * block_k + inner
        allowed = (place >= low) & (place <= high)
        out = []
        grad_key = dk_ref[pl.ds(start, block_k), :]
        grad_value = dv_ref[pl.ds(start, block_k), :]
        for head in range(2):
            scores = mm(keys, queries[head], NT)
            probs = jnp.where(allowed, jnp.exp(scores - lse_ref[head : head + 1, :]), 0.0)
            grad_probs = mm(values, grads[head], NT)
            grad_scores = (probs * (grad_probs - deltas[head])).astype(bf16)
            grad_key = grad_key + mm(grad_scores, queries[head])
            grad_value = grad_value + mm(probs.astype(bf16), grads[head])
            out.append(carried[head] + mm(keys, grad_scores, TN))
        dk_ref[pl.ds(start, block_k), :] = grad_key
        dv_ref[pl.ds(start, block_k), :] = grad_value
        return tuple(out)

    fresh = jnp.zeros((LANES, block_q), f32)
    done = lax.fori_loop(first, stop, visit, (fresh, fresh))
    turned = jnp.concatenate([done[0][:HD], done[1][HD:]], axis=0) * (1.0 / math.sqrt(HD))
    dq_ref[...] = jnp.transpose(turned).astype(bf16)

    @pl.when(step == span // block_q - 1)
    def leave():
        for turn, out_ref in enumerate(refs[:-2]):
            out_ref[:, :LANES] = dk_ref[turn * span : (turn + 1) * span, :].astype(bf16)
            out_ref[:, LANES:] = dv_ref[turn * span : (turn + 1) * span, :].astype(bf16)


def attn_bwd(base, rows, low_first, here, low, queries, keys_values, lse, att, grads):
    span = queries.shape[0]
    block_q, block_k = 256, 512
    reach = keys_values.shape[0]
    by_row, one_lane, two_lane, by_lane = attn_specs(block_q, rows, span)
    return pl.pallas_call(
        lambda *refs: attn_bwd_kernel(base, span, rows, block_k, *refs),
        grid_spec=pltpu.PrefetchScalarGridSpec(
            num_scalar_prefetch=2,
            grid=(span // block_q,),
            in_specs=[
                by_row,
                pl.BlockSpec(keys_values.shape, lambda i, s, here: (0, 0)),
                one_lane,
                two_lane,
                by_lane,
                by_row,
            ],
            out_specs=[by_row]
            + [pl.BlockSpec((span, 2 * LANES), lambda i, s, here: (0, 0))] * (reach // span),
            scratch_shapes=[pltpu.VMEM((reach, LANES), f32), pltpu.VMEM((reach, LANES), f32)],
        ),
        out_shape=[jax.ShapeDtypeStruct((span, LANES), bf16)]
        + [jax.ShapeDtypeStruct((span, 2 * LANES), bf16)] * (reach // span),
        compiler_params=params(48),
        cost_estimate=lasting(keys_values.shape[0] / 200),
        name="attn_bwd",
    )(low_first[::block_q], here, queries, keys_values, low[None, :], lse, att, grads)


def hits(count, row):
    return lax.broadcasted_iota(jnp.int32, (count, row.shape[1]), 0) == row


def one_hot(count, row):
    return jnp.where(hits(count, row), 1.0, 0.0).astype(bf16)


def wide_hits(count, ref, top, rows):
    return [hits(count, ref[row : row + 1, :]) for row in range(top, top + rows)]


def bucket_rows(high_ref, low_ref, load_refs, places):
    batch = 8
    total = jnp.zeros((places, len(load_refs) * LANES), f32)
    for top in range(0, high_ref.shape[0], batch):
        high = [
            jnp.where(hit, 1.0, 0.0).astype(bf16) for hit in wide_hits(places, high_ref, top, batch)
        ]
        low = wide_hits(LANES, low_ref, top, batch)
        parts = [
            jnp.concatenate(
                [
                    jnp.where(low[row], load_ref[top + row : top + row + 1, :], 0.0).astype(bf16)
                    for row in range(batch)
                ],
                axis=1,
            )
            for load_ref in load_refs
        ]
        total = total + mm(jnp.concatenate(high, axis=1), jnp.concatenate(parts, axis=0), NT)
    return total


def entries_kernel(high_ref, low_ref, first_ref, second_ref, out_ref, token_ref):
    token_ref[...] = lax.broadcasted_iota(jnp.int32, token_ref.shape, 0).astype(f32)
    loads = (token_ref, first_ref, second_ref)
    out_ref[...] = bucket_rows(high_ref, low_ref, loads, out_ref.shape[0]).astype(bf16)


def make_entries(high, low, first, second, places):
    return pl.pallas_call(
        entries_kernel,
        out_shape=jax.ShapeDtypeStruct((places // LANES, 3 * LANES), bf16),
        scratch_shapes=[pltpu.VMEM(high.shape, f32)],
        compiler_params=params(32),
        cost_estimate=lasting(5),
        name="make_entries",
    )(high, low, first.astype(f32), second.astype(f32))


def weights_kernel(picked_ref, high_ref, low_ref, weight_ref, out_ref):
    parts = []
    for head in range(MH):
        picked = picked_ref[2 * head] + picked_ref[2 * head + 1]
        powers = jnp.exp(picked - jnp.max(picked, axis=0, keepdims=True))
        parts.append(powers / jnp.sum(powers, axis=0, keepdims=True))
    weight_ref[...] = jnp.transpose(jnp.concatenate(parts, axis=0))
    out_ref[...] = bucket_rows(high_ref, low_ref, (weight_ref,), out_ref.shape[0]).astype(bf16)


def make_weights(picked, high, low, places):
    return pl.pallas_call(
        weights_kernel,
        out_shape=[
            jax.ShapeDtypeStruct(high.shape, f32),
            jax.ShapeDtypeStruct((places // LANES, LANES), bf16),
        ],
        compiler_params=params(32),
        cost_estimate=lasting(3),
        name="make_weights",
    )(picked, high, low)


def grads_kernel(high_ref, low_ref, weight_ref, table_ref, out_ref, found_ref):
    turned = jnp.transpose(table_ref[...])
    main = turned.astype(bf16)
    rest = (turned - main.astype(f32)).astype(bf16)
    batch = 8
    for top in range(0, high_ref.shape[0], batch):
        high = jnp.concatenate(
            [
                jnp.where(hit, 1.0, 0.0).astype(bf16)
                for hit in wide_hits(table_ref.shape[0], high_ref, top, batch)
            ],
            axis=1,
        )
        found = mm(main, high) + mm(rest, high)
        low = jnp.concatenate(wide_hits(LANES, low_ref, top, batch), axis=1)
        line = jnp.sum(jnp.where(low, found, 0.0), axis=0, keepdims=True)
        for row in range(batch):
            found_ref[top + row : top + row + 1, :] = line[:, row * LANES : (row + 1) * LANES]
    grads = jnp.transpose(found_ref[...])
    weights = jnp.transpose(weight_ref[...])
    for head in range(MH):
        rows = slice(head * KPICK, (head + 1) * KPICK)
        coupled = jnp.sum(weights[rows] * grads[rows], axis=0, keepdims=True)
        out_ref[rows, :] = weights[rows] * (grads[rows] - coupled)


def pick_grads(high, low, weights, table):
    return pl.pallas_call(
        grads_kernel,
        out_shape=jax.ShapeDtypeStruct((high.shape[1], high.shape[0]), f32),
        scratch_shapes=[pltpu.VMEM(high.shape, f32)],
        compiler_params=params(32),
        cost_estimate=lasting(5),
        name="pick_grads",
    )(high, low, weights, table)


def place_rows(rows, subs, token_row, first_row):
    tokens = one_hot(rows, token_row)
    return jnp.concatenate(
        [tokens * jnp.where(first_row == first, 1.0, 0.0).astype(bf16) for first in range(subs)],
        axis=0,
    )


def spread_kernel(
    rows, subs, outer, here_ref, token_ref, first_ref, second_ref, weight_ref, value_ref, *refs
):
    table_ref, keep_ref, send_ref = refs[-3:]
    count = token_ref.shape[1]
    fold = rows // outer
    for block in range(count):
        left = place_rows(rows, subs, token_ref[0, block], first_ref[0, block])
        right = jnp.where(hits(NSUB, second_ref[0, block]), weight_ref[0, block], 0.0).astype(bf16)
        table = mm(left, right, NT).astype(bf16)
        for first in range(subs):
            table_ref[0, block * rows : (block + 1) * rows, first * NSUB : (first + 1) * NSUB] = (
                table[first * rows : (first + 1) * rows]
            )
    partial = mm(table_ref[0], value_ref[...]).astype(bf16)
    here = here_ref[0]
    chip = here // 2

    def store(core):
        for there in range(TP):
            target_ref = keep_ref if there % 2 == core else send_ref
            place = jnp.bitwise_xor(chip, there // 2)
            for block in range(count):
                for part in range(outer):
                    top = block * rows + part * fold
                    target_ref[place, 0, part, block] = partial[
                        top : top + fold, there * LANES : (there + 1) * LANES
                    ]

    pl.when(here % 2 == 0)(lambda: store(0))
    pl.when(here % 2 == 1)(lambda: store(1))


def spread_weights(
    rows, subs, heads, outer, turn, turns, here, token, first, second, weight, values, table
):
    blocks, capacity = token.shape[1], token.shape[3]
    width = values.shape[1]
    count = 2
    steps = blocks // turns // count
    fold = rows // outer
    row = pl.BlockSpec((1, count, 1, capacity), lambda h, i, s: (h, turn * steps + i, 0, 0))
    piece = pl.BlockSpec(
        (TP // 2, 1, outer, count, fold, LANES), lambda h, i, s: (0, h, 0, i, 0, 0)
    )
    piece_shape = jax.ShapeDtypeStruct(
        (TP // 2, heads, outer, blocks // turns, fold, LANES), bf16
    )
    operands = [here, token, first, second, weight, values]
    in_specs = [row, row, row, row, pl.BlockSpec(values.shape, lambda h, i, s: (0, 0))]
    aliases = {}
    if table is not None:
        operands.append(table)
        in_specs.append(pl.BlockSpec(memory_space=pl.ANY))
        aliases = {6: 0}
    return pl.pallas_call(
        lambda *refs: spread_kernel(rows, subs, outer, *refs),
        grid_spec=pltpu.PrefetchScalarGridSpec(
            num_scalar_prefetch=1,
            grid=(heads, steps),
            in_specs=in_specs,
            out_specs=[
                pl.BlockSpec(
                    (1, count * rows, subs * NSUB), lambda h, i, s: (h, turn * steps + i, 0)
                ),
                piece,
                piece,
            ],
        ),
        out_shape=[
            jax.ShapeDtypeStruct((heads, blocks * rows, subs * NSUB), bf16),
            piece_shape,
            piece_shape,
        ],
        input_output_aliases=aliases,
        compiler_params=params(48),
        cost_estimate=lasting(heads * blocks // turns * rows / 90),
        name="spread_weights",
    )(*operands)


def dots_kernel(
    rows, subs, outer, token_ref, first_ref, second_ref, grad_ref, value_ref, *refs
):
    out_ref, dense_ref = refs[-2:]
    count = token_ref.shape[1]
    fold = rows // outer
    for block in range(count):
        for part in range(outer):
            top = block * rows + part * fold
            for there in range(TP):
                dense_ref[0, top : top + fold, there * LANES : (there + 1) * LANES] = grad_ref[
                    0, part, there, block
                ]
    dense = dense_ref[0]
    found = [
        mm(value_ref[first * NSUB : (first + 1) * NSUB, :], dense, NT).astype(bf16)
        for first in range(subs)
    ]
    for block in range(count):
        left = place_rows(rows, subs, token_ref[0, block], first_ref[0, block])
        table = jnp.concatenate(
            [
                found[first][:, block * rows : (block + 1) * rows] for first in range(subs)
            ],
            axis=1,
        )
        spread = mm(table, left)
        out_ref[0, block] = jnp.sum(
            jnp.where(hits(NSUB, second_ref[0, block]), spread, 0.0), axis=0, keepdims=True
        )


def row_dots(rows, subs, head, outer, token, first, second, grads, values, dense):
    heads, blocks, capacity = token.shape[0], token.shape[1], token.shape[3]
    width = values.shape[1]
    count = 2
    fold = rows // outer
    row = pl.BlockSpec((1, count, 1, capacity), lambda i: (head, i, 0, 0))
    operands = [token, first, second, grads, values]
    in_specs = [
        row,
        row,
        row,
        pl.BlockSpec((1, outer, TP, count, fold, LANES), lambda i: (head, 0, 0, i, 0, 0)),
        pl.BlockSpec(values.shape, lambda i: (0, 0)),
    ]
    aliases = {}
    if dense is not None:
        operands.append(dense)
        in_specs.append(pl.BlockSpec(memory_space=pl.ANY))
        aliases = {5: 1}
    return pl.pallas_call(
        lambda *refs: dots_kernel(rows, subs, outer, *refs),
        grid=(blocks // count,),
        in_specs=in_specs,
        out_specs=[
            pl.BlockSpec((1, count, 1, capacity), lambda i: (0, i, 0, 0)),
            pl.BlockSpec((1, count * rows, width), lambda i: (head, i, 0)),
        ],
        out_shape=[
            jax.ShapeDtypeStruct((1, blocks, 1, capacity), f32),
            jax.ShapeDtypeStruct((heads, blocks * rows, width), bf16),
        ],
        input_output_aliases=aliases,
        compiler_params=params(48),
        cost_estimate=lasting(blocks * rows / 90),
        name="row_dots",
    )(*operands)


def value_grads_kernel(table_ref, dense_ref, *refs):
    out_ref = refs[-1]
    out_ref[...] = mm(table_ref[...], dense_ref[...], TN)


def value_grads(turn, turns, table, dense, sums):
    tokens, own_rows = table.shape
    width = dense.shape[1]
    block = min(512, own_rows // turns)
    steps = own_rows // turns // block
    operands = [table, dense]
    in_specs = [
        pl.BlockSpec((tokens, block), lambda i: (0, turn * steps + i)),
        pl.BlockSpec(dense.shape, lambda i: (0, 0)),
    ]
    aliases = {}
    if sums is not None:
        operands.append(sums)
        in_specs.append(pl.BlockSpec(memory_space=pl.ANY))
        aliases = {2: 0}
    return pl.pallas_call(
        value_grads_kernel,
        grid=(steps,),
        in_specs=in_specs,
        out_specs=pl.BlockSpec((block, width), lambda i: (turn * steps + i, 0)),
        out_shape=jax.ShapeDtypeStruct((own_rows, width), f32),
        input_output_aliases=aliases,
        compiler_params=params(56),
        cost_estimate=lasting(15 * 2 / turns),
        name="value_grads",
    )(*operands)


def pick_kernel(query_ref, table_ref, index_ref, out_ref):
    scores = mm(query_ref[...], table_ref[...], NT)
    index = index_ref[...]
    place = jnp.bitwise_and(index, LANES - 1)
    low = jnp.take_along_axis(scores[:, :LANES], place, axis=1)
    high = jnp.take_along_axis(scores[:, LANES:], place, axis=1)
    out_ref[...] = jnp.transpose(jnp.where(index < LANES, low, high))[:KPICK]


def pick_scores(query, table, index):
    rows = query.shape[0]
    block = 256
    return pl.pallas_call(
        pick_kernel,
        grid=(rows // block,),
        in_specs=[
            pl.BlockSpec((block, QHALF), lambda i: (i, 0)),
            pl.BlockSpec((NSUB, QHALF), lambda i: (0, 0)),
            pl.BlockSpec((block, LANES), lambda i: (i, 0)),
        ],
        out_specs=pl.BlockSpec((KPICK, block), lambda i: (0, i)),
        out_shape=jax.ShapeDtypeStruct((KPICK, rows), f32),
        compiler_params=params(32),
        cost_estimate=lasting(rows / 600),
        name="pick_scores",
    )(query, table, index)


def unpick_kernel(grad_ref, index_ref, table_ref, sub_ref, query_ref):
    count = grad_ref.shape[1]
    place = lax.broadcasted_iota(jnp.int32, (NSUB, count), 0)
    total = jnp.zeros((NSUB, count), f32)
    for pick in range(KPICK):
        hit = place == index_ref[pick : pick + 1, :]
        total = total + jnp.where(hit, grad_ref[pick : pick + 1, :], 0.0)
    low = total.astype(bf16)
    sub_ref[...] = low
    query_ref[...] = mm(low, table_ref[...], TN).astype(bf16)


def unpick_scores(grads, index, table):
    rows = grads.shape[1]
    block = 256
    return pl.pallas_call(
        unpick_kernel,
        grid=(rows // block,),
        in_specs=[
            pl.BlockSpec((KPICK, block), lambda i: (0, i)),
            pl.BlockSpec((KPICK, block), lambda i: (0, i)),
            pl.BlockSpec((NSUB, QHALF), lambda i: (0, 0)),
        ],
        out_specs=[
            pl.BlockSpec((NSUB, block), lambda i: (0, i)),
            pl.BlockSpec((block, QHALF), lambda i: (i, 0)),
        ],
        out_shape=[
            jax.ShapeDtypeStruct((NSUB, rows), bf16),
            jax.ShapeDtypeStruct((rows, QHALF), bf16),
        ],
        compiler_params=params(32),
        cost_estimate=lasting(rows / 180),
        name="unpick_scores",
    )(grads, index, table)


def swap(array, axes):
    return lax.all_to_all(array, axes, split_axis=0, concat_axis=0, tiled=True)


def gather(array, axes):
    return lax.all_gather(array, axes, axis=0, tiled=True)


def across(array, distance):
    return lax.ppermute(array, "tp", [(at, at ^ distance) for at in range(TP)])


def onward(array, count, step):
    pairs = [(at, at + step) for at in range(count) if 0 <= at + step < count]
    return lax.ppermute(array, GROUP, pairs)


def gather_tp(own):
    half = own.shape[0] // 2
    near = across(own, 2)
    next_one = across(own, 4)
    far = jnp.concatenate([across(near[:half], 4), across(next_one[half:], 2)])
    quad = jnp.stack([own, near, next_one, far])
    both = jnp.stack([quad, across(quad, 1)], axis=1)
    return both.reshape((TP * own.shape[0],) + own.shape[1:])


def halves(array):
    blocks = array.reshape((TP // 2, 2, -1) + array.shape[1:])
    return tuple(blocks[:, core].reshape((-1,) + array.shape[1:]) for core in range(2))


def sum_back_start(left, right, dims, rows):
    keep_left, send_left = halves(left)
    met = across(mm(send_left, right, dims).astype(bf16), 1)
    return mm(keep_left, right, dims).reshape(4, rows, -1), met.reshape(4, rows, -1)


def first_hop(keep, met):
    half = keep.shape[1] // 2
    sums = keep + met.astype(f32)
    stay = (sums[0::2, :half], sums[:2, half:])
    got = (across(sums[1::2, :half].astype(bf16), 2), across(sums[2:, half:].astype(bf16), 4))
    return stay, got


def second_hop(stay, got):
    sums = (stay[0] + got[0].astype(f32), stay[1] + got[1].astype(f32))
    got = (across(sums[0][1].astype(bf16), 4), across(sums[1][1].astype(bf16), 2))
    return (sums[0][0], sums[1][0]), got


def last_hop(stay, got):
    return jnp.concatenate(
        [stay[0] + got[0].astype(f32), stay[1] + got[1].astype(f32)], axis=0
    )


def sum_back(left, right, dims, rows):
    return last_hop(*second_hop(*first_hop(*sum_back_start(left, right, dims, rows))))


def chip_sums(keep_ref, met_ref, chip, half):
    size = keep_ref.shape[2] // 2
    rows = slice(half * size, (half + 1) * size)
    return keep_ref[chip, 0, rows].astype(f32) + met_ref[chip, 0, rows].astype(f32)


def leave_kernel(keep_ref, met_ref, along_ref, aside_ref):
    for turn in range(2):
        along_ref[turn, 0] = chip_sums(keep_ref, met_ref, 2 * turn + 1, 0).astype(bf16)
        aside_ref[turn, 0] = chip_sums(keep_ref, met_ref, 2 + turn, 1).astype(bf16)


def pass_kernel(keep_ref, met_ref, along_ref, aside_ref, out_along_ref, out_aside_ref):
    along = chip_sums(keep_ref, met_ref, 2, 0) + along_ref[1, 0].astype(f32)
    aside = chip_sums(keep_ref, met_ref, 1, 1) + aside_ref[1, 0].astype(f32)
    out_along_ref[0] = along.astype(bf16)
    out_aside_ref[0] = aside.astype(bf16)


def total_kernel(keep_ref, met_ref, along_ref, aside_ref, far_ref, side_ref, out_ref):
    size = keep_ref.shape[2] // 2
    along = chip_sums(keep_ref, met_ref, 0, 0) + along_ref[0, 0].astype(f32)
    aside = chip_sums(keep_ref, met_ref, 0, 1) + aside_ref[0, 0].astype(f32)
    out_ref[0, :size] = (along + far_ref[0].astype(f32)).astype(bf16)
    out_ref[0, size:] = (aside + side_ref[0].astype(f32)).astype(bf16)


def hop_call(kernel, name, keep, outs, *operands):
    groups, rows = keep.shape[1:3]
    four = pl.BlockSpec((4, 1, rows, LANES), lambda i: (0, i, 0, 0))
    two = pl.BlockSpec((2, 1, rows // 2, LANES), lambda i: (0, i, 0, 0))
    one = pl.BlockSpec((1, rows // 2, LANES), lambda i: (i, 0, 0))
    whole = pl.BlockSpec((1, rows, LANES), lambda i: (i, 0, 0))
    specs = {"two": two, "one": one, "whole": whole}
    shapes = {
        "two": (2, groups, rows // 2, LANES),
        "one": (groups, rows // 2, LANES),
        "whole": (groups, rows, LANES),
    }
    return pl.pallas_call(
        kernel,
        grid=(groups,),
        in_specs=[four, four, two, two, one, one][: len(operands) + 1],
        out_specs=[specs[out] for out in outs],
        out_shape=[jax.ShapeDtypeStruct(shapes[out], bf16) for out in outs],
        compiler_params=params(32),
        cost_estimate=lasting(keep.size / 5e5),
        name=name,
    )(keep, *operands)


def sum_groups_start(total, groups, group_index):
    parts = [lax.dynamic_index_in_dim(total, group_index, 0, keepdims=False)]
    low = total.astype(bf16)
    for away in range(1, groups):
        piece = lax.dynamic_index_in_dim(
            low, lax.rem(group_index + away, groups), 0, keepdims=False
        )
        pairs = [(at, (at + away) % groups) for at in range(groups)]
        parts.append(lax.ppermute(piece, GROUP, pairs))
    return parts


def sum_groups(total, groups, group_index):
    return sum(part.astype(f32) for part in sum_groups_start(total, groups, group_index))


def shift(own, groups, away):
    return lax.ppermute(own, GROUP, [(at, (at + away) % groups) for at in range(groups)])


def by_group(own, shifts, groups, group_index):
    result = jnp.zeros((groups,) + own.shape, own.dtype)
    result = lax.dynamic_update_index_in_dim(result, own, group_index, 0)
    for away, piece in shifts.items():
        source = lax.rem(group_index + groups - away, groups)
        result = lax.dynamic_update_index_in_dim(result, piece, source, 0)
    return result


def tie(*arrays):
    return lax.optimization_barrier(arrays)


def norm_scale(hidden):
    return lax.rsqrt(jnp.mean(hidden * hidden, axis=-1, keepdims=True) + epsilon)


def norm_back(hidden, scale, weighted):
    coupled = jnp.mean(hidden * weighted, axis=-1, keepdims=True)
    return scale * weighted - hidden * (scale * scale * scale) * coupled


def body(
    inputs,
    attn_gain,
    attn_qkv,
    attn_out,
    memory_gain,
    memory_query,
    sub_keys,
    memory_gate,
    memory_out,
    memory_values,
    doc_lengths,
    token_order,
    memory_picks,
    cotangent,
):
    rows, width = inputs.shape
    outer = lax.axis_size("outer")
    heads = lax.axis_size("head")
    groups = heads * outer
    blocks = outer * TP
    devices = groups * TP
    share = rows // blocks
    fold = TP * share
    span = TP * rows
    tokens = token_order.shape[0]
    head_index = lax.axis_index("head")
    outer_index = lax.axis_index("outer")
    here = lax.axis_index("tp")
    here_word = here.astype(jnp.int32)[None]
    group_index = head_index * outer + outer_index
    rows_w = attn_qkv.shape[0]
    subs = memory_values.shape[0] // NSUB
    picks = MH * KPICK
    capacity = 2 * rows * picks // devices
    back = min(groups - 1, -(-(tokens // 2 - 1) // span))
    base = back * span

    group_inputs = gather_tp(inputs)
    gain_one = attn_gain.astype(f32)[:, None]
    gain_two = memory_gain.astype(f32)[:, None]
    scaled_qkv = (attn_qkv.astype(f32) * gain_one).astype(bf16)
    scaled_query = (memory_query.astype(f32) * gain_two).astype(bf16)
    scaled_gate = (memory_gate.astype(f32) * gain_two).astype(bf16)
    qkv_cut = jnp.transpose(scaled_qkv.reshape(rows_w, 3, TP, LANES), (2, 0, 1, 3))
    qkv_cut = jnp.broadcast_to(
        qkv_cut.reshape(1, TP, rows_w, 3 * LANES), (groups, TP, rows_w, 3 * LANES)
    ).reshape(devices, rows_w, 3 * LANES)
    weight_qkv = swap(qkv_cut, ALL).reshape(width, 3 * LANES)
    to_turned = [
        (groups * part + group, group * TP + part) for group in range(groups) for part in range(TP)
    ]
    from_turned = [(there, at) for at, there in to_turned]

    def columns(piece):
        return jnp.moveaxis(piece.reshape(rows_w, TP, -1), 1, 0)

    by_half = jnp.transpose(memory_picks.reshape(outer, fold, MH, KPICK, 2), (0, 2, 4, 3, 1))
    by_half = by_half.reshape(blocks, KPICK, fold).astype(bf16)
    rest_cut = jnp.concatenate([columns(scaled_query), columns(scaled_gate)], axis=2)
    rest_width = rest_cut.shape[2]
    row_cut = jnp.stack([attn_out, memory_out, sub_keys.reshape(rows_w, width)])

    laid = token_order.reshape(heads, blocks, outer, fold)
    mine = lax.dynamic_index_in_dim(laid, head_index, 0, keepdims=False)
    mine = lax.dynamic_index_in_dim(mine, outer_index, 1, keepdims=False)
    local = jnp.bitwise_xor(mine.reshape(span) - group_index * span, here * rows)
    span_range = jnp.arange(span, dtype=jnp.int32)
    deal = (local[:, None] == span_range[None, :]).astype(bf16)
    undeal = (span_range[:, None] == local[None, :]).astype(bf16)

    group_wide = group_inputs.astype(f32)
    normed_one = (group_wide * norm_scale(group_wide)).astype(bf16)
    projected = mm(normed_one, weight_qkv).astype(bf16)
    queries = projected[:, :LANES] * jnp.asarray(1.0 / math.sqrt(HD), bf16)
    kv_pieces = [projected[:, LANES:]]
    own_cot, own_picks, rest_cut, by_half, row_cut, unused = tie(
        cotangent, memory_picks, rest_cut, by_half, row_cut, kv_pieces[0]
    )
    if back > 0:
        kv_pieces.insert(0, onward(kv_pieces[0], groups, 1))
    group_cot = gather_tp(own_cot)
    row_cut = lax.ppermute(row_cut, ALL, to_turned)
    attn_shifts = {away: shift(row_cut[0], groups, away) for away in range(1, groups)}
    weight_attn = by_group(row_cut[0], attn_shifts, groups, group_index).reshape(LANES, width)
    if by_half.shape[:2] == rest_cut.shape[:2]:
        both = swap(jnp.concatenate([rest_cut, by_half], axis=2), "tp")
        rest_rows, by_half = both[:, :, :rest_width], both[:, :, rest_width:]
    else:
        rest_rows, by_half = swap(rest_cut, "tp"), swap(by_half, BLK)
    rest_rows = rest_rows.reshape(TP * rows_w, rest_width)
    kv_pieces[0], rest_rows = tie(kv_pieces[0], rest_rows)
    for away in range(1, back):
        kv_pieces.insert(0, onward(kv_pieces[0], groups, 1))

    first_pick = own_picks[:, :, :, 0].reshape(rows, picks)
    second_pick = own_picks[:, :, :, 1].reshape(rows, picks)
    owner = first_pick // subs
    device_range = jnp.arange(devices, dtype=jnp.int32)
    owned = (owner[None] == device_range[:, None, None]).astype(bf16)
    before = (
        jnp.arange(picks, dtype=jnp.int32)[:, None] < jnp.arange(picks, dtype=jnp.int32)[None, :]
    ).astype(bf16)
    before_rows = (
        jnp.arange(rows, dtype=jnp.int32)[:, None] < jnp.arange(rows, dtype=jnp.int32)[None, :]
    ).astype(bf16)
    in_row = jnp.einsum("dtk,kj->dtj", owned, before, preferred_element_type=f32)
    row_counts = jnp.sum(owned.astype(f32), axis=2)
    of_rows = jnp.dot(row_counts.astype(bf16), before_rows, preferred_element_type=f32)
    rank = jnp.sum(owned.astype(f32) * (in_row + of_rows[:, :, None]), axis=0).astype(jnp.int32)
    target = owner * capacity + rank
    target_high = target // LANES
    target_low = target % LANES
    places = devices * capacity
    entries = make_entries(target_high, target_low, first_pick % subs, second_pick, places)

    turned_one, unused = tie(jnp.transpose(normed_one), kv_pieces[0])
    keys_values, rest_rows, by_half, entries, turned_one, group_cot, row_cut = tie(
        jnp.concatenate(kv_pieces, axis=0),
        rest_rows,
        by_half,
        entries,
        turned_one,
        group_cot,
        row_cut,
    )
    half_index = jnp.moveaxis(by_half, 1, 0).reshape(KPICK, span).astype(jnp.int32)
    wide_index = jnp.pad(jnp.transpose(half_index), ((0, 0), (0, LANES - KPICK)))
    rest_shifts = {away: shift(rest_rows, groups, away) for away in range(1, groups, 2)}
    doc_ends = jnp.cumsum(doc_lengths)

    def lowest(inside):
        positions = group_index * span + inside
        starts = jnp.where(positions[:, None] >= doc_ends[None, :], doc_ends[None, :], 0)
        return jnp.max(starts, axis=1) - (group_index - back) * span

    low_first = lowest(span_range)
    low = lowest(jnp.bitwise_xor(span_range, here * rows))
    attended, lse, attended_low = attn_fwd(
        base, rows, low_first, here_word, low, queries, keys_values
    )
    attended_low, rest_rows, *shifted = tie(attended_low, rest_rows, *rest_shifts.values())
    rest_shifts = dict(zip(rest_shifts, shifted))
    even_shifts = {away: shift(rest_rows, groups, away) for away in range(2, groups, 2)}
    inputs_wide = inputs.astype(f32)
    hidden_one = inputs_wide + sum_back(attended_low, weight_attn, NN, rows)
    hidden_one, row_cut, *shifted = tie(hidden_one, row_cut, *even_shifts.values())
    rest_shifts.update(zip(even_shifts, shifted))
    weight_rest = by_group(rest_rows, rest_shifts, groups, group_index).reshape(width, rest_width)
    row_shifts = {away: shift(row_cut[1:], groups, away) for away in range(1, groups)}
    row_all = by_group(row_cut[1:], row_shifts, groups, group_index)
    row_all = jnp.moveaxis(row_all, 0, 1).reshape(2, LANES, width)
    weight_mixed = row_all[0]
    key_table = row_all[1].reshape(NSUB, QHALF)
    scale_two = norm_scale(hidden_one)
    group_cot, unused = tie(group_cot, attended_low)
    dealt_cot = mm(deal, group_cot).astype(bf16)
    grad_mixed = mm(dealt_cot, weight_mixed, NT)
    normed_two = mm(deal, gather_tp((hidden_one * scale_two).astype(bf16))).astype(bf16)

    pre = mm(normed_two, weight_rest)
    query_mem = pre[:, :QHALF].astype(bf16)
    gate_pre = pre[:, QHALF:]
    gate_sig = jax.nn.sigmoid(gate_pre)
    grad_memory = (grad_mixed * gate_pre * gate_sig).astype(bf16)
    query_mem, grad_memory = tie(query_mem, grad_memory)
    every_grad = gather(grad_memory, ALL).reshape(heads, outer, TP, blocks, fold, LANES)
    picked_half = pick_scores(query_mem, key_table, wide_index).reshape(KPICK, blocks, fold)
    picked = swap(jnp.moveaxis(picked_half, 1, 0), BLK)
    turned_two, unused = tie(jnp.transpose(normed_two), picked_half)
    picked, turned_two = tie(picked, turned_two)
    picked = jnp.moveaxis(picked.reshape(outer, TP, KPICK, fold), 0, 2).reshape(TP, KPICK, rows)
    pick_weights, sent_weights = make_weights(picked, target_high, target_low, places)
    sent = jnp.concatenate([entries, sent_weights], axis=1)
    sent = jnp.moveaxis(sent.reshape(devices, capacity // LANES, 4, LANES), 2, 1)
    entries = swap(sent.reshape(devices, 4, capacity), ALL).astype(f32)
    entries = entries.reshape(heads, blocks, 4, 1, capacity)
    entry_token = entries[:, :, 0].astype(jnp.int32)
    entry_first = entries[:, :, 1].astype(jnp.int32)
    entry_second = entries[:, :, 2].astype(jnp.int32)
    entry_weight = entries[:, :, 3]

    turns = 2
    table = None
    leaving = []
    flat = (TP // 2, groups, span // turns, LANES)
    for turn in range(turns):
        table, keep, send = spread_weights(
            rows,
            subs,
            heads,
            outer,
            turn,
            turns,
            here_word,
            entry_token,
            entry_first,
            entry_second,
            entry_weight,
            memory_values,
            table,
        )
        leaving.append((keep.reshape(flat), across(send.reshape(flat), 1)))
    leaves = []
    for keep, met in leaving:
        leaves += hop_call(leave_kernel, "sums_first", keep, ("two", "two"), met)

    parts = [None] * heads

    def dots(head, dense, *moved):
        parts[head], dense = row_dots(
            rows,
            subs,
            head,
            outer,
            entry_token,
            entry_first,
            entry_second,
            every_grad,
            memory_values,
            dense,
        )
        parts[head], dense, *moved = tie(parts[head], dense, *moved)
        return dense, moved

    every_grad, *leaves = tie(every_grad, *leaves)
    first = [across(leaf, (2, 4)[turn % 2]) for turn, leaf in enumerate(leaves)]
    dense, unused = dots(0, None)
    dense, first = dots(1, dense, *first)
    leaves = []
    for turn, (keep, met) in enumerate(leaving):
        leaves += hop_call(
            pass_kernel, "sums_second", keep, ("one", "one"), met, *first[2 * turn : 2 * turn + 2]
        )
    dense, *leaves = tie(dense, *leaves)
    second = [across(leaf, (4, 2)[turn % 2]) for turn, leaf in enumerate(leaves)]
    dense, second = dots(2, dense, *second)
    total = jnp.concatenate(
        [
            hop_call(
                total_kernel,
                "sums_last",
                keep,
                ("whole",),
                met,
                *first[2 * turn : 2 * turn + 2],
                *second[2 * turn : 2 * turn + 2],
            )[0]
            for turn, (keep, met) in enumerate(leaving)
        ],
        axis=1,
    )
    dense, total = tie(dense, total)
    dense, unused = dots(3, dense)
    for head in range(4, heads):
        dense, unused = dots(head, dense)
    memory = sum_groups(total, groups, group_index)

    entry_dots = jnp.concatenate(parts, axis=0).reshape(devices, capacity)
    returned = swap(entry_dots, ALL).reshape(places // LANES, LANES)
    table = table.reshape(tokens, subs * NSUB)
    dense = dense.reshape(tokens, width)
    grad_values = value_grads(0, turns, table, dense, None)
    returned, grad_values = tie(returned, grad_values)
    grad_picked = pick_grads(target_high, target_low, pick_weights, returned)
    to_half = jnp.moveaxis(grad_picked.reshape(MH, KPICK, outer, fold), 2, 0)
    to_half = jnp.broadcast_to(to_half[:, :, None], (outer, MH, 2, KPICK, fold))
    grad_half = swap(to_half.reshape(blocks, KPICK, fold), BLK)
    grad_half = jnp.moveaxis(grad_half, 1, 0).reshape(KPICK, span)
    grad_sub, grad_query = unpick_scores(grad_half, half_index, key_table)

    mixed_low = (memory * gate_pre * gate_sig).astype(bf16)
    grad_gate = (grad_mixed * memory * gate_sig * (1.0 + gate_pre * (1.0 - gate_sig))).astype(bf16)
    grad_pre = jnp.concatenate([grad_query, grad_gate], axis=1)
    home_pre = mm(undeal, grad_pre).astype(bf16)

    keep, met = sum_back_start(home_pre, weight_rest, NT, rows)
    met, grad_pre, mixed_low, grad_sub = tie(met, grad_pre, mixed_low, grad_sub)
    stay, got = first_hop(keep, met)
    rest_grads = mm(turned_two, grad_pre).astype(bf16)
    row_grads = [mm(mixed_low, dealt_cot, TN), mm(grad_sub, query_mem).reshape(LANES, width)]
    row_grads = jnp.stack(row_grads).astype(bf16).reshape(2, groups, rows_w, width)
    row_grads = jnp.moveaxis(row_grads, 0, 1).reshape(groups * TP * rows_w, -1)
    memory_grads = jnp.concatenate([rest_grads, row_grads], axis=1)
    got_0, got_1, memory_grads = tie(*got, memory_grads)
    weighted_two = last_hop(*second_hop(stay, (got_0, got_1)))
    memory_grads = lax.psum_scatter(memory_grads, GROUP, scatter_dimension=0, tiled=True)
    grad_hidden = cotangent.astype(f32) + norm_back(hidden_one, scale_two, weighted_two)

    grad_branch = gather_tp(grad_hidden.astype(bf16))
    grad_attended = mm(grad_branch, weight_attn, NT).astype(bf16)
    grad_q, *grad_kv = attn_bwd(
        base, rows, low_first, here_word, low, queries, keys_values, lse, attended, grad_attended
    )
    mixed_low, table, memory_grads, *grad_kv = tie(mixed_low, table, memory_grads, *grad_kv)
    home_mixed = mm(undeal, mixed_low).astype(bf16)
    output_stay, output_got = first_hop(*sum_back_start(home_mixed, weight_mixed, NN, rows))
    carry = grad_kv[0]
    for away in range(back):
        met = onward(carry, groups, -1)
        if away == 0:
            grad_values = value_grads(1, turns, table, dense, grad_values)
            met, grad_values, memory_grads, *output_got = tie(
                met, grad_values, memory_grads, *output_got
            )
        carry = (grad_kv[away + 1].astype(f32) + met.astype(f32)).astype(bf16)
    if back == 0:
        grad_values = value_grads(1, turns, table, dense, grad_values)
    output_stay, output_got = second_hop(output_stay, output_got)
    output = (hidden_one + last_hop(output_stay, output_got)).astype(bf16)

    def columns_home(cut, *splits):
        home = jnp.moveaxis(swap(cut.reshape(TP, rows_w, -1), "tp"), 0, 1).astype(f32)
        return jnp.split(home, splits, axis=2)

    query_home, gate_home = columns_home(memory_grads[:, :rest_width], QHALF)
    query_home = query_home.reshape(rows_w, -1)
    gate_home = gate_home.reshape(rows_w, -1)
    grad_projected = jnp.concatenate([grad_q, carry], axis=1)
    grad_projected, output, query_home, gate_home = tie(
        grad_projected, output, query_home, gate_home
    )

    stay, got = first_hop(*sum_back_start(grad_projected, weight_qkv, NT, rows))
    late_grads = mm(turned_one, grad_projected).reshape(groups, TP * rows_w, 3 * LANES)
    attn_rows = mm(attended_low, grad_branch, TN).reshape(groups, TP * rows_w, LANES)
    late_grads = jnp.concatenate([late_grads, attn_rows], axis=2)
    late_parts = sum_groups_start(late_grads, groups, group_index)
    got_0, got_1, *late_parts = tie(*got, *late_parts)
    stay, got = second_hop(stay, (got_0, got_1))
    late_grads = sum(part.astype(f32) for part in late_parts).astype(bf16)
    got_0, got_1, late_grads = tie(*got, late_grads)
    weighted_one = last_hop(stay, (got_0, got_1))
    grad_inputs = grad_hidden + norm_back(inputs_wide, norm_scale(inputs_wide), weighted_one)
    qkv_home = columns_home(late_grads[:, : 3 * LANES])[0]
    qkv_home = jnp.moveaxis(qkv_home.reshape(rows_w, TP, 3, LANES), 1, 2).reshape(rows_w, -1)
    row_sums = memory_grads[:, rest_width:].reshape(2, rows_w, width)
    row_home = jnp.concatenate([late_grads[:, 3 * LANES :].reshape(1, rows_w, width), row_sums])
    row_home = lax.ppermute(row_home, ALL, from_turned).astype(f32)
    grad_attn_gain = jnp.sum(qkv_home * attn_qkv.astype(f32), axis=1)
    grad_memory_gain = jnp.sum(query_home * memory_query.astype(f32), axis=1) + jnp.sum(
        gate_home * memory_gate.astype(f32), axis=1
    )
    return (
        output,
        grad_inputs,
        grad_attn_gain,
        qkv_home * gain_one,
        row_home[0],
        grad_memory_gain,
        query_home * gain_two,
        row_home[2].reshape(sub_keys.shape),
        gate_home * gain_two,
        row_home[1],
        grad_values,
    )


def solution(mesh):
    heads, blocks = mesh.devices.shape
    cut_mesh = Mesh(mesh.devices.reshape(heads, blocks // TP, TP), ALL)
    matrix = P(ALL, None)
    in_specs = (
        matrix,
        P(ALL),
        matrix,
        matrix,
        P(ALL),
        matrix,
        matrix,
        matrix,
        matrix,
        matrix,
        P(),
        P(),
        P(ALL, None, None, None),
        matrix,
    )
    out_specs = (
        matrix,
        matrix,
        P(ALL),
        matrix,
        matrix,
        P(ALL),
        matrix,
        matrix,
        matrix,
        matrix,
        matrix,
    )
    return jax.shard_map(
        body, mesh=cut_mesh, in_specs=in_specs, out_specs=out_specs, check_vma=False
    )
```

```python
import math

import jax
import jax.numpy as jnp
from jax import lax
from jax.experimental import pallas as pl
from jax.experimental.pallas import tpu as pltpu
from jax.sharding import Mesh
from jax.sharding import PartitionSpec as P

NH = 16
HD = 64
MH = 4
QHALF = 512
NSUB = 256
KPICK = 32
TP = 2 * MH

GROUP = ("head", "outer")
BLK = ("outer", "tp")
ALL = ("head", "outer", "tp")

epsilon = 1e-06
neg_big = -1e30
LANES = 128
bf16 = jnp.bfloat16
f32 = jnp.float32
NN = (((1,), (0,)), ((), ()))
NT = (((1,), (1,)), ((), ()))
TN = (((0,), (0,)), ((), ()))


def mm(left, right, dims=NN):
    return lax.dot_general(left, right, dims, preferred_element_type=f32)


def params(mib):
    return pltpu.CompilerParams(vmem_limit_bytes=mib * 1024 * 1024)


def lasting(microseconds):
    return pl.CostEstimate(
        flops=0, bytes_accessed=int(microseconds * 3.5e6), transcendentals=0
    )


def head_rows(pair):
    lane = lax.broadcasted_iota(jnp.int32, pair.shape, 1)
    zero = jnp.zeros_like(pair)
    return (jnp.where(lane < HD, pair, zero), jnp.where(lane < HD, zero, pair))


def turned_block(step, here, block, rows):
    return jnp.bitwise_xor(step, here * rows // block)


def turned_iota(shape, axis, here, rows):
    place = lax.broadcasted_iota(jnp.int32, shape, axis)
    return jnp.bitwise_xor(place, lax.rem(here * rows, shape[axis]))


def key_blocks(step, base, block_q, block_k, low_first_ref):
    return (
        low_first_ref[step] // block_k,
        (base + (step + 1) * block_q - 1) // block_k + 1,
    )


def key_start(turn, span, here, block_k, rows):
    per_group = span // block_k
    group = turn // per_group
    within = turned_block(lax.rem(turn, per_group), here, block_k, rows)
    return pl.multiple_of(group * span + within * block_k, block_k)


def attn_fwd_kernel(
    base, span, rows, block_k, low_first_ref, here_ref, q_ref, kv_ref, low_ref, att_ref, lse_ref, out_ref
):
    block_q = q_ref.shape[0]
    step = pl.program_id(0)
    here = here_ref[0]
    first, stop = key_blocks(step, base, block_q, block_k, low_first_ref)
    queries = head_rows(q_ref[...])
    low = low_ref[...]
    high = base + step * block_q + turned_iota((1, block_q), 1, here, rows)
    inner = turned_iota((block_k, block_q), 0, here, rows)

    def visit(turn, carried):
        start = key_start(turn, span, here, block_k, rows)
        keys = kv_ref[pl.ds(start, block_k), :LANES]
        values = kv_ref[pl.ds(start, block_k), LANES:]
        place = turn * block_k + inner
        allowed = (place >= low) & (place <= high)
        out = []
        for head in range(2):
            run_max, run_sum, run_acc = carried[head]
            scores = jnp.where(allowed, mm(keys, queries[head], NT), neg_big)
            new_max = jnp.maximum(run_max, jnp.max(scores, axis=0, keepdims=True))
            powers = jnp.exp(scores - new_max)
            rescale = jnp.exp(run_max - new_max)
            run_sum = run_sum * rescale + jnp.sum(powers, axis=0, keepdims=True)
            run_acc = run_acc * rescale + mm(values, powers.astype(bf16), TN)
            out.append((new_max, run_sum, run_acc))
        return tuple(out)

    fresh = (
        jnp.full((1, block_q), neg_big, f32),
        jnp.zeros((1, block_q), f32),
        jnp.zeros((LANES, block_q), f32),
    )
    done = lax.fori_loop(first, stop, visit, (fresh, fresh))
    att_ref[:HD, :] = done[0][2][:HD] / done[0][1]
    att_ref[HD:, :] = done[1][2][HD:] / done[1][1]
    out_ref[...] = jnp.transpose(att_ref[...]).astype(bf16)
    lse_ref[0:1, :] = done[0][0] + jnp.log(done[0][1])
    lse_ref[1:2, :] = done[1][0] + jnp.log(done[1][1])


def attn_specs(block_q, rows, span):
    def turn(i, here):
        return turned_block(i, here[0], block_q, rows)

    return (
        pl.BlockSpec((block_q, LANES), lambda i, s, here: (turn(i, here), 0)),
        pl.BlockSpec((1, block_q), lambda i, s, here: (0, turn(i, here))),
        pl.BlockSpec((2, block_q), lambda i, s, here: (0, turn(i, here))),
        pl.BlockSpec((LANES, block_q), lambda i, s, here: (0, turn(i, here))),
    )


def attn_fwd(base, rows, low_first, here, low, queries, keys_values):
    span = queries.shape[0]
    block_q, block_k = 512, 512
    by_row, one_lane, two_lane, by_lane = attn_specs(block_q, rows, span)
    return pl.pallas_call(
        lambda *refs: attn_fwd_kernel(base, span, rows, block_k, *refs),
        grid_spec=pltpu.PrefetchScalarGridSpec(
            num_scalar_prefetch=2,
            grid=(span // block_q,),
            in_specs=[
                by_row,
                pl.BlockSpec(keys_values.shape, lambda i, s, here: (0, 0)),
                one_lane,
            ],
            out_specs=[by_lane, two_lane, by_row],
        ),
        out_shape=[
            jax.ShapeDtypeStruct((LANES, span), f32),
            jax.ShapeDtypeStruct((2, span), f32),
            jax.ShapeDtypeStruct((span, LANES), bf16),
        ],
        compiler_params=params(24),
        cost_estimate=lasting(keys_values.shape[0] / 250),
        name="attn_fwd",
    )(low_first[::block_q], here, queries, keys_values, low[None, :])


def attn_bwd_kernel(
    base,
    span,
    rows,
    block_k,
    low_first_ref,
    here_ref,
    q_ref,
    kv_ref,
    low_ref,
    lse_ref,
    att_ref,
    grad_ref,
    dq_ref,
    *refs,
):
    dk_ref, dv_ref = refs[-2:]
    block_q = q_ref.shape[0]
    step = pl.program_id(0)
    here = here_ref[0]
    first, stop = key_blocks(step, base, block_q, block_k, low_first_ref)

    @pl.when(step == 0)
    def clear():
        dk_ref[...] = jnp.zeros_like(dk_ref)
        dv_ref[...] = jnp.zeros_like(dv_ref)

    queries = head_rows(q_ref[...])
    grads = head_rows(grad_ref[...])
    grad_turned = jnp.transpose(grad_ref[...].astype(f32)) * att_ref[...]
    deltas = (
        jnp.sum(grad_turned[:HD], axis=0, keepdims=True),
        jnp.sum(grad_turned[HD:], axis=0, keepdims=True),
    )
    low = low_ref[...]
    high = base + step * block_q + turned_iota((1, block_q), 1, here, rows)
    inner = turned_iota((block_k, block_q), 0, here, rows)

    def visit(turn, carried):
        start = key_start(turn, span, here, block_k, rows)
        keys = kv_ref[pl.ds(start, block_k), :LANES]
        values = kv_ref[pl.ds(start, block_k), LANES:]
        place = turn * block_k + inner
        allowed = (place >= low) & (place <= high)
        out = []
        grad_key = dk_ref[pl.ds(start, block_k), :]
        grad_value = dv_ref[pl.ds(start, block_k), :]
        for head in range(2):
            scores = mm(keys, queries[head], NT)
            probs = jnp.where(allowed, jnp.exp(scores - lse_ref[head : head + 1, :]), 0.0)
            grad_probs = mm(values, grads[head], NT)
            grad_scores = (probs * (grad_probs - deltas[head])).astype(bf16)
            grad_key = grad_key + mm(grad_scores, queries[head])
            grad_value = grad_value + mm(probs.astype(bf16), grads[head])
            out.append(carried[head] + mm(keys, grad_scores, TN))
        dk_ref[pl.ds(start, block_k), :] = grad_key
        dv_ref[pl.ds(start, block_k), :] = grad_value
        return tuple(out)

    fresh = jnp.zeros((LANES, block_q), f32)
    done = lax.fori_loop(first, stop, visit, (fresh, fresh))
    turned = jnp.concatenate([done[0][:HD], done[1][HD:]], axis=0) * (1.0 / math.sqrt(HD))
    dq_ref[...] = jnp.transpose(turned).astype(bf16)

    @pl.when(step == span // block_q - 1)
    def leave():
        for turn, out_ref in enumerate(refs[:-2]):
            out_ref[:, :LANES] = dk_ref[turn * span : (turn + 1) * span, :].astype(bf16)
            out_ref[:, LANES:] = dv_ref[turn * span : (turn + 1) * span, :].astype(bf16)


def attn_bwd(base, rows, low_first, here, low, queries, keys_values, lse, att, grads):
    span = queries.shape[0]
    block_q, block_k = 512, 512
    reach = keys_values.shape[0]
    by_row, one_lane, two_lane, by_lane = attn_specs(block_q, rows, span)
    return pl.pallas_call(
        lambda *refs: attn_bwd_kernel(base, span, rows, block_k, *refs),
        grid_spec=pltpu.PrefetchScalarGridSpec(
            num_scalar_prefetch=2,
            grid=(span // block_q,),
            in_specs=[
                by_row,
                pl.BlockSpec(keys_values.shape, lambda i, s, here: (0, 0)),
                one_lane,
                two_lane,
                by_lane,
                by_row,
            ],
            out_specs=[by_row]
            + [pl.BlockSpec((span, 2 * LANES), lambda i, s, here: (0, 0))] * (reach // span),
            scratch_shapes=[pltpu.VMEM((reach, LANES), f32), pltpu.VMEM((reach, LANES), f32)],
        ),
        out_shape=[jax.ShapeDtypeStruct((span, LANES), bf16)]
        + [jax.ShapeDtypeStruct((span, 2 * LANES), bf16)] * (reach // span),
        compiler_params=params(32),
        cost_estimate=lasting(keys_values.shape[0] / 200),
        name="attn_bwd",
    )(low_first[::block_q], here, queries, keys_values, low[None, :], lse, att, grads)


def hits(count, row):
    return lax.broadcasted_iota(jnp.int32, (count, row.shape[1]), 0) == row


def one_hot(count, row):
    return jnp.where(hits(count, row), 1.0, 0.0).astype(bf16)


def wide_hits(count, ref, top, rows):
    return [hits(count, ref[row : row + 1, :]) for row in range(top, top + rows)]


def bucket_rows(high_ref, low_ref, load_refs, places):
    batch = 8
    total = jnp.zeros((places, len(load_refs) * LANES), f32)
    for top in range(0, high_ref.shape[0], batch):
        high = [
            jnp.where(hit, 1.0, 0.0).astype(bf16) for hit in wide_hits(places, high_ref, top, batch)
        ]
        low = wide_hits(LANES, low_ref, top, batch)
        parts = [
            jnp.concatenate(
                [
                    jnp.where(low[row], load_ref[top + row : top + row + 1, :], 0.0).astype(bf16)
                    for row in range(batch)
                ],
                axis=1,
            )
            for load_ref in load_refs
        ]
        total = total + mm(jnp.concatenate(high, axis=1), jnp.concatenate(parts, axis=0), NT)
    return total


def entries_kernel(high_ref, low_ref, first_ref, second_ref, out_ref, token_ref):
    token_ref[...] = lax.broadcasted_iota(jnp.int32, token_ref.shape, 0).astype(f32)
    loads = (token_ref, first_ref, second_ref)
    out_ref[...] = bucket_rows(high_ref, low_ref, loads, out_ref.shape[0]).astype(bf16)


def make_entries(high, low, first, second, places):
    return pl.pallas_call(
        entries_kernel,
        out_shape=jax.ShapeDtypeStruct((places // LANES, 3 * LANES), bf16),
        scratch_shapes=[pltpu.VMEM(high.shape, f32)],
        compiler_params=params(16),
        cost_estimate=lasting(5),
        name="make_entries",
    )(high, low, first.astype(f32), second.astype(f32))


def weights_kernel(picked_ref, high_ref, low_ref, weight_ref, out_ref):
    parts = []
    for head in range(MH):
        picked = picked_ref[2 * head] + picked_ref[2 * head + 1]
        powers = jnp.exp(picked - jnp.max(picked, axis=0, keepdims=True))
        parts.append(powers / jnp.sum(powers, axis=0, keepdims=True))
    weight_ref[...] = jnp.transpose(jnp.concatenate(parts, axis=0))
    out_ref[...] = bucket_rows(high_ref, low_ref, (weight_ref,), out_ref.shape[0]).astype(bf16)


def make_weights(picked, high, low, places):
    return pl.pallas_call(
        weights_kernel,
        out_shape=[
            jax.ShapeDtypeStruct(high.shape, f32),
            jax.ShapeDtypeStruct((places // LANES, LANES), bf16),
        ],
        compiler_params=params(16),
        cost_estimate=lasting(3),
        name="make_weights",
    )(picked, high, low)


def grads_kernel(high_ref, low_ref, weight_ref, table_ref, out_ref, found_ref):
    turned = jnp.transpose(table_ref[...])
    main = turned.astype(bf16)
    rest = (turned - main.astype(f32)).astype(bf16)
    batch = 8
    for top in range(0, high_ref.shape[0], batch):
        high = jnp.concatenate(
            [
                jnp.where(hit, 1.0, 0.0).astype(bf16)
                for hit in wide_hits(table_ref.shape[0], high_ref, top, batch)
            ],
            axis=1,
        )
        found = mm(main, high) + mm(rest, high)
        low = jnp.concatenate(wide_hits(LANES, low_ref, top, batch), axis=1)
        line = jnp.sum(jnp.where(low, found, 0.0), axis=0, keepdims=True)
        for row in range(batch):
            found_ref[top + row : top + row + 1, :] = line[:, row * LANES : (row + 1) * LANES]
    grads = jnp.transpose(found_ref[...])
    weights = jnp.transpose(weight_ref[...])
    for head in range(MH):
        rows = slice(head * KPICK, (head + 1) * KPICK)
        coupled = jnp.sum(weights[rows] * grads[rows], axis=0, keepdims=True)
        out_ref[rows, :] = weights[rows] * (grads[rows] - coupled)


def pick_grads(high, low, weights, table):
    return pl.pallas_call(
        grads_kernel,
        out_shape=jax.ShapeDtypeStruct((high.shape[1], high.shape[0]), f32),
        scratch_shapes=[pltpu.VMEM(high.shape, f32)],
        compiler_params=params(16),
        cost_estimate=lasting(5),
        name="pick_grads",
    )(high, low, weights, table)


def place_rows(rows, subs, token_row, first_row):
    tokens = one_hot(rows, token_row)
    return jnp.concatenate(
        [tokens * jnp.where(first_row == first, 1.0, 0.0).astype(bf16) for first in range(subs)],
        axis=0,
    )


def spread_kernel(
    rows, subs, outer, here_ref, token_ref, first_ref, second_ref, weight_ref, value_ref, *refs
):
    table_ref, keep_ref, send_ref = refs[-3:]
    count = token_ref.shape[1]
    fold = rows // outer
    for block in range(count):
        left = place_rows(rows, subs, token_ref[0, block], first_ref[0, block])
        right = jnp.where(hits(NSUB, second_ref[0, block]), weight_ref[0, block], 0.0).astype(bf16)
        table = mm(left, right, NT).astype(bf16)
        for first in range(subs):
            table_ref[0, block * rows : (block + 1) * rows, first * NSUB : (first + 1) * NSUB] = (
                table[first * rows : (first + 1) * rows]
            )
    partial = mm(table_ref[0], value_ref[...]).astype(bf16)
    here = here_ref[0]
    chip = here // 2

    def store(core):
        for there in range(TP):
            target_ref = keep_ref if there % 2 == core else send_ref
            place = jnp.bitwise_xor(chip, there // 2)
            for block in range(count):
                for part in range(outer):
                    top = block * rows + part * fold
                    target_ref[place, 0, part, block] = partial[
                        top : top + fold, there * LANES : (there + 1) * LANES
                    ]

    pl.when(here % 2 == 0)(lambda: store(0))
    pl.when(here % 2 == 1)(lambda: store(1))


def spread_weights(
    rows, subs, heads, outer, turn, turns, here, token, first, second, weight, values, table
):
    blocks, capacity = token.shape[1], token.shape[3]
    width = values.shape[1]
    count = 2
    steps = blocks // turns // count
    fold = rows // outer
    row = pl.BlockSpec((1, count, 1, capacity), lambda h, i, s: (h, turn * steps + i, 0, 0))
    piece = pl.BlockSpec(
        (TP // 2, 1, outer, count, fold, LANES), lambda h, i, s: (0, h, 0, i, 0, 0)
    )
    piece_shape = jax.ShapeDtypeStruct(
        (TP // 2, heads, outer, blocks // turns, fold, LANES), bf16
    )
    operands = [here, token, first, second, weight, values]
    in_specs = [row, row, row, row, pl.BlockSpec(values.shape, lambda h, i, s: (0, 0))]
    aliases = {}
    if table is not None:
        operands.append(table)
        in_specs.append(pl.BlockSpec(memory_space=pl.ANY))
        aliases = {6: 0}
    return pl.pallas_call(
        lambda *refs: spread_kernel(rows, subs, outer, *refs),
        grid_spec=pltpu.PrefetchScalarGridSpec(
            num_scalar_prefetch=1,
            grid=(heads, steps),
            in_specs=in_specs,
            out_specs=[
                pl.BlockSpec(
                    (1, count * rows, subs * NSUB), lambda h, i, s: (h, turn * steps + i, 0)
                ),
                piece,
                piece,
            ],
        ),
        out_shape=[
            jax.ShapeDtypeStruct((heads, blocks * rows, subs * NSUB), bf16),
            piece_shape,
            piece_shape,
        ],
        input_output_aliases=aliases,
        compiler_params=params(36),
        cost_estimate=lasting(heads * blocks // turns * rows / 90),
        name="spread_weights",
    )(*operands)


def dots_kernel(
    rows, subs, outer, token_ref, first_ref, second_ref, grad_ref, value_ref, *refs
):
    out_ref, dense_ref = refs[-2:]
    count = token_ref.shape[1]
    fold = rows // outer
    for block in range(count):
        for part in range(outer):
            top = block * rows + part * fold
            for there in range(TP):
                dense_ref[0, top : top + fold, there * LANES : (there + 1) * LANES] = grad_ref[
                    0, part, there, block
                ]
    dense = dense_ref[0]
    found = [
        mm(value_ref[first * NSUB : (first + 1) * NSUB, :], dense, NT).astype(bf16)
        for first in range(subs)
    ]
    for block in range(count):
        left = place_rows(rows, subs, token_ref[0, block], first_ref[0, block])
        table = jnp.concatenate(
            [
                found[first][:, block * rows : (block + 1) * rows] for first in range(subs)
            ],
            axis=1,
        )
        spread = mm(table, left)
        out_ref[0, block] = jnp.sum(
            jnp.where(hits(NSUB, second_ref[0, block]), spread, 0.0), axis=0, keepdims=True
        )


def row_dots(rows, subs, part, parts, outer, token, first, second, grads, values, dense):
    heads, blocks, capacity = token.shape[0], token.shape[1], token.shape[3]
    width = values.shape[1]
    count = 2
    fold = rows // outer
    mine = heads // parts
    top = part * mine
    row = pl.BlockSpec((1, count, 1, capacity), lambda h, i: (top + h, i, 0, 0))
    operands = [token, first, second, grads, values]
    in_specs = [
        row,
        row,
        row,
        pl.BlockSpec((1, outer, TP, count, fold, LANES), lambda h, i: (top + h, 0, 0, i, 0, 0)),
        pl.BlockSpec(values.shape, lambda h, i: (0, 0)),
    ]
    aliases = {}
    if dense is not None:
        operands.append(dense)
        in_specs.append(pl.BlockSpec(memory_space=pl.ANY))
        aliases = {5: 1}
    return pl.pallas_call(
        lambda *refs: dots_kernel(rows, subs, outer, *refs),
        grid=(mine, blocks // count),
        in_specs=in_specs,
        out_specs=[
            pl.BlockSpec((1, count, 1, capacity), lambda h, i: (h, i, 0, 0)),
            pl.BlockSpec((1, count * rows, width), lambda h, i: (top + h, i, 0)),
        ],
        out_shape=[
            jax.ShapeDtypeStruct((mine, blocks, 1, capacity), f32),
            jax.ShapeDtypeStruct((heads, blocks * rows, width), bf16),
        ],
        input_output_aliases=aliases,
        compiler_params=params(36),
        cost_estimate=lasting(mine * blocks * rows / 90),
        name="row_dots",
    )(*operands)


def value_grads_kernel(table_ref, dense_ref, *refs):
    out_ref = refs[-1]
    out_ref[...] = mm(table_ref[...], dense_ref[...], TN)


def value_grads(turn, turns, table, dense, sums):
    tokens, own_rows = table.shape
    width = dense.shape[1]
    block = min(512, own_rows // turns)
    steps = own_rows // turns // block
    operands = [table, dense]
    in_specs = [
        pl.BlockSpec((tokens, block), lambda i: (0, turn * steps + i)),
        pl.BlockSpec(dense.shape, lambda i: (0, 0)),
    ]
    aliases = {}
    if sums is not None:
        operands.append(sums)
        in_specs.append(pl.BlockSpec(memory_space=pl.ANY))
        aliases = {2: 0}
    return pl.pallas_call(
        value_grads_kernel,
        grid=(steps,),
        in_specs=in_specs,
        out_specs=pl.BlockSpec((block, width), lambda i: (turn * steps + i, 0)),
        out_shape=jax.ShapeDtypeStruct((own_rows, width), f32),
        input_output_aliases=aliases,
        compiler_params=params(48 if dense.size <= 2**23 else 58),
        cost_estimate=lasting(15 * 2 / turns),
        name="value_grads",
    )(*operands)


def pick_kernel(query_ref, table_ref, index_ref, out_ref):
    scores = mm(query_ref[...], table_ref[...], NT)
    index = index_ref[...]
    place = jnp.bitwise_and(index, LANES - 1)
    low = jnp.take_along_axis(scores[:, :LANES], place, axis=1)
    high = jnp.take_along_axis(scores[:, LANES:], place, axis=1)
    out_ref[...] = jnp.transpose(jnp.where(index < LANES, low, high))[:KPICK]


def pick_scores(query, table, index):
    rows = query.shape[0]
    block = 256
    return pl.pallas_call(
        pick_kernel,
        grid=(rows // block,),
        in_specs=[
            pl.BlockSpec((block, QHALF), lambda i: (i, 0)),
            pl.BlockSpec((NSUB, QHALF), lambda i: (0, 0)),
            pl.BlockSpec((block, LANES), lambda i: (i, 0)),
        ],
        out_specs=pl.BlockSpec((KPICK, block), lambda i: (0, i)),
        out_shape=jax.ShapeDtypeStruct((KPICK, rows), f32),
        compiler_params=params(16),
        cost_estimate=lasting(rows / 600),
        name="pick_scores",
    )(query, table, index)


def unpick_kernel(grad_ref, index_ref, table_ref, sub_ref, query_ref):
    count = grad_ref.shape[1]
    place = lax.broadcasted_iota(jnp.int32, (NSUB, count), 0)
    total = jnp.zeros((NSUB, count), f32)
    for pick in range(KPICK):
        hit = place == index_ref[pick : pick + 1, :]
        total = total + jnp.where(hit, grad_ref[pick : pick + 1, :], 0.0)
    low = total.astype(bf16)
    sub_ref[...] = low
    query_ref[...] = mm(low, table_ref[...], TN).astype(bf16)


def unpick_scores(grads, index, table):
    rows = grads.shape[1]
    block = 256
    return pl.pallas_call(
        unpick_kernel,
        grid=(rows // block,),
        in_specs=[
            pl.BlockSpec((KPICK, block), lambda i: (0, i)),
            pl.BlockSpec((KPICK, block), lambda i: (0, i)),
            pl.BlockSpec((NSUB, QHALF), lambda i: (0, 0)),
        ],
        out_specs=[
            pl.BlockSpec((NSUB, block), lambda i: (0, i)),
            pl.BlockSpec((block, QHALF), lambda i: (i, 0)),
        ],
        out_shape=[
            jax.ShapeDtypeStruct((NSUB, rows), bf16),
            jax.ShapeDtypeStruct((rows, QHALF), bf16),
        ],
        compiler_params=params(16),
        cost_estimate=lasting(rows / 180),
        name="unpick_scores",
    )(grads, index, table)


def products_kernel(dims, rows, *refs):
    left_ref, right_ref, keep_ref, send_ref = refs[-4:]
    if len(refs) > 4:
        place = lax.broadcasted_iota(jnp.int32, (2 * rows, refs[0].shape[1]), 0)
        home = place + pl.program_id(0) * 2 * rows == refs[0][...]
        left = mm(jnp.where(home, 1.0, 0.0).astype(bf16), left_ref[...]).astype(bf16)
    else:
        left = left_ref[...]
    product = mm(left, right_ref[...], dims).astype(bf16)
    keep_ref[0] = product[:rows]
    send_ref[0] = product[rows:]


def two_products(left, right, dims, rows, dealt_from=None):
    width = right.shape[1] if dims == NN else right.shape[0]
    operands = [left, right]
    in_specs = [
        pl.BlockSpec((2 * rows, left.shape[1]), lambda i: (i, 0)),
        pl.BlockSpec(right.shape, lambda i: (0, 0)),
    ]
    if dealt_from is not None:
        in_specs[0] = pl.BlockSpec(left.shape, lambda i: (0, 0))
        operands.insert(0, dealt_from[None, :])
        in_specs.insert(0, pl.BlockSpec((1, dealt_from.shape[0]), lambda i: (0, 0)))
    return pl.pallas_call(
        lambda *refs: products_kernel(dims, rows, *refs),
        grid=(TP // 2,),
        in_specs=in_specs,
        out_specs=[pl.BlockSpec((1, rows, width), lambda i: (i, 0, 0))] * 2,
        out_shape=[jax.ShapeDtypeStruct((TP // 2, rows, width), bf16)] * 2,
        compiler_params=params(16),
        cost_estimate=lasting(4),
        name="two_products",
    )(*operands)


def shards_kernel(splits, sums_ref, gain_ref, weight_refs, out_refs, gain_grad_ref):
    sources = sums_ref.shape[0]
    turned = jnp.zeros(gain_grad_ref.shape, f32)
    for part in range(TP):
        total = sums_ref[part].astype(f32)
        for more in range(part + TP, sources, TP):
            total = total + sums_ref[more].astype(f32)
        start = 0
        for (width, stride, offset), weight_ref, out_ref in zip(splits, weight_refs, out_refs):
            here = slice(offset + part * stride, offset + part * stride + width)
            piece = total[:, start : start + width]
            product = piece * weight_ref[:, here].astype(f32)
            turned = turned + jnp.sum(product, axis=1, keepdims=True)
            out_ref[:, here] = piece * gain_ref[...]
            start = start + width
    gain_grad_ref[...] = turned


def shard_grads(sums, gain, splits, *weights):
    rows = gain.shape[0]
    count = len(weights)
    owners = [min(at, count - 1) for at in range(len(splits))]

    def kernel(sums_ref, gain_ref, *refs):
        weight_refs = [refs[at] for at in owners]
        out_refs = [refs[count + at] for at in owners]
        shards_kernel(splits, sums_ref, gain_ref, weight_refs, out_refs, refs[-1])

    return pl.pallas_call(
        kernel,
        out_shape=[jax.ShapeDtypeStruct(weight.shape, f32) for weight in weights]
        + [jax.ShapeDtypeStruct((rows, 1), f32)],
        compiler_params=params(16),
        cost_estimate=lasting(3),
        name="shard_grads",
    )(sums, gain, *weights)


def swap(array, axes):
    return lax.all_to_all(array, axes, split_axis=0, concat_axis=0, tiled=True)


def gather(array, axes):
    return lax.all_gather(array, axes, axis=0, tiled=True)


def across(array, distance):
    return lax.ppermute(array, "tp", [(at, at ^ distance) for at in range(TP)])


def onward(array, count, step):
    pairs = [(at, at + step) for at in range(count) if 0 <= at + step < count]
    return lax.ppermute(array, GROUP, pairs)


def gather_hop(own):
    far = across(own, 6)
    return across(own, 2), across(own, 4), far


def gather_cores(own, near):
    quad = jnp.stack([own, *near])
    both = jnp.stack([quad, across(quad, 1)], axis=1)
    return both.reshape((TP * own.shape[0],) + own.shape[1:])


def gather_tp(own):
    return gather_cores(own, gather_hop(own))


def chip_send(sums):
    return sums[0], [across(sums[turn].astype(bf16), 2 * turn) for turn in (3, 1, 2)]


def chip_hop(keep, met):
    return chip_send(keep.astype(f32) + met.astype(f32))


def last_hop(own, got):
    return own + sum(part.astype(f32) for part in got)


def sum_back(left, right, dims, rows):
    keep, send = two_products(left, right, dims, rows)
    return last_hop(*chip_hop(keep, across(send, 1)))


def chip_sums(keep_ref, met_ref, chip, half):
    size = keep_ref.shape[2] // 2
    rows = slice(half * size, (half + 1) * size)
    return keep_ref[chip, 0, rows].astype(f32) + met_ref[chip, 0, rows].astype(f32)


def leave_kernel(keep_ref, met_ref, along_ref, aside_ref):
    for turn in range(2):
        along_ref[turn, 0] = chip_sums(keep_ref, met_ref, 2 * turn + 1, 0).astype(bf16)
        aside_ref[turn, 0] = chip_sums(keep_ref, met_ref, 2 + turn, 1).astype(bf16)


def pass_kernel(keep_ref, met_ref, along_ref, aside_ref, out_along_ref, out_aside_ref):
    along = chip_sums(keep_ref, met_ref, 2, 0) + along_ref[1, 0].astype(f32)
    aside = chip_sums(keep_ref, met_ref, 1, 1) + aside_ref[1, 0].astype(f32)
    out_along_ref[0] = along.astype(bf16)
    out_aside_ref[0] = aside.astype(bf16)


def total_kernel(keep_ref, met_ref, along_ref, aside_ref, far_ref, side_ref, out_ref):
    size = keep_ref.shape[2] // 2
    along = chip_sums(keep_ref, met_ref, 0, 0) + along_ref[0, 0].astype(f32)
    aside = chip_sums(keep_ref, met_ref, 0, 1) + aside_ref[0, 0].astype(f32)
    out_ref[0, :size] = (along + far_ref[0].astype(f32)).astype(bf16)
    out_ref[0, size:] = (aside + side_ref[0].astype(f32)).astype(bf16)


def hop_call(kernel, name, keep, outs, *operands):
    groups, rows = keep.shape[1:3]
    four = pl.BlockSpec((4, 1, rows, LANES), lambda i: (0, i, 0, 0))
    two = pl.BlockSpec((2, 1, rows // 2, LANES), lambda i: (0, i, 0, 0))
    one = pl.BlockSpec((1, rows // 2, LANES), lambda i: (i, 0, 0))
    whole = pl.BlockSpec((1, rows, LANES), lambda i: (i, 0, 0))
    specs = {"two": two, "one": one, "whole": whole}
    shapes = {
        "two": (2, groups, rows // 2, LANES),
        "one": (groups, rows // 2, LANES),
        "whole": (groups, rows, LANES),
    }
    return pl.pallas_call(
        kernel,
        grid=(groups,),
        in_specs=[four, four, two, two, one, one][: len(operands) + 1],
        out_specs=[specs[out] for out in outs],
        out_shape=[jax.ShapeDtypeStruct(shapes[out], bf16) for out in outs],
        compiler_params=params(16),
        cost_estimate=lasting(keep.size / 5e5),
        name=name,
    )(keep, *operands)


def sum_groups_start(total, groups, group_index):
    parts = [lax.dynamic_index_in_dim(total, group_index, 0, keepdims=False)]
    low = total.astype(bf16)
    for away in range(1, groups):
        piece = lax.dynamic_index_in_dim(
            low, lax.rem(group_index + away, groups), 0, keepdims=False
        )
        pairs = [(at, (at + away) % groups) for at in range(groups)]
        parts.append(lax.ppermute(piece, GROUP, pairs))
    return parts


def sum_groups(total, groups, group_index):
    return sum(part.astype(f32) for part in sum_groups_start(total, groups, group_index))


def shift(own, groups, away):
    return lax.ppermute(own, GROUP, [(at, (at + away) % groups) for at in range(groups)])


def by_group(own, shifts, groups, group_index):
    result = jnp.zeros((groups,) + own.shape, own.dtype)
    result = lax.dynamic_update_index_in_dim(result, own, group_index, 0)
    for away, piece in shifts.items():
        source = lax.rem(group_index + groups - away, groups)
        result = lax.dynamic_update_index_in_dim(result, piece, source, 0)
    return result


def tie(*arrays):
    return lax.optimization_barrier(arrays)


def norm_scale(hidden):
    return lax.rsqrt(jnp.mean(hidden * hidden, axis=-1, keepdims=True) + epsilon)


def norm_back(hidden, scale, weighted):
    coupled = jnp.mean(hidden * weighted, axis=-1, keepdims=True)
    return scale * weighted - hidden * (scale * scale * scale) * coupled


def body(
    inputs,
    attn_gain,
    attn_qkv,
    attn_out,
    memory_gain,
    memory_query,
    sub_keys,
    memory_gate,
    memory_out,
    memory_values,
    doc_lengths,
    token_order,
    memory_picks,
    cotangent,
):
    rows, width = inputs.shape
    outer = lax.axis_size("outer")
    heads = lax.axis_size("head")
    groups = heads * outer
    blocks = outer * TP
    devices = groups * TP
    share = rows // blocks
    fold = TP * share
    span = TP * rows
    tokens = token_order.shape[0]
    head_index = lax.axis_index("head")
    outer_index = lax.axis_index("outer")
    here = lax.axis_index("tp")
    here_word = here.astype(jnp.int32)[None]
    group_index = head_index * outer + outer_index
    rows_w = attn_qkv.shape[0]
    subs = memory_values.shape[0] // NSUB
    picks = MH * KPICK
    capacity = 2 * rows * picks // devices
    back = min(groups - 1, -(-(tokens // 2 - 1) // span))
    base = back * span

    near = gather_hop(inputs)
    row_cut = jnp.stack([attn_out, memory_out, sub_keys.reshape(rows_w, width)])
    own_cot, row_cut, *near = tie(cotangent, row_cut, *near)
    near_cot = gather_hop(own_cot)
    to_turned = [
        (groups * part + group, group * TP + part) for group in range(groups) for part in range(TP)
    ]
    from_turned = [(there, at) for at, there in to_turned]
    row_cut = lax.ppermute(row_cut, ALL, to_turned)
    group_inputs = gather_cores(inputs, near)
    gain_one = attn_gain.astype(f32)[:, None]
    gain_two = memory_gain.astype(f32)[:, None]
    scaled_qkv = (attn_qkv.astype(f32) * gain_one).astype(bf16)
    scaled_query = (memory_query.astype(f32) * gain_two).astype(bf16)
    scaled_gate = (memory_gate.astype(f32) * gain_two).astype(bf16)
    qkv_cut = jnp.transpose(scaled_qkv.reshape(rows_w, 3, TP, LANES), (2, 0, 1, 3))
    qkv_cut = jnp.broadcast_to(
        qkv_cut.reshape(1, TP, rows_w, 3 * LANES), (groups, TP, rows_w, 3 * LANES)
    ).reshape(devices, rows_w, 3 * LANES)
    weight_qkv = swap(qkv_cut, ALL).reshape(width, 3 * LANES)

    def columns(piece):
        return jnp.moveaxis(piece.reshape(rows_w, TP, -1), 1, 0)

    by_half = jnp.transpose(memory_picks.reshape(outer, fold, MH, KPICK, 2), (0, 2, 4, 3, 1))
    by_half = by_half.reshape(blocks, KPICK, fold).astype(bf16)
    rest_cut = jnp.concatenate([columns(scaled_query), columns(scaled_gate)], axis=2)
    rest_width = rest_cut.shape[2]

    laid = token_order.reshape(heads, blocks, outer, fold)
    mine = lax.dynamic_index_in_dim(laid, head_index, 0, keepdims=False)
    mine = lax.dynamic_index_in_dim(mine, outer_index, 1, keepdims=False)
    local = jnp.bitwise_xor(mine.reshape(span) - group_index * span, here * rows)
    span_range = jnp.arange(span, dtype=jnp.int32)
    deal = (local[:, None] == span_range[None, :]).astype(bf16)

    group_wide = group_inputs.astype(f32)
    normed_one = (group_wide * norm_scale(group_wide)).astype(bf16)
    projected = mm(normed_one, weight_qkv).astype(bf16)
    queries = projected[:, :LANES] * jnp.asarray(1.0 / math.sqrt(HD), bf16)
    kv_pieces = [projected[:, LANES:]]
    own_picks, rest_cut, by_half, kv_pieces[0] = tie(
        memory_picks, rest_cut, by_half, kv_pieces[0]
    )
    if back > 0:
        kv_pieces.insert(0, onward(kv_pieces[0], groups, 1))
    if by_half.shape[:2] == rest_cut.shape[:2]:
        both = swap(jnp.concatenate([rest_cut, by_half], axis=2), "tp")
        rest_rows, by_half = both[:, :, :rest_width], both[:, :, rest_width:]
    else:
        rest_rows, by_half = swap(rest_cut, "tp"), swap(by_half, BLK)
    rest_rows = rest_rows.reshape(TP * rows_w, rest_width)
    kv_pieces[0], row_cut, *near_cot = tie(kv_pieces[0], row_cut, *near_cot)
    for away in range(1, back):
        kv_pieces.insert(0, onward(kv_pieces[0], groups, 1))
    group_cot = gather_cores(own_cot, near_cot)

    first_pick = own_picks[:, :, :, 0].reshape(rows, picks)
    second_pick = own_picks[:, :, :, 1].reshape(rows, picks)
    owner = first_pick // subs
    device_range = jnp.arange(devices, dtype=jnp.int32)
    owned = (owner[None] == device_range[:, None, None]).astype(bf16)
    before = (
        jnp.arange(picks, dtype=jnp.int32)[:, None] < jnp.arange(picks, dtype=jnp.int32)[None, :]
    ).astype(bf16)
    before_rows = (
        jnp.arange(rows, dtype=jnp.int32)[:, None] < jnp.arange(rows, dtype=jnp.int32)[None, :]
    ).astype(bf16)
    in_row = jnp.einsum("dtk,kj->dtj", owned, before, preferred_element_type=f32)
    row_counts = jnp.sum(owned.astype(f32), axis=2)
    of_rows = jnp.dot(row_counts.astype(bf16), before_rows, preferred_element_type=f32)
    rank = jnp.sum(owned.astype(f32) * (in_row + of_rows[:, :, None]), axis=0).astype(jnp.int32)
    target = owner * capacity + rank
    target_high = target // LANES
    target_low = target % LANES
    places = devices * capacity
    entries = make_entries(target_high, target_low, first_pick % subs, second_pick, places)

    turned_one, unused = tie(jnp.transpose(normed_one), kv_pieces[0])
    keys_values, rest_rows, by_half, entries, turned_one, row_cut = tie(
        jnp.concatenate(kv_pieces, axis=0),
        rest_rows,
        by_half,
        entries,
        turned_one,
        row_cut,
    )
    half_index = jnp.moveaxis(by_half, 1, 0).reshape(KPICK, span).astype(jnp.int32)
    wide_index = jnp.pad(jnp.transpose(half_index), ((0, 0), (0, LANES - KPICK)))
    rest_shifts = {away: shift(rest_rows, groups, away) for away in range(1, groups, 2)}
    doc_ends = jnp.cumsum(doc_lengths)

    def lowest(inside):
        positions = group_index * span + inside
        starts = jnp.where(positions[:, None] >= doc_ends[None, :], doc_ends[None, :], 0)
        return jnp.max(starts, axis=1) - (group_index - back) * span

    low_first = lowest(span_range)
    low = lowest(jnp.bitwise_xor(span_range, here * rows))
    attended, lse, attended_low = attn_fwd(
        base, rows, low_first, here_word, low, queries, keys_values
    )
    attn_shifts = {away: shift(row_cut[0], groups, away) for away in range(1, groups)}
    attended_low, group_cot, rest_rows, *shifted = tie(
        attended_low, group_cot, rest_rows, *attn_shifts.values(), *rest_shifts.values()
    )
    attn_shifts = dict(zip(attn_shifts, shifted))
    rest_shifts = dict(zip(rest_shifts, shifted[len(attn_shifts) :]))
    weight_attn = by_group(row_cut[0], attn_shifts, groups, group_index).reshape(LANES, width)
    even_shifts = {away: shift(rest_rows, groups, away) for away in range(2, groups, 2)}
    inputs_wide = inputs.astype(f32)
    hidden_one = inputs_wide + sum_back(attended_low, weight_attn, NN, rows)
    hidden_one, row_cut, *shifted = tie(hidden_one, row_cut, *even_shifts.values())
    rest_shifts.update(zip(even_shifts, shifted))
    weight_rest = by_group(rest_rows, rest_shifts, groups, group_index).reshape(width, rest_width)
    row_shifts = {away: shift(row_cut[1:], groups, away) for away in range(1, groups)}
    row_all = by_group(row_cut[1:], row_shifts, groups, group_index)
    row_all = jnp.moveaxis(row_all, 0, 1).reshape(2, LANES, width)
    weight_mixed = row_all[0]
    key_table = row_all[1].reshape(NSUB, QHALF)
    scale_two = norm_scale(hidden_one)
    dealt_cot = mm(deal, group_cot).astype(bf16)
    grad_mixed = mm(dealt_cot, weight_mixed, NT)
    normed_two = mm(deal, gather_tp((hidden_one * scale_two).astype(bf16))).astype(bf16)

    pre = mm(normed_two, weight_rest)
    query_mem = pre[:, :QHALF].astype(bf16)
    gate_pre = pre[:, QHALF:]
    gate_sig = jax.nn.sigmoid(gate_pre)
    grad_memory = (grad_mixed * gate_pre * gate_sig).astype(bf16)
    query_mem, grad_memory = tie(query_mem, grad_memory)
    every_grad = gather(grad_memory, ALL).reshape(heads, outer, TP, blocks, fold, LANES)
    picked_half = pick_scores(query_mem, key_table, wide_index).reshape(KPICK, blocks, fold)
    picked = swap(jnp.moveaxis(picked_half, 1, 0), BLK)
    turned_two, unused = tie(jnp.transpose(normed_two), picked_half)
    picked, turned_two = tie(picked, turned_two)
    picked = jnp.moveaxis(picked.reshape(outer, TP, KPICK, fold), 0, 2).reshape(TP, KPICK, rows)
    pick_weights, sent_weights = make_weights(picked, target_high, target_low, places)
    sent = jnp.concatenate([entries, sent_weights], axis=1)
    sent = jnp.moveaxis(sent.reshape(devices, capacity // LANES, 4, LANES), 2, 1)
    entries = swap(sent.reshape(devices, 4, capacity), ALL).astype(f32)
    entries = entries.reshape(heads, blocks, 4, 1, capacity)
    entry_token = entries[:, :, 0].astype(jnp.int32)
    entry_first = entries[:, :, 1].astype(jnp.int32)
    entry_second = entries[:, :, 2].astype(jnp.int32)
    entry_weight = entries[:, :, 3]

    turns = 2
    table = None
    leaving = []
    flat = (TP // 2, groups, span // turns, LANES)
    for turn in range(turns):
        table, keep, send = spread_weights(
            rows,
            subs,
            heads,
            outer,
            turn,
            turns,
            here_word,
            entry_token,
            entry_first,
            entry_second,
            entry_weight,
            memory_values,
            table,
        )
        leaving.append((keep.reshape(flat), across(send.reshape(flat), 1)))
    dots = []
    dense = None

    def more_dots(dense, *moved):
        if len(dots) == heads:
            return dense, moved
        part, dense = row_dots(
            rows,
            subs,
            len(dots),
            heads,
            outer,
            entry_token,
            entry_first,
            entry_second,
            every_grad,
            memory_values,
            dense,
        )
        part, dense, *moved = tie(part, dense, *moved)
        dots.append(part)
        return dense, moved

    def sums_call(kernel, name, outs, half, *operands):
        keep, met = leaving[half]
        return hop_call(kernel, name, keep, outs, met, *operands)

    leaves = sums_call(leave_kernel, "sums_first", ("two", "two"), 0)
    every_grad, *leaves = tie(every_grad, *leaves)
    first = [[across(leaves[0], 2), across(leaves[1], 4)]]
    dense, leaving[1] = more_dots(dense, *leaving[1])
    leaves = sums_call(leave_kernel, "sums_first", ("two", "two"), 1)
    dense, *leaves = tie(dense, *leaves)
    first.append([across(leaves[0], 2), across(leaves[1], 4)])
    dense, first[0] = more_dots(dense, *first[0])
    leaves = sums_call(pass_kernel, "sums_second", ("one", "one"), 0, *first[0])
    dense, *leaves = tie(dense, *leaves)
    second = [[across(leaves[0], 4), across(leaves[1], 2)]]
    dense, moved = more_dots(dense, *first[1], *second[0])
    first[1], second[0] = moved[:2], moved[2:]
    leaves = sums_call(pass_kernel, "sums_second", ("one", "one"), 1, *first[1])
    total = sums_call(total_kernel, "sums_last", ("whole",), 0, *first[0], *second[0])
    dense, *leaves = tie(dense, *leaves)
    second.append([across(leaves[0], 4), across(leaves[1], 2)])
    dense, second[1] = more_dots(dense, *second[1])
    while len(dots) < heads:
        dense, unused = more_dots(dense)
    total += sums_call(total_kernel, "sums_last", ("whole",), 1, *first[1], *second[1])
    total = jnp.concatenate(total, axis=1)
    memory = sum_groups(total, groups, group_index)

    entry_dots = jnp.concatenate(dots, axis=0).reshape(devices, capacity)
    returned = swap(entry_dots, ALL).reshape(places // LANES, LANES)
    table = table.reshape(tokens, subs * NSUB)
    dense = dense.reshape(tokens, width)
    grad_values = value_grads(0, turns, table, dense, None)
    returned, grad_values = tie(returned, grad_values)
    grad_picked = pick_grads(target_high, target_low, pick_weights, returned)
    to_half = jnp.moveaxis(grad_picked.reshape(MH, KPICK, outer, fold), 2, 0)
    to_half = jnp.broadcast_to(to_half[:, :, None], (outer, MH, 2, KPICK, fold))
    grad_half = swap(to_half.reshape(blocks, KPICK, fold), BLK)
    grad_half = jnp.moveaxis(grad_half, 1, 0).reshape(KPICK, span)
    grad_sub, grad_query = unpick_scores(grad_half, half_index, key_table)

    mixed_low = (memory * gate_pre * gate_sig).astype(bf16)
    grad_gate = (grad_mixed * memory * gate_sig * (1.0 + gate_pre * (1.0 - gate_sig))).astype(bf16)
    grad_pre = jnp.concatenate([grad_query, grad_gate], axis=1)
    keep, send = two_products(grad_pre, weight_rest, NT, rows, local)
    met = across(send, 1)

    met, grad_pre, mixed_low, grad_sub = tie(met, grad_pre, mixed_low, grad_sub)
    own, got = chip_hop(keep, met)
    rest_grads = mm(turned_two, grad_pre).astype(bf16)
    row_grads = [mm(mixed_low, dealt_cot, TN), mm(grad_sub, query_mem).reshape(LANES, width)]
    row_grads = jnp.stack(row_grads).astype(bf16).reshape(2, groups, rows_w, width)
    row_grads = jnp.moveaxis(row_grads, 0, 1).reshape(groups * TP * rows_w, -1)
    memory_grads = jnp.concatenate([rest_grads, row_grads], axis=1)
    memory_grads, mixed_low, *got = tie(memory_grads, mixed_low, *got)
    memory_grads = lax.psum_scatter(memory_grads, GROUP, scatter_dimension=0, tiled=True)
    weighted_two = last_hop(own, got)
    grad_hidden = cotangent.astype(f32) + norm_back(hidden_one, scale_two, weighted_two)

    output_keep, output_met = two_products(mixed_low, weight_mixed, NN, rows, local)
    own_branch = grad_hidden.astype(bf16)
    near_branch = gather_hop(own_branch)
    output_keep, output_met, *near_branch = tie(output_keep, output_met, *near_branch)
    output_met = across(output_met, 1)
    grad_branch = gather_cores(own_branch, near_branch)
    grad_attended = mm(grad_branch, weight_attn, NT).astype(bf16)
    grad_q, *grad_kv = attn_bwd(
        base, rows, low_first, here_word, low, queries, keys_values, lse, attended, grad_attended
    )
    output_keep, output_met, table, memory_grads, *grad_kv = tie(
        output_keep, output_met, table, memory_grads, *grad_kv
    )

    rest_home = swap(memory_grads[:, :rest_width].reshape(TP, rows_w, -1), "tp")
    attended_low, unused = tie(attended_low, grad_kv[0])
    attn_rows = mm(attended_low, grad_branch, TN).astype(bf16).reshape(groups, rows_w, width)
    attn_rows = sum_groups_start(attn_rows, groups, group_index)
    output_got = None
    carry = grad_kv[0]
    for away in range(back):
        met = onward(carry, groups, -1)
        if away == back - 1:
            output_own, output_got = chip_hop(output_keep, output_met)
            grad_values = value_grads(1, turns, table, dense, grad_values)
            met, grad_values, *output_got = tie(met, grad_values, *output_got)
        if away == 0:
            met, rest_home, output_keep, output_met, table = tie(
                met, rest_home, output_keep, output_met, table
            )
        carry = (grad_kv[away + 1].astype(f32) + met.astype(f32)).astype(bf16)
    if back == 0:
        output_own, output_got = chip_hop(output_keep, output_met)
        grad_values = value_grads(1, turns, table, dense, grad_values)
    grad_projected = jnp.concatenate([grad_q, carry], axis=1)

    late_grads = mm(turned_one, grad_projected).astype(bf16)
    grad_projected, late_grads = tie(grad_projected, late_grads)
    qkv_home = swap(late_grads.reshape(devices, rows_w, 3 * LANES), ALL)
    keep, send = two_products(grad_projected, weight_qkv, NT, rows)
    sums = keep.astype(f32) + across(send, 1).astype(f32)
    sums, rest_home, memory_grads, *attn_rows = tie(sums, rest_home, memory_grads, *attn_rows)
    own, got = chip_send(sums)
    attn_rows = sum(part.astype(f32) for part in attn_rows).astype(bf16)
    row_sums = memory_grads[:, rest_width:].reshape(2, rows_w, width)
    row_home = jnp.concatenate([attn_rows[None], row_sums])
    row_home = lax.ppermute(row_home, ALL, from_turned)
    weighted_one = last_hop(own, got)
    grad_inputs = grad_hidden + norm_back(inputs_wide, norm_scale(inputs_wide), weighted_one)
    output = (hidden_one + last_hop(output_own, output_got)).astype(bf16)
    row_home = row_home.astype(f32)
    splits = ((QHALF, QHALF, 0), (LANES, LANES, 0))
    grad_query_home, grad_gate_home, grad_memory_gain = shard_grads(
        rest_home, gain_two, splits, memory_query, memory_gate
    )
    splits = tuple((LANES, LANES, part * width) for part in range(3))
    grad_qkv_home, grad_attn_gain = shard_grads(qkv_home, gain_one, splits, attn_qkv)
    return (
        output,
        grad_inputs,
        grad_attn_gain.reshape(-1),
        grad_qkv_home,
        row_home[0],
        grad_memory_gain.reshape(-1),
        grad_query_home,
        row_home[2].reshape(sub_keys.shape),
        grad_gate_home,
        row_home[1],
        grad_values,
    )


def solution(mesh):
    heads, blocks = mesh.devices.shape
    cut_mesh = Mesh(mesh.devices.reshape(heads, blocks // TP, TP), ALL)
    matrix = P(ALL, None)
    in_specs = (
        matrix,
        P(ALL),
        matrix,
        matrix,
        P(ALL),
        matrix,
        matrix,
        matrix,
        matrix,
        matrix,
        P(),
        P(),
        P(ALL, None, None, None),
        matrix,
    )
    out_specs = (
        matrix,
        matrix,
        P(ALL),
        matrix,
        matrix,
        P(ALL),
        matrix,
        matrix,
        matrix,
        matrix,
        matrix,
    )
    return jax.shard_map(
        body, mesh=cut_mesh, in_specs=in_specs, out_specs=out_specs, check_vma=False
    )
```

```python
import math

import jax
import jax.numpy as jnp
from jax import lax
from jax.experimental import pallas as pl
from jax.experimental.pallas import tpu as pltpu
from jax.sharding import Mesh
from jax.sharding import PartitionSpec as P

NH = 16
HD = 64
MH = 4
QHALF = 512
NSUB = 256
KPICK = 32
TP = 2 * MH

GROUP = ("head", "outer")
BLK = ("outer", "tp")
ALL = ("head", "outer", "tp")

epsilon = 1e-06
neg_big = -1e30
LANES = 128
bf16 = jnp.bfloat16
f32 = jnp.float32
NN = (((1,), (0,)), ((), ()))
NT = (((1,), (1,)), ((), ()))
TN = (((0,), (0,)), ((), ()))


def mm(left, right, dims=NN):
    return lax.dot_general(left, right, dims, preferred_element_type=f32)


def params(mib):
    return pltpu.CompilerParams(vmem_limit_bytes=mib * 1024 * 1024)


def lasting(microseconds):
    return pl.CostEstimate(
        flops=0, bytes_accessed=int(microseconds * 3.5e6), transcendentals=0
    )


def head_rows(pair):
    lane = lax.broadcasted_iota(jnp.int32, pair.shape, 1)
    zero = jnp.zeros_like(pair)
    return (jnp.where(lane < HD, pair, zero), jnp.where(lane < HD, zero, pair))


def turned_block(step, here, block, rows):
    return jnp.bitwise_xor(step, here * rows // block)


def turned_iota(shape, axis, here, rows):
    place = lax.broadcasted_iota(jnp.int32, shape, axis)
    return jnp.bitwise_xor(place, lax.rem(here * rows, shape[axis]))


def key_blocks(step, base, span, bounds, block_q, block_k, low_first_ref):
    first = jnp.maximum(low_first_ref[step], bounds[0] * span) // block_k
    stop = (base + (step + 1) * block_q - 1) // block_k + 1
    return first, jnp.minimum(stop, bounds[1] * span // block_k)


def key_start(turn, span, here, block_k, rows, skipped):
    per_group = span // block_k
    group = turn // per_group - skipped
    within = turned_block(lax.rem(turn, per_group), here, block_k, rows)
    return pl.multiple_of(group * span + within * block_k, block_k)


def attn_fwd_kernel(
    base, span, rows, block_k, bounds, low_first_ref, here_ref, q_ref, kv_ref, low_ref, *refs
):
    att_ref, lse_ref, out_ref = refs[-3:]
    block_q = q_ref.shape[0]
    step = pl.program_id(0)
    here = here_ref[0]
    first, stop = key_blocks(step, base, span, bounds, block_q, block_k, low_first_ref)
    queries = head_rows(q_ref[...])
    low = low_ref[...]
    high = base + step * block_q + turned_iota((1, block_q), 1, here, rows)
    inner = turned_iota((block_k, block_q), 0, here, rows)

    def visit(turn, carried):
        start = key_start(turn, span, here, block_k, rows, bounds[0])
        keys = kv_ref[pl.ds(start, block_k), :LANES]
        values = kv_ref[pl.ds(start, block_k), LANES:]
        place = turn * block_k + inner
        allowed = (place >= low) & (place <= high)
        out = []
        for head in range(2):
            run_max, run_sum, run_acc = carried[head]
            scores = jnp.where(allowed, mm(keys, queries[head], NT), neg_big)
            new_max = jnp.maximum(run_max, jnp.max(scores, axis=0, keepdims=True))
            powers = jnp.exp(scores - new_max)
            rescale = jnp.exp(run_max - new_max)
            run_sum = run_sum * rescale + jnp.sum(powers, axis=0, keepdims=True)
            run_acc = run_acc * rescale + mm(values, powers.astype(bf16), TN)
            out.append((new_max, run_sum, run_acc))
        return tuple(out)

    if len(refs) > 3:
        near_att = refs[0][...]
        fresh = tuple(
            (refs[1][head : head + 1, :], jnp.ones((1, block_q), f32), near_att)
            for head in range(2)
        )
    else:
        fresh = (
            jnp.full((1, block_q), neg_big, f32),
            jnp.zeros((1, block_q), f32),
            jnp.zeros((LANES, block_q), f32),
        )
        fresh = (fresh, fresh)
    done = lax.fori_loop(first, stop, visit, fresh)
    att_ref[:HD, :] = done[0][2][:HD] / done[0][1]
    att_ref[HD:, :] = done[1][2][HD:] / done[1][1]
    out_ref[...] = jnp.transpose(att_ref[...]).astype(bf16)
    lse_ref[0:1, :] = done[0][0] + jnp.log(done[0][1])
    lse_ref[1:2, :] = done[1][0] + jnp.log(done[1][1])


def attn_specs(block_q, rows, span):
    def turn(i, here):
        return turned_block(i, here[0], block_q, rows)

    return (
        pl.BlockSpec((block_q, LANES), lambda i, s, here: (turn(i, here), 0)),
        pl.BlockSpec((1, block_q), lambda i, s, here: (0, turn(i, here))),
        pl.BlockSpec((2, block_q), lambda i, s, here: (0, turn(i, here))),
        pl.BlockSpec((LANES, block_q), lambda i, s, here: (0, turn(i, here))),
    )


def attn_fwd(base, rows, bounds, low_first, here, low, queries, keys_values, near=()):
    span = queries.shape[0]
    block_q, block_k = 512, 512
    by_row, one_lane, two_lane, by_lane = attn_specs(block_q, rows, span)
    in_specs = [
        by_row,
        pl.BlockSpec(keys_values.shape, lambda i, s, here: (0, 0)),
        one_lane,
        by_lane,
        two_lane,
    ]
    return pl.pallas_call(
        lambda *refs: attn_fwd_kernel(base, span, rows, block_k, bounds, *refs),
        grid_spec=pltpu.PrefetchScalarGridSpec(
            num_scalar_prefetch=2,
            grid=(span // block_q,),
            in_specs=in_specs[: 3 + len(near)],
            out_specs=[by_lane, two_lane, by_row],
        ),
        out_shape=[
            jax.ShapeDtypeStruct((LANES, span), f32),
            jax.ShapeDtypeStruct((2, span), f32),
            jax.ShapeDtypeStruct((span, LANES), bf16),
        ],
        compiler_params=params(24),
        cost_estimate=lasting(keys_values.shape[0] / 250),
        name="attn_fwd",
    )(low_first[::block_q], here, queries, keys_values, low[None, :], *near)


def attn_bwd_kernel(
    base,
    span,
    rows,
    block_k,
    bounds,
    low_first_ref,
    here_ref,
    q_ref,
    kv_ref,
    low_ref,
    lse_ref,
    att_ref,
    grad_ref,
    *refs,
):
    dk_ref, dv_ref = refs[-2:]
    count = bounds[1] - bounds[0]
    out_refs = refs[-2 - count : -2]
    dq_ref = refs[-3 - count]
    block_q = q_ref.shape[0]
    step = pl.program_id(0)
    here = here_ref[0]
    first, stop = key_blocks(step, base, span, bounds, block_q, block_k, low_first_ref)

    @pl.when(step == 0)
    def clear():
        dk_ref[...] = jnp.zeros_like(dk_ref)
        dv_ref[...] = jnp.zeros_like(dv_ref)

    queries = head_rows(q_ref[...])
    grads = head_rows(grad_ref[...])
    grad_turned = jnp.transpose(grad_ref[...].astype(f32)) * att_ref[...]
    deltas = (
        jnp.sum(grad_turned[:HD], axis=0, keepdims=True),
        jnp.sum(grad_turned[HD:], axis=0, keepdims=True),
    )
    low = low_ref[...]
    high = base + step * block_q + turned_iota((1, block_q), 1, here, rows)
    inner = turned_iota((block_k, block_q), 0, here, rows)

    def visit(turn, carried):
        start = key_start(turn, span, here, block_k, rows, bounds[0])
        keys = kv_ref[pl.ds(start, block_k), :LANES]
        values = kv_ref[pl.ds(start, block_k), LANES:]
        place = turn * block_k + inner
        allowed = (place >= low) & (place <= high)
        out = []
        grad_key = dk_ref[pl.ds(start, block_k), :]
        grad_value = dv_ref[pl.ds(start, block_k), :]
        for head in range(2):
            scores = mm(keys, queries[head], NT)
            probs = jnp.where(allowed, jnp.exp(scores - lse_ref[head : head + 1, :]), 0.0)
            grad_probs = mm(values, grads[head], NT)
            grad_scores = (probs * (grad_probs - deltas[head])).astype(bf16)
            grad_key = grad_key + mm(grad_scores, queries[head])
            grad_value = grad_value + mm(probs.astype(bf16), grads[head])
            out.append(carried[head] + mm(keys, grad_scores, TN))
        dk_ref[pl.ds(start, block_k), :] = grad_key
        dv_ref[pl.ds(start, block_k), :] = grad_value
        return tuple(out)

    fresh = jnp.zeros((LANES, block_q), f32)
    done = lax.fori_loop(first, stop, visit, (fresh, fresh))
    turned = jnp.concatenate([done[0][:HD], done[1][HD:]], axis=0) * (1.0 / math.sqrt(HD))
    total = jnp.transpose(turned)
    if len(refs) > 3 + count:
        total = total + refs[0][...].astype(f32)
    dq_ref[...] = total.astype(bf16)

    @pl.when(step == span // block_q - 1)
    def leave():
        for turn, out_ref in enumerate(out_refs):
            out_ref[:, :LANES] = dk_ref[turn * span : (turn + 1) * span, :].astype(bf16)
            out_ref[:, LANES:] = dv_ref[turn * span : (turn + 1) * span, :].astype(bf16)


def attn_bwd(
    base, rows, bounds, low_first, here, low, queries, keys_values, lse, att, grads, far=()
):
    span = queries.shape[0]
    block_q, block_k = 512, 512
    reach = keys_values.shape[0]
    by_row, one_lane, two_lane, by_lane = attn_specs(block_q, rows, span)
    in_specs = [
        by_row,
        pl.BlockSpec(keys_values.shape, lambda i, s, here: (0, 0)),
        one_lane,
        two_lane,
        by_lane,
        by_row,
        by_row,
    ]
    return pl.pallas_call(
        lambda *refs: attn_bwd_kernel(base, span, rows, block_k, bounds, *refs),
        grid_spec=pltpu.PrefetchScalarGridSpec(
            num_scalar_prefetch=2,
            grid=(span // block_q,),
            in_specs=in_specs[: 6 + len(far)],
            out_specs=[by_row]
            + [pl.BlockSpec((span, 2 * LANES), lambda i, s, here: (0, 0))] * (reach // span),
            scratch_shapes=[pltpu.VMEM((reach, LANES), f32), pltpu.VMEM((reach, LANES), f32)],
        ),
        out_shape=[jax.ShapeDtypeStruct((span, LANES), bf16)]
        + [jax.ShapeDtypeStruct((span, 2 * LANES), bf16)] * (reach // span),
        compiler_params=params(32),
        cost_estimate=lasting(keys_values.shape[0] / 200),
        name="attn_bwd",
    )(low_first[::block_q], here, queries, keys_values, low[None, :], lse, att, grads, *far)


def hits(count, row):
    return lax.broadcasted_iota(jnp.int32, (count, row.shape[1]), 0) == row


def one_hot(count, row):
    return jnp.where(hits(count, row), 1.0, 0.0).astype(bf16)


def wide_hits(count, ref, top, rows):
    return [hits(count, ref[row : row + 1, :]) for row in range(top, top + rows)]


def bucket_rows(high_ref, low_ref, load_refs, places):
    batch = 8
    total = jnp.zeros((places, len(load_refs) * LANES), f32)
    for top in range(0, high_ref.shape[0], batch):
        high = [
            jnp.where(hit, 1.0, 0.0).astype(bf16) for hit in wide_hits(places, high_ref, top, batch)
        ]
        low = wide_hits(LANES, low_ref, top, batch)
        parts = [
            jnp.concatenate(
                [
                    jnp.where(low[row], load_ref[top + row : top + row + 1, :], 0.0).astype(bf16)
                    for row in range(batch)
                ],
                axis=1,
            )
            for load_ref in load_refs
        ]
        total = total + mm(jnp.concatenate(high, axis=1), jnp.concatenate(parts, axis=0), NT)
    return total


def entries_kernel(high_ref, low_ref, first_ref, second_ref, out_ref, token_ref):
    token_ref[...] = lax.broadcasted_iota(jnp.int32, token_ref.shape, 0).astype(f32)
    loads = (token_ref, first_ref, second_ref)
    out_ref[...] = bucket_rows(high_ref, low_ref, loads, out_ref.shape[0]).astype(bf16)


def make_entries(high, low, first, second, places):
    return pl.pallas_call(
        entries_kernel,
        out_shape=jax.ShapeDtypeStruct((places // LANES, 3 * LANES), bf16),
        scratch_shapes=[pltpu.VMEM(high.shape, f32)],
        compiler_params=params(16),
        cost_estimate=lasting(5),
        name="make_entries",
    )(high, low, first.astype(f32), second.astype(f32))


def weights_kernel(picked_ref, high_ref, low_ref, weight_ref, out_ref):
    parts = []
    for head in range(MH):
        picked = picked_ref[2 * head] + picked_ref[2 * head + 1]
        powers = jnp.exp(picked - jnp.max(picked, axis=0, keepdims=True))
        parts.append(powers / jnp.sum(powers, axis=0, keepdims=True))
    weight_ref[...] = jnp.transpose(jnp.concatenate(parts, axis=0))
    out_ref[...] = bucket_rows(high_ref, low_ref, (weight_ref,), out_ref.shape[0]).astype(bf16)


def make_weights(picked, high, low, places):
    return pl.pallas_call(
        weights_kernel,
        out_shape=[
            jax.ShapeDtypeStruct(high.shape, f32),
            jax.ShapeDtypeStruct((places // LANES, LANES), bf16),
        ],
        compiler_params=params(16),
        cost_estimate=lasting(3),
        name="make_weights",
    )(picked, high, low)


def grads_kernel(high_ref, low_ref, weight_ref, table_ref, out_ref, found_ref):
    turned = jnp.transpose(table_ref[...])
    main = turned.astype(bf16)
    rest = (turned - main.astype(f32)).astype(bf16)
    batch = 8
    for top in range(0, high_ref.shape[0], batch):
        high = jnp.concatenate(
            [
                jnp.where(hit, 1.0, 0.0).astype(bf16)
                for hit in wide_hits(table_ref.shape[0], high_ref, top, batch)
            ],
            axis=1,
        )
        found = mm(main, high) + mm(rest, high)
        low = jnp.concatenate(wide_hits(LANES, low_ref, top, batch), axis=1)
        line = jnp.sum(jnp.where(low, found, 0.0), axis=0, keepdims=True)
        for row in range(batch):
            found_ref[top + row : top + row + 1, :] = line[:, row * LANES : (row + 1) * LANES]
    grads = jnp.transpose(found_ref[...])
    weights = jnp.transpose(weight_ref[...])
    for head in range(MH):
        rows = slice(head * KPICK, (head + 1) * KPICK)
        coupled = jnp.sum(weights[rows] * grads[rows], axis=0, keepdims=True)
        out_ref[rows, :] = weights[rows] * (grads[rows] - coupled)


def pick_grads(high, low, weights, table):
    return pl.pallas_call(
        grads_kernel,
        out_shape=jax.ShapeDtypeStruct((high.shape[1], high.shape[0]), f32),
        scratch_shapes=[pltpu.VMEM(high.shape, f32)],
        compiler_params=params(16),
        cost_estimate=lasting(5),
        name="pick_grads",
    )(high, low, weights, table)


def place_rows(rows, subs, token_row, first_row):
    tokens = one_hot(rows, token_row)
    return jnp.concatenate(
        [tokens * jnp.where(first_row == first, 1.0, 0.0).astype(bf16) for first in range(subs)],
        axis=0,
    )


def spread_kernel(
    rows, subs, outer, here_ref, token_ref, first_ref, second_ref, weight_ref, value_ref, *refs
):
    table_ref, keep_ref, send_ref = refs[-3:]
    count = token_ref.shape[1]
    fold = rows // outer
    for block in range(count):
        left = place_rows(rows, subs, token_ref[0, block], first_ref[0, block])
        right = jnp.where(hits(NSUB, second_ref[0, block]), weight_ref[0, block], 0.0).astype(bf16)
        table = mm(left, right, NT).astype(bf16)
        for first in range(subs):
            table_ref[0, block * rows : (block + 1) * rows, first * NSUB : (first + 1) * NSUB] = (
                table[first * rows : (first + 1) * rows]
            )
    partial = mm(table_ref[0], value_ref[...]).astype(bf16)
    here = here_ref[0]
    chip = here // 2

    def store(core):
        for there in range(TP):
            target_ref = keep_ref if there % 2 == core else send_ref
            place = jnp.bitwise_xor(chip, there // 2)
            for block in range(count):
                for part in range(outer):
                    top = block * rows + part * fold
                    target_ref[place, 0, part, block] = partial[
                        top : top + fold, there * LANES : (there + 1) * LANES
                    ]

    pl.when(here % 2 == 0)(lambda: store(0))
    pl.when(here % 2 == 1)(lambda: store(1))


def spread_weights(
    rows, subs, heads, outer, turn, turns, here, token, first, second, weight, values, table
):
    blocks, capacity = token.shape[1], token.shape[3]
    width = values.shape[1]
    count = 2
    steps = blocks // turns // count
    fold = rows // outer
    row = pl.BlockSpec((1, count, 1, capacity), lambda h, i, s: (h, turn * steps + i, 0, 0))
    piece = pl.BlockSpec(
        (TP // 2, 1, outer, count, fold, LANES), lambda h, i, s: (0, h, 0, i, 0, 0)
    )
    piece_shape = jax.ShapeDtypeStruct(
        (TP // 2, heads, outer, blocks // turns, fold, LANES), bf16
    )
    operands = [here, token, first, second, weight, values]
    in_specs = [row, row, row, row, pl.BlockSpec(values.shape, lambda h, i, s: (0, 0))]
    aliases = {}
    if table is not None:
        operands.append(table)
        in_specs.append(pl.BlockSpec(memory_space=pl.ANY))
        aliases = {6: 0}
    return pl.pallas_call(
        lambda *refs: spread_kernel(rows, subs, outer, *refs),
        grid_spec=pltpu.PrefetchScalarGridSpec(
            num_scalar_prefetch=1,
            grid=(heads, steps),
            in_specs=in_specs,
            out_specs=[
                pl.BlockSpec(
                    (1, count * rows, subs * NSUB), lambda h, i, s: (h, turn * steps + i, 0)
                ),
                piece,
                piece,
            ],
        ),
        out_shape=[
            jax.ShapeDtypeStruct((heads, blocks * rows, subs * NSUB), bf16),
            piece_shape,
            piece_shape,
        ],
        input_output_aliases=aliases,
        compiler_params=params(36),
        cost_estimate=lasting(heads * blocks // turns * rows / 90),
        name="spread_weights",
    )(*operands)


def dots_kernel(
    rows, subs, outer, token_ref, first_ref, second_ref, grad_ref, value_ref, *refs
):
    out_ref, dense_ref = refs[-2:]
    count = token_ref.shape[1]
    fold = rows // outer
    for block in range(count):
        for part in range(outer):
            top = block * rows + part * fold
            for there in range(TP):
                dense_ref[0, top : top + fold, there * LANES : (there + 1) * LANES] = grad_ref[
                    0, part, there, block
                ]
    dense = dense_ref[0]
    found = [
        mm(value_ref[first * NSUB : (first + 1) * NSUB, :], dense, NT).astype(bf16)
        for first in range(subs)
    ]
    for block in range(count):
        left = place_rows(rows, subs, token_ref[0, block], first_ref[0, block])
        table = jnp.concatenate(
            [
                found[first][:, block * rows : (block + 1) * rows] for first in range(subs)
            ],
            axis=1,
        )
        spread = mm(table, left)
        out_ref[0, block] = jnp.sum(
            jnp.where(hits(NSUB, second_ref[0, block]), spread, 0.0), axis=0, keepdims=True
        )


def row_dots(rows, subs, part, parts, outer, token, first, second, grads, values, dense):
    heads, blocks, capacity = token.shape[0], token.shape[1], token.shape[3]
    width = values.shape[1]
    count = 2
    fold = rows // outer
    mine = heads // parts
    top = part * mine
    row = pl.BlockSpec((1, count, 1, capacity), lambda h, i: (top + h, i, 0, 0))
    operands = [token, first, second, grads, values]
    in_specs = [
        row,
        row,
        row,
        pl.BlockSpec((1, outer, TP, count, fold, LANES), lambda h, i: (top + h, 0, 0, i, 0, 0)),
        pl.BlockSpec(values.shape, lambda h, i: (0, 0)),
    ]
    aliases = {}
    if dense is not None:
        operands.append(dense)
        in_specs.append(pl.BlockSpec(memory_space=pl.ANY))
        aliases = {5: 1}
    return pl.pallas_call(
        lambda *refs: dots_kernel(rows, subs, outer, *refs),
        grid=(mine, blocks // count),
        in_specs=in_specs,
        out_specs=[
            pl.BlockSpec((1, count, 1, capacity), lambda h, i: (h, i, 0, 0)),
            pl.BlockSpec((1, count * rows, width), lambda h, i: (top + h, i, 0)),
        ],
        out_shape=[
            jax.ShapeDtypeStruct((mine, blocks, 1, capacity), f32),
            jax.ShapeDtypeStruct((heads, blocks * rows, width), bf16),
        ],
        input_output_aliases=aliases,
        compiler_params=params(36),
        cost_estimate=lasting(mine * blocks * rows / 90),
        name="row_dots",
    )(*operands)


def value_grads_kernel(table_ref, dense_ref, *refs):
    out_ref = refs[-1]
    out_ref[...] = mm(table_ref[...], dense_ref[...], TN)


def value_grads(turn, turns, table, dense, sums):
    tokens, own_rows = table.shape
    width = dense.shape[1]
    block = min(256, own_rows // turns)
    steps = own_rows // turns // block
    operands = [table, dense]
    in_specs = [
        pl.BlockSpec((tokens, block), lambda i: (0, turn * steps + i)),
        pl.BlockSpec(dense.shape, lambda i: (0, 0), pipeline_mode=pl.Buffered(1)),
    ]
    aliases = {}
    if sums is not None:
        operands.append(sums)
        in_specs.append(pl.BlockSpec(memory_space=pl.ANY))
        aliases = {2: 0}
    return pl.pallas_call(
        value_grads_kernel,
        grid=(steps,),
        in_specs=in_specs,
        out_specs=pl.BlockSpec((block, width), lambda i: (turn * steps + i, 0)),
        out_shape=jax.ShapeDtypeStruct((own_rows, width), f32),
        input_output_aliases=aliases,
        compiler_params=params(30 if dense.size <= 2**23 else 58),
        cost_estimate=lasting(15 * 2 / turns),
        name="value_grads",
    )(*operands)


def pick_kernel(query_ref, table_ref, index_ref, out_ref):
    scores = mm(query_ref[...], table_ref[...], NT)
    index = index_ref[...]
    place = jnp.bitwise_and(index, LANES - 1)
    low = jnp.take_along_axis(scores[:, :LANES], place, axis=1)
    high = jnp.take_along_axis(scores[:, LANES:], place, axis=1)
    out_ref[...] = jnp.transpose(jnp.where(index < LANES, low, high))[:KPICK]


def pick_scores(query, table, index):
    rows = query.shape[0]
    block = 256
    return pl.pallas_call(
        pick_kernel,
        grid=(rows // block,),
        in_specs=[
            pl.BlockSpec((block, QHALF), lambda i: (i, 0)),
            pl.BlockSpec((NSUB, QHALF), lambda i: (0, 0)),
            pl.BlockSpec((block, LANES), lambda i: (i, 0)),
        ],
        out_specs=pl.BlockSpec((KPICK, block), lambda i: (0, i)),
        out_shape=jax.ShapeDtypeStruct((KPICK, rows), f32),
        compiler_params=params(16),
        cost_estimate=lasting(rows / 600),
        name="pick_scores",
    )(query, table, index)


def unpick_kernel(grad_ref, index_ref, table_ref, sub_ref, query_ref):
    count = grad_ref.shape[1]
    place = lax.broadcasted_iota(jnp.int32, (NSUB, count), 0)
    total = jnp.zeros((NSUB, count), f32)
    for pick in range(KPICK):
        hit = place == index_ref[pick : pick + 1, :]
        total = total + jnp.where(hit, grad_ref[pick : pick + 1, :], 0.0)
    low = total.astype(bf16)
    sub_ref[...] = low
    query_ref[...] = mm(low, table_ref[...], TN).astype(bf16)


def unpick_scores(grads, index, table):
    rows = grads.shape[1]
    block = 256
    return pl.pallas_call(
        unpick_kernel,
        grid=(rows // block,),
        in_specs=[
            pl.BlockSpec((KPICK, block), lambda i: (0, i)),
            pl.BlockSpec((KPICK, block), lambda i: (0, i)),
            pl.BlockSpec((NSUB, QHALF), lambda i: (0, 0)),
        ],
        out_specs=[
            pl.BlockSpec((NSUB, block), lambda i: (0, i)),
            pl.BlockSpec((block, QHALF), lambda i: (i, 0)),
        ],
        out_shape=[
            jax.ShapeDtypeStruct((NSUB, rows), bf16),
            jax.ShapeDtypeStruct((rows, QHALF), bf16),
        ],
        compiler_params=params(16),
        cost_estimate=lasting(rows / 180),
        name="unpick_scores",
    )(grads, index, table)


def products_kernel(dims, rows, *refs):
    left_ref, right_ref, keep_ref, send_ref = refs[-4:]
    if len(refs) > 4:
        place = lax.broadcasted_iota(jnp.int32, (2 * rows, refs[0].shape[1]), 0)
        home = place + pl.program_id(0) * 2 * rows == refs[0][...]
        left = mm(jnp.where(home, 1.0, 0.0).astype(bf16), left_ref[...]).astype(bf16)
    else:
        left = left_ref[...]
    product = mm(left, right_ref[...], dims).astype(bf16)
    keep_ref[0] = product[:rows]
    send_ref[0] = product[rows:]


def two_products(left, right, dims, rows, dealt_from=None):
    width = right.shape[1] if dims == NN else right.shape[0]
    operands = [left, right]
    in_specs = [
        pl.BlockSpec((2 * rows, left.shape[1]), lambda i: (i, 0)),
        pl.BlockSpec(right.shape, lambda i: (0, 0)),
    ]
    if dealt_from is not None:
        in_specs[0] = pl.BlockSpec(left.shape, lambda i: (0, 0))
        operands.insert(0, dealt_from[None, :])
        in_specs.insert(0, pl.BlockSpec((1, dealt_from.shape[0]), lambda i: (0, 0)))
    return pl.pallas_call(
        lambda *refs: products_kernel(dims, rows, *refs),
        grid=(TP // 2,),
        in_specs=in_specs,
        out_specs=[pl.BlockSpec((1, rows, width), lambda i: (i, 0, 0))] * 2,
        out_shape=[jax.ShapeDtypeStruct((TP // 2, rows, width), bf16)] * 2,
        compiler_params=params(16),
        cost_estimate=lasting(4),
        name="two_products",
    )(*operands)


def shards_kernel(splits, sums_ref, gain_ref, weight_refs, out_refs, gain_grad_ref):
    sources = sums_ref.shape[0]
    turned = jnp.zeros(gain_grad_ref.shape, f32)
    for part in range(TP):
        total = sums_ref[part].astype(f32)
        for more in range(part + TP, sources, TP):
            total = total + sums_ref[more].astype(f32)
        start = 0
        for (width, stride, offset), weight_ref, out_ref in zip(splits, weight_refs, out_refs):
            here = slice(offset + part * stride, offset + part * stride + width)
            piece = total[:, start : start + width]
            product = piece * weight_ref[:, here].astype(f32)
            turned = turned + jnp.sum(product, axis=1, keepdims=True)
            out_ref[:, here] = piece * gain_ref[...]
            start = start + width
    gain_grad_ref[...] = turned


def shard_grads(sums, gain, splits, *weights):
    rows = gain.shape[0]
    count = len(weights)
    owners = [min(at, count - 1) for at in range(len(splits))]

    def kernel(sums_ref, gain_ref, *refs):
        weight_refs = [refs[at] for at in owners]
        out_refs = [refs[count + at] for at in owners]
        shards_kernel(splits, sums_ref, gain_ref, weight_refs, out_refs, refs[-1])

    return pl.pallas_call(
        kernel,
        out_shape=[jax.ShapeDtypeStruct(weight.shape, f32) for weight in weights]
        + [jax.ShapeDtypeStruct((rows, 1), f32)],
        compiler_params=params(16),
        cost_estimate=lasting(3),
        name="shard_grads",
    )(sums, gain, *weights)


def swap(array, axes):
    return lax.all_to_all(array, axes, split_axis=0, concat_axis=0, tiled=True)


def gather(array, axes):
    return lax.all_gather(array, axes, axis=0, tiled=True)


def across(array, distance):
    return lax.ppermute(array, "tp", [(at, at ^ distance) for at in range(TP)])


def onward(array, count, step):
    pairs = [(at, at + step) for at in range(count) if 0 <= at + step < count]
    return lax.ppermute(array, GROUP, pairs)


def gather_hop(own):
    far = across(own, 6)
    return across(own, 2), across(own, 4), far


def gather_cores(own, near):
    quad = jnp.stack([own, *near])
    both = jnp.stack([quad, across(quad, 1)], axis=1)
    return both.reshape((TP * own.shape[0],) + own.shape[1:])


def gather_tp(own):
    return gather_cores(own, gather_hop(own))


def chip_send(sums):
    return sums[0], [across(sums[turn].astype(bf16), 2 * turn) for turn in (3, 1, 2)]


def chip_hop(keep, met):
    return chip_send(keep.astype(f32) + met.astype(f32))


def last_hop(own, got):
    return own + sum(part.astype(f32) for part in got)


def sum_back(left, right, dims, rows):
    keep, send = two_products(left, right, dims, rows)
    return last_hop(*chip_hop(keep, across(send, 1)))


def chip_sums(keep_ref, met_ref, chip, half):
    size = keep_ref.shape[2] // 2
    rows = slice(half * size, (half + 1) * size)
    return keep_ref[chip, 0, rows].astype(f32) + met_ref[chip, 0, rows].astype(f32)


def leave_kernel(keep_ref, met_ref, along_ref, aside_ref):
    for turn in range(2):
        along_ref[turn, 0] = chip_sums(keep_ref, met_ref, 2 * turn + 1, 0).astype(bf16)
        aside_ref[turn, 0] = chip_sums(keep_ref, met_ref, 2 + turn, 1).astype(bf16)


def pass_kernel(keep_ref, met_ref, along_ref, aside_ref, out_along_ref, out_aside_ref):
    along = chip_sums(keep_ref, met_ref, 2, 0) + along_ref[1, 0].astype(f32)
    aside = chip_sums(keep_ref, met_ref, 1, 1) + aside_ref[1, 0].astype(f32)
    out_along_ref[0] = along.astype(bf16)
    out_aside_ref[0] = aside.astype(bf16)


def total_kernel(keep_ref, met_ref, along_ref, aside_ref, far_ref, side_ref, out_ref):
    size = keep_ref.shape[2] // 2
    along = chip_sums(keep_ref, met_ref, 0, 0) + along_ref[0, 0].astype(f32)
    aside = chip_sums(keep_ref, met_ref, 0, 1) + aside_ref[0, 0].astype(f32)
    out_ref[0, :size] = (along + far_ref[0].astype(f32)).astype(bf16)
    out_ref[0, size:] = (aside + side_ref[0].astype(f32)).astype(bf16)


def hop_call(kernel, name, keep, outs, *operands):
    groups, rows = keep.shape[1:3]
    four = pl.BlockSpec((4, 1, rows, LANES), lambda i: (0, i, 0, 0))
    two = pl.BlockSpec((2, 1, rows // 2, LANES), lambda i: (0, i, 0, 0))
    one = pl.BlockSpec((1, rows // 2, LANES), lambda i: (i, 0, 0))
    whole = pl.BlockSpec((1, rows, LANES), lambda i: (i, 0, 0))
    specs = {"two": two, "one": one, "whole": whole}
    shapes = {
        "two": (2, groups, rows // 2, LANES),
        "one": (groups, rows // 2, LANES),
        "whole": (groups, rows, LANES),
    }
    return pl.pallas_call(
        kernel,
        grid=(groups,),
        in_specs=[four, four, two, two, one, one][: len(operands) + 1],
        out_specs=[specs[out] for out in outs],
        out_shape=[jax.ShapeDtypeStruct(shapes[out], bf16) for out in outs],
        compiler_params=params(16),
        cost_estimate=lasting(keep.size / 5e5),
        name=name,
    )(keep, *operands)


def sum_groups_start(total, groups, group_index):
    parts = [lax.dynamic_index_in_dim(total, group_index, 0, keepdims=False)]
    low = total.astype(bf16)
    for away in range(1, groups):
        piece = lax.dynamic_index_in_dim(
            low, lax.rem(group_index + away, groups), 0, keepdims=False
        )
        pairs = [(at, (at + away) % groups) for at in range(groups)]
        parts.append(lax.ppermute(piece, GROUP, pairs))
    return parts


def sum_groups(total, groups, group_index):
    return sum(part.astype(f32) for part in sum_groups_start(total, groups, group_index))


def shift(own, groups, away):
    return lax.ppermute(own, GROUP, [(at, (at + away) % groups) for at in range(groups)])


def by_group(own, shifts, groups, group_index):
    result = jnp.zeros((groups,) + own.shape, own.dtype)
    result = lax.dynamic_update_index_in_dim(result, own, group_index, 0)
    for away, piece in shifts.items():
        source = lax.rem(group_index + groups - away, groups)
        result = lax.dynamic_update_index_in_dim(result, piece, source, 0)
    return result


def rows_home(attn_parts, memory_sums, pairs):
    attn_sums = sum(part.astype(f32) for part in attn_parts).astype(bf16)
    memory_sums = memory_sums.reshape((2,) + attn_sums.shape)
    return lax.ppermute(jnp.concatenate([attn_sums[None], memory_sums]), ALL, pairs)


def tie(*arrays):
    return lax.optimization_barrier(arrays)


def norm_scale(hidden):
    return lax.rsqrt(jnp.mean(hidden * hidden, axis=-1, keepdims=True) + epsilon)


def norm_back(hidden, scale, weighted):
    coupled = jnp.mean(hidden * weighted, axis=-1, keepdims=True)
    return scale * weighted - hidden * (scale * scale * scale) * coupled


def body(
    inputs,
    attn_gain,
    attn_qkv,
    attn_out,
    memory_gain,
    memory_query,
    sub_keys,
    memory_gate,
    memory_out,
    memory_values,
    doc_lengths,
    token_order,
    memory_picks,
    cotangent,
):
    rows, width = inputs.shape
    outer = lax.axis_size("outer")
    heads = lax.axis_size("head")
    groups = heads * outer
    blocks = outer * TP
    devices = groups * TP
    share = rows // blocks
    fold = TP * share
    span = TP * rows
    tokens = token_order.shape[0]
    head_index = lax.axis_index("head")
    outer_index = lax.axis_index("outer")
    here = lax.axis_index("tp")
    here_word = here.astype(jnp.int32)[None]
    group_index = head_index * outer + outer_index
    rows_w = attn_qkv.shape[0]
    subs = memory_values.shape[0] // NSUB
    picks = MH * KPICK
    capacity = 2 * rows * picks // devices
    back = min(groups - 1, -(-(tokens // 2 - 1) // span))
    base = back * span

    near = gather_hop(inputs)
    row_cut = jnp.stack([attn_out, memory_out, sub_keys.reshape(rows_w, width)])
    own_cot, row_cut, *near = tie(cotangent, row_cut, *near)
    near_cot = gather_hop(own_cot)
    to_turned = [
        (groups * part + group, group * TP + part) for group in range(groups) for part in range(TP)
    ]
    from_turned = [(there, at) for at, there in to_turned]
    row_cut = lax.ppermute(row_cut, ALL, to_turned)
    group_inputs = gather_cores(inputs, near)
    gain_one = attn_gain.astype(f32)[:, None]
    gain_two = memory_gain.astype(f32)[:, None]
    scaled_qkv = (attn_qkv.astype(f32) * gain_one).astype(bf16)
    scaled_query = (memory_query.astype(f32) * gain_two).astype(bf16)
    scaled_gate = (memory_gate.astype(f32) * gain_two).astype(bf16)
    qkv_cut = jnp.transpose(scaled_qkv.reshape(rows_w, 3, TP, LANES), (2, 0, 1, 3))
    qkv_cut = jnp.broadcast_to(
        qkv_cut.reshape(1, TP, rows_w, 3 * LANES), (groups, TP, rows_w, 3 * LANES)
    ).reshape(devices, rows_w, 3 * LANES)
    weight_qkv = swap(qkv_cut, ALL).reshape(width, 3 * LANES)

    def columns(piece):
        return jnp.moveaxis(piece.reshape(rows_w, TP, -1), 1, 0)

    by_half = jnp.transpose(memory_picks.reshape(outer, fold, MH, KPICK, 2), (0, 2, 4, 3, 1))
    by_half = by_half.reshape(blocks, KPICK, fold).astype(bf16)
    rest_cut = jnp.concatenate([columns(scaled_query), columns(scaled_gate)], axis=2)
    rest_width = rest_cut.shape[2]

    laid = token_order.reshape(heads, blocks, outer, fold)
    mine = lax.dynamic_index_in_dim(laid, head_index, 0, keepdims=False)
    mine = lax.dynamic_index_in_dim(mine, outer_index, 1, keepdims=False)
    local = jnp.bitwise_xor(mine.reshape(span) - group_index * span, here * rows)
    span_range = jnp.arange(span, dtype=jnp.int32)
    deal = (local[:, None] == span_range[None, :]).astype(bf16)

    group_wide = group_inputs.astype(f32)
    normed_one = (group_wide * norm_scale(group_wide)).astype(bf16)
    projected = mm(normed_one, weight_qkv).astype(bf16)
    queries = projected[:, :LANES] * jnp.asarray(1.0 / math.sqrt(HD), bf16)
    kv_pieces = [projected[:, LANES:]]
    own_picks, rest_cut, by_half, kv_pieces[0] = tie(
        memory_picks, rest_cut, by_half, kv_pieces[0]
    )
    if back > 0:
        kv_pieces.insert(0, onward(kv_pieces[0], groups, 1))
    if by_half.shape[:2] == rest_cut.shape[:2]:
        both = swap(jnp.concatenate([rest_cut, by_half], axis=2), "tp")
        rest_rows, by_half = both[:, :, :rest_width], both[:, :, rest_width:]
    else:
        rest_rows, by_half = swap(rest_cut, "tp"), swap(by_half, BLK)
    rest_rows = rest_rows.reshape(TP * rows_w, rest_width)
    kv_pieces[0], row_cut, *near_cot = tie(kv_pieces[0], row_cut, *near_cot)
    for away in range(1, back):
        kv_pieces.insert(0, onward(kv_pieces[0], groups, 1))
    group_cot = gather_cores(own_cot, near_cot)

    first_pick = own_picks[:, :, :, 0].reshape(rows, picks)
    second_pick = own_picks[:, :, :, 1].reshape(rows, picks)
    owner = first_pick // subs
    device_range = jnp.arange(devices, dtype=jnp.int32)
    owned = (owner[None] == device_range[:, None, None]).astype(bf16)
    before = (
        jnp.arange(picks, dtype=jnp.int32)[:, None] < jnp.arange(picks, dtype=jnp.int32)[None, :]
    ).astype(bf16)
    before_rows = (
        jnp.arange(rows, dtype=jnp.int32)[:, None] < jnp.arange(rows, dtype=jnp.int32)[None, :]
    ).astype(bf16)
    in_row = jnp.einsum("dtk,kj->dtj", owned, before, preferred_element_type=f32)
    row_counts = jnp.sum(owned.astype(f32), axis=2)
    of_rows = jnp.dot(row_counts.astype(bf16), before_rows, preferred_element_type=f32)
    rank = jnp.sum(owned.astype(f32) * (in_row + of_rows[:, :, None]), axis=0).astype(jnp.int32)
    target = owner * capacity + rank
    target_high = target // LANES
    target_low = target % LANES
    places = devices * capacity
    entries = make_entries(target_high, target_low, first_pick % subs, second_pick, places)

    turned_one, unused = tie(jnp.transpose(normed_one), kv_pieces[0])
    keys_values, rest_rows, by_half, entries, turned_one, row_cut = tie(
        jnp.concatenate(kv_pieces, axis=0),
        rest_rows,
        by_half,
        entries,
        turned_one,
        row_cut,
    )
    half_index = jnp.moveaxis(by_half, 1, 0).reshape(KPICK, span).astype(jnp.int32)
    wide_index = jnp.pad(jnp.transpose(half_index), ((0, 0), (0, LANES - KPICK)))
    rest_shifts = {away: shift(rest_rows, groups, away) for away in range(1, groups, 2)}
    doc_ends = jnp.cumsum(doc_lengths)

    def lowest(inside):
        positions = group_index * span + inside
        starts = jnp.where(positions[:, None] >= doc_ends[None, :], doc_ends[None, :], 0)
        return jnp.max(starts, axis=1) - (group_index - back) * span

    low_first = lowest(span_range)
    low = lowest(jnp.bitwise_xor(span_range, here * rows))
    attended, lse, attended_low = attn_fwd(
        base, rows, (0, back + 1), low_first, here_word, low, queries, keys_values
    )
    split = back > 1
    near_bounds = (1 if split else 0, back + 1)
    far_kv = keys_values[:span]
    near_kv = keys_values[near_bounds[0] * span :]
    attn_shifts = {away: shift(row_cut[0], groups, away) for away in range(1, groups)}
    attended_low, group_cot, rest_rows, *shifted = tie(
        attended_low, group_cot, rest_rows, *attn_shifts.values(), *rest_shifts.values()
    )
    attn_shifts = dict(zip(attn_shifts, shifted))
    rest_shifts = dict(zip(rest_shifts, shifted[len(attn_shifts) :]))
    weight_attn = by_group(row_cut[0], attn_shifts, groups, group_index).reshape(LANES, width)
    even_shifts = {away: shift(rest_rows, groups, away) for away in range(2, groups, 2)}
    inputs_wide = inputs.astype(f32)
    hidden_one = inputs_wide + sum_back(attended_low, weight_attn, NN, rows)
    hidden_one, row_cut, *shifted = tie(hidden_one, row_cut, *even_shifts.values())
    rest_shifts.update(zip(even_shifts, shifted))
    weight_rest = by_group(rest_rows, rest_shifts, groups, group_index).reshape(width, rest_width)
    row_shifts = {away: shift(row_cut[1:], groups, away) for away in range(1, groups)}
    row_all = by_group(row_cut[1:], row_shifts, groups, group_index)
    row_all = jnp.moveaxis(row_all, 0, 1).reshape(2, LANES, width)
    weight_mixed = row_all[0]
    key_table = row_all[1].reshape(NSUB, QHALF)
    scale_two = norm_scale(hidden_one)
    dealt_cot = mm(deal, group_cot).astype(bf16)
    grad_mixed = mm(dealt_cot, weight_mixed, NT)
    normed_two = mm(deal, gather_tp((hidden_one * scale_two).astype(bf16))).astype(bf16)

    pre = mm(normed_two, weight_rest)
    query_mem = pre[:, :QHALF].astype(bf16)
    gate_pre = pre[:, QHALF:]
    gate_sig = jax.nn.sigmoid(gate_pre)
    grad_memory = (grad_mixed * gate_pre * gate_sig).astype(bf16)
    query_mem, grad_memory = tie(query_mem, grad_memory)
    every_grad = gather(grad_memory, ALL).reshape(heads, outer, TP, blocks, fold, LANES)
    picked_half = pick_scores(query_mem, key_table, wide_index).reshape(KPICK, blocks, fold)
    picked = swap(jnp.moveaxis(picked_half, 1, 0), BLK)
    turned_two, unused = tie(jnp.transpose(normed_two), picked_half)
    picked, turned_two = tie(picked, turned_two)
    picked = jnp.moveaxis(picked.reshape(outer, TP, KPICK, fold), 0, 2).reshape(TP, KPICK, rows)
    pick_weights, sent_weights = make_weights(picked, target_high, target_low, places)
    sent = jnp.concatenate([entries, sent_weights], axis=1)
    sent = jnp.moveaxis(sent.reshape(devices, capacity // LANES, 4, LANES), 2, 1)
    entries = swap(sent.reshape(devices, 4, capacity), ALL).astype(f32)
    entries = entries.reshape(heads, blocks, 4, 1, capacity)
    entry_token = entries[:, :, 0].astype(jnp.int32)
    entry_first = entries[:, :, 1].astype(jnp.int32)
    entry_second = entries[:, :, 2].astype(jnp.int32)
    entry_weight = entries[:, :, 3]

    turns = 2
    table = None
    leaving = []
    flat = (TP // 2, groups, span // turns, LANES)
    for turn in range(turns):
        table, keep, send = spread_weights(
            rows,
            subs,
            heads,
            outer,
            turn,
            turns,
            here_word,
            entry_token,
            entry_first,
            entry_second,
            entry_weight,
            memory_values,
            table,
        )
        leaving.append((keep.reshape(flat), across(send.reshape(flat), 1)))
    dots = []
    dense = None

    def more_dots(dense, *moved):
        if len(dots) == heads:
            return dense, moved
        part, dense = row_dots(
            rows,
            subs,
            len(dots),
            heads,
            outer,
            entry_token,
            entry_first,
            entry_second,
            every_grad,
            memory_values,
            dense,
        )
        part, dense, *moved = tie(part, dense, *moved)
        dots.append(part)
        return dense, moved

    def sums_call(kernel, name, outs, half, *operands):
        keep, met = leaving[half]
        return hop_call(kernel, name, keep, outs, met, *operands)

    leaves = sums_call(leave_kernel, "sums_first", ("two", "two"), 0)
    every_grad, *leaves = tie(every_grad, *leaves)
    first = [[across(leaves[0], 2), across(leaves[1], 4)]]
    dense, leaving[1] = more_dots(dense, *leaving[1])
    leaves = sums_call(leave_kernel, "sums_first", ("two", "two"), 1)
    dense, *leaves = tie(dense, *leaves)
    first.append([across(leaves[0], 2), across(leaves[1], 4)])
    dense, first[0] = more_dots(dense, *first[0])
    leaves = sums_call(pass_kernel, "sums_second", ("one", "one"), 0, *first[0])
    dense, *leaves = tie(dense, *leaves)
    second = [[across(leaves[0], 4), across(leaves[1], 2)]]
    dense, moved = more_dots(dense, *first[1], *second[0])
    first[1], second[0] = moved[:2], moved[2:]
    leaves = sums_call(pass_kernel, "sums_second", ("one", "one"), 1, *first[1])
    total = sums_call(total_kernel, "sums_last", ("whole",), 0, *first[0], *second[0])
    dense, *leaves = tie(dense, *leaves)
    second.append([across(leaves[0], 4), across(leaves[1], 2)])
    dense, second[1] = more_dots(dense, *second[1])
    while len(dots) < heads:
        dense, unused = more_dots(dense)
    total += sums_call(total_kernel, "sums_last", ("whole",), 1, *first[1], *second[1])
    total = jnp.concatenate(total, axis=1)
    memory = sum_groups(total, groups, group_index)

    entry_dots = jnp.concatenate(dots, axis=0).reshape(devices, capacity)
    returned = swap(entry_dots, ALL).reshape(places // LANES, LANES)
    table = table.reshape(tokens, subs * NSUB)
    dense = dense.reshape(tokens, width)
    grad_values = value_grads(0, turns, table, dense, None)
    returned, grad_values = tie(returned, grad_values)
    grad_picked = pick_grads(target_high, target_low, pick_weights, returned)
    to_half = jnp.moveaxis(grad_picked.reshape(MH, KPICK, outer, fold), 2, 0)
    to_half = jnp.broadcast_to(to_half[:, :, None], (outer, MH, 2, KPICK, fold))
    grad_half = swap(to_half.reshape(blocks, KPICK, fold), BLK)
    grad_half = jnp.moveaxis(grad_half, 1, 0).reshape(KPICK, span)
    grad_sub, grad_query = unpick_scores(grad_half, half_index, key_table)

    mixed_low = (memory * gate_pre * gate_sig).astype(bf16)
    grad_gate = (grad_mixed * memory * gate_sig * (1.0 + gate_pre * (1.0 - gate_sig))).astype(bf16)
    grad_pre = jnp.concatenate([grad_query, grad_gate], axis=1)
    keep, send = two_products(grad_pre, weight_rest, NT, rows, local)
    met = across(send, 1)

    met, grad_pre, mixed_low, grad_sub = tie(met, grad_pre, mixed_low, grad_sub)
    own, got = chip_hop(keep, met)
    rest_grads = mm(turned_two, grad_pre).astype(bf16)
    row_grads = [mm(mixed_low, dealt_cot, TN), mm(grad_sub, query_mem).reshape(LANES, width)]
    row_grads = jnp.stack(row_grads).astype(bf16).reshape(2, groups, rows_w, width)
    row_grads = jnp.moveaxis(row_grads, 0, 1).reshape(groups * TP * rows_w, -1)
    memory_grads = jnp.concatenate([rest_grads, row_grads], axis=1)
    memory_grads, mixed_low, *got = tie(memory_grads, mixed_low, *got)
    memory_grads = lax.psum_scatter(memory_grads, GROUP, scatter_dimension=0, tiled=True)
    weighted_two = last_hop(own, got)
    grad_hidden = cotangent.astype(f32) + norm_back(hidden_one, scale_two, weighted_two)

    output_keep, output_met = two_products(mixed_low, weight_mixed, NN, rows, local)
    own_branch = grad_hidden.astype(bf16)
    near_branch = gather_hop(own_branch)
    output_keep, output_met, *near_branch = tie(output_keep, output_met, *near_branch)
    output_met = across(output_met, 1)
    grad_branch = gather_cores(own_branch, near_branch)
    grad_attended = mm(grad_branch, weight_attn, NT).astype(bf16)
    through = (low_first, here_word, low, queries)
    results = (lse, attended, grad_attended)
    far = far_grads = ()
    if split:
        far_grad_q, *far_grads = attn_bwd(base, rows, (0, 1), *through, far_kv, *results)
        far = (far_grad_q,)
        output_keep, output_met, far_grads[0] = tie(output_keep, output_met, far_grads[0])
        output_own, output_got = chip_hop(output_keep, output_met)
        attended_low, far_grads[0] = tie(attended_low, far_grads[0])
    attn_rows = mm(attended_low, grad_branch, TN).astype(bf16).reshape(groups, rows_w, width)
    attn_rows = sum_groups_start(attn_rows, groups, group_index)
    grad_q, *grad_kv = attn_bwd(base, rows, near_bounds, *through, near_kv, *results, far)
    grad_kv = [*far_grads, *grad_kv]
    if not split:
        output_own, output_got = chip_hop(output_keep, output_met)
    output_own, table, memory_grads, *near_grads = tie(
        output_own, table, memory_grads, *grad_kv[len(far_grads) :]
    )
    grad_kv = [*far_grads, *near_grads]

    row_home = None
    carry = grad_kv[0]
    for away in range(back):
        met = onward(carry, groups, -1)
        if away == back - 1:
            rest_home = swap(memory_grads[:, :rest_width].reshape(TP, rows_w, -1), "tp")
            grad_values = value_grads(1, turns, table, dense, grad_values)
            row_home = rows_home(attn_rows, memory_grads[:, rest_width:], from_turned)
            met, rest_home, row_home, grad_values, *output_got = tie(
                met, rest_home, row_home, grad_values, *output_got
            )
        if away == 0:
            met, memory_grads, table, *attn_rows = tie(met, memory_grads, table, *attn_rows)
        carry = (grad_kv[away + 1].astype(f32) + met.astype(f32)).astype(bf16)
    if back == 0:
        rest_home = swap(memory_grads[:, :rest_width].reshape(TP, rows_w, -1), "tp")
        row_home = rows_home(attn_rows, memory_grads[:, rest_width:], from_turned)
        grad_values = value_grads(1, turns, table, dense, grad_values)
    grad_projected = jnp.concatenate([grad_q, carry], axis=1)

    late_grads = mm(turned_one, grad_projected).astype(bf16)
    grad_projected, late_grads = tie(grad_projected, late_grads)
    qkv_home = swap(late_grads.reshape(devices, rows_w, 3 * LANES), ALL)
    keep, send = two_products(grad_projected, weight_qkv, NT, rows)
    sums = keep.astype(f32) + across(send, 1).astype(f32)
    own, got = chip_send(sums)
    weighted_one = last_hop(own, got)
    grad_inputs = grad_hidden + norm_back(inputs_wide, norm_scale(inputs_wide), weighted_one)
    output = (hidden_one + last_hop(output_own, output_got)).astype(bf16)
    row_home = row_home.astype(f32)
    splits = ((QHALF, QHALF, 0), (LANES, LANES, 0))
    grad_query_home, grad_gate_home, grad_memory_gain = shard_grads(
        rest_home, gain_two, splits, memory_query, memory_gate
    )
    splits = tuple((LANES, LANES, part * width) for part in range(3))
    grad_qkv_home, grad_attn_gain = shard_grads(qkv_home, gain_one, splits, attn_qkv)
    return (
        output,
        grad_inputs,
        grad_attn_gain.reshape(-1),
        grad_qkv_home,
        row_home[0],
        grad_memory_gain.reshape(-1),
        grad_query_home,
        row_home[2].reshape(sub_keys.shape),
        grad_gate_home,
        row_home[1],
        grad_values,
    )


def solution(mesh):
    heads, blocks = mesh.devices.shape
    cut_mesh = Mesh(mesh.devices.reshape(heads, blocks // TP, TP), ALL)
    matrix = P(ALL, None)
    in_specs = (
        matrix,
        P(ALL),
        matrix,
        matrix,
        P(ALL),
        matrix,
        matrix,
        matrix,
        matrix,
        matrix,
        P(),
        P(),
        P(ALL, None, None, None),
        matrix,
    )
    out_specs = (
        matrix,
        matrix,
        P(ALL),
        matrix,
        matrix,
        P(ALL),
        matrix,
        matrix,
        matrix,
        matrix,
        matrix,
    )
    return jax.shard_map(
        body, mesh=cut_mesh, in_specs=in_specs, out_specs=out_specs, check_vma=False
    )
```

```python
import math

import jax
import jax.numpy as jnp
from jax import lax
from jax.experimental import pallas as pl
from jax.experimental.pallas import tpu as pltpu
from jax.sharding import Mesh
from jax.sharding import PartitionSpec as P

NH = 16
HD = 64
MH = 4
QHALF = 512
NSUB = 256
KPICK = 32
TP = 2 * MH

GROUP = ("head", "outer")
BLK = ("outer", "tp")
ALL = ("head", "outer", "tp")

epsilon = 1e-06
neg_big = -1e30
LANES = 128
bf16 = jnp.bfloat16
f32 = jnp.float32
NN = (((1,), (0,)), ((), ()))
NT = (((1,), (1,)), ((), ()))
TN = (((0,), (0,)), ((), ()))


def mm(left, right, dims=NN):
    return lax.dot_general(left, right, dims, preferred_element_type=f32)


def params(mib):
    return pltpu.CompilerParams(vmem_limit_bytes=mib * 1024 * 1024)


def lasting(microseconds):
    return pl.CostEstimate(
        flops=0, bytes_accessed=int(microseconds * 3.5e6), transcendentals=0
    )


def head_rows(pair):
    lane = lax.broadcasted_iota(jnp.int32, pair.shape, 1)
    zero = jnp.zeros_like(pair)
    return (jnp.where(lane < HD, pair, zero), jnp.where(lane < HD, zero, pair))


def turned_block(step, here, block, rows):
    return jnp.bitwise_xor(step, here * rows // block)


def turned_iota(shape, axis, here, rows):
    place = lax.broadcasted_iota(jnp.int32, shape, axis)
    return jnp.bitwise_xor(place, lax.rem(here * rows, shape[axis]))


def key_blocks(step, base, span, bounds, block_q, block_k, low_first_ref):
    first = jnp.maximum(low_first_ref[step], bounds[0] * span) // block_k
    stop = (base + (step + 1) * block_q - 1) // block_k + 1
    return first, jnp.minimum(stop, bounds[1] * span // block_k)


def key_start(turn, span, here, block_k, rows, skipped):
    per_group = span // block_k
    group = turn // per_group - skipped
    within = turned_block(lax.rem(turn, per_group), here, block_k, rows)
    return pl.multiple_of(group * span + within * block_k, block_k)


def attn_fwd_kernel(
    base, span, rows, block_k, bounds, low_first_ref, here_ref, q_ref, kv_ref, low_ref, *refs
):
    att_ref, lse_ref, out_ref = refs[-3:]
    block_q = q_ref.shape[0]
    step = pl.program_id(0)
    here = here_ref[0]
    first, stop = key_blocks(step, base, span, bounds, block_q, block_k, low_first_ref)
    queries = head_rows(q_ref[...])
    low = low_ref[...]
    high = base + step * block_q + turned_iota((1, block_q), 1, here, rows)
    inner = turned_iota((block_k, block_q), 0, here, rows)

    def visit(turn, carried):
        start = key_start(turn, span, here, block_k, rows, bounds[0])
        keys = kv_ref[pl.ds(start, block_k), :LANES]
        values = kv_ref[pl.ds(start, block_k), LANES:]
        place = turn * block_k + inner
        allowed = (place >= low) & (place <= high)
        out = []
        for head in range(2):
            run_max, run_sum, run_acc = carried[head]
            scores = jnp.where(allowed, mm(keys, queries[head], NT), neg_big)
            new_max = jnp.maximum(run_max, jnp.max(scores, axis=0, keepdims=True))
            powers = jnp.exp(scores - new_max)
            rescale = jnp.exp(run_max - new_max)
            run_sum = run_sum * rescale + jnp.sum(powers, axis=0, keepdims=True)
            run_acc = run_acc * rescale + mm(values, powers.astype(bf16), TN)
            out.append((new_max, run_sum, run_acc))
        return tuple(out)

    if len(refs) > 3:
        near_att = refs[0][...]
        fresh = tuple(
            (refs[1][head : head + 1, :], jnp.ones((1, block_q), f32), near_att)
            for head in range(2)
        )
    else:
        fresh = (
            jnp.full((1, block_q), neg_big, f32),
            jnp.zeros((1, block_q), f32),
            jnp.zeros((LANES, block_q), f32),
        )
        fresh = (fresh, fresh)
    done = lax.fori_loop(first, stop, visit, fresh)
    att_ref[:HD, :] = done[0][2][:HD] / done[0][1]
    att_ref[HD:, :] = done[1][2][HD:] / done[1][1]
    out_ref[...] = jnp.transpose(att_ref[...]).astype(bf16)
    lse_ref[0:1, :] = done[0][0] + jnp.log(done[0][1])
    lse_ref[1:2, :] = done[1][0] + jnp.log(done[1][1])


def attn_specs(block_q, rows, span):
    def turn(i, here):
        return turned_block(i, here[0], block_q, rows)

    return (
        pl.BlockSpec((block_q, LANES), lambda i, s, here: (turn(i, here), 0)),
        pl.BlockSpec((1, block_q), lambda i, s, here: (0, turn(i, here))),
        pl.BlockSpec((2, block_q), lambda i, s, here: (0, turn(i, here))),
        pl.BlockSpec((LANES, block_q), lambda i, s, here: (0, turn(i, here))),
    )


def attn_fwd(base, rows, bounds, low_first, here, low, queries, keys_values, near=()):
    span = queries.shape[0]
    block_q, block_k = 512, 512
    by_row, one_lane, two_lane, by_lane = attn_specs(block_q, rows, span)
    in_specs = [
        by_row,
        pl.BlockSpec(keys_values.shape, lambda i, s, here: (0, 0)),
        one_lane,
        by_lane,
        two_lane,
    ]
    return pl.pallas_call(
        lambda *refs: attn_fwd_kernel(base, span, rows, block_k, bounds, *refs),
        grid_spec=pltpu.PrefetchScalarGridSpec(
            num_scalar_prefetch=2,
            grid=(span // block_q,),
            in_specs=in_specs[: 3 + len(near)],
            out_specs=[by_lane, two_lane, by_row],
        ),
        out_shape=[
            jax.ShapeDtypeStruct((LANES, span), f32),
            jax.ShapeDtypeStruct((2, span), f32),
            jax.ShapeDtypeStruct((span, LANES), bf16),
        ],
        compiler_params=params(24),
        cost_estimate=lasting(keys_values.shape[0] / 250),
        name="attn_fwd",
    )(low_first[::block_q], here, queries, keys_values, low[None, :], *near)


def attn_bwd_kernel(
    base,
    span,
    rows,
    block_k,
    bounds,
    low_first_ref,
    here_ref,
    q_ref,
    kv_ref,
    low_ref,
    lse_ref,
    att_ref,
    grad_ref,
    *refs,
):
    dk_ref, dv_ref = refs[-2:]
    count = bounds[1] - bounds[0]
    out_refs = refs[-2 - count : -2]
    dq_ref = refs[-3 - count]
    block_q = q_ref.shape[0]
    step = pl.program_id(0)
    here = here_ref[0]
    first, stop = key_blocks(step, base, span, bounds, block_q, block_k, low_first_ref)

    @pl.when(step == 0)
    def clear():
        dk_ref[...] = jnp.zeros_like(dk_ref)
        dv_ref[...] = jnp.zeros_like(dv_ref)

    queries = head_rows(q_ref[...])
    grads = head_rows(grad_ref[...])
    grad_turned = jnp.transpose(grad_ref[...].astype(f32)) * att_ref[...]
    deltas = (
        jnp.sum(grad_turned[:HD], axis=0, keepdims=True),
        jnp.sum(grad_turned[HD:], axis=0, keepdims=True),
    )
    low = low_ref[...]
    high = base + step * block_q + turned_iota((1, block_q), 1, here, rows)
    inner = turned_iota((block_k, block_q), 0, here, rows)

    def visit(turn, carried):
        start = key_start(turn, span, here, block_k, rows, bounds[0])
        keys = kv_ref[pl.ds(start, block_k), :LANES]
        values = kv_ref[pl.ds(start, block_k), LANES:]
        place = turn * block_k + inner
        allowed = (place >= low) & (place <= high)
        out = []
        grad_key = dk_ref[pl.ds(start, block_k), :]
        grad_value = dv_ref[pl.ds(start, block_k), :]
        for head in range(2):
            scores = mm(keys, queries[head], NT)
            probs = jnp.where(allowed, jnp.exp(scores - lse_ref[head : head + 1, :]), 0.0)
            grad_probs = mm(values, grads[head], NT)
            grad_scores = (probs * (grad_probs - deltas[head])).astype(bf16)
            grad_key = grad_key + mm(grad_scores, queries[head])
            grad_value = grad_value + mm(probs.astype(bf16), grads[head])
            out.append(carried[head] + mm(keys, grad_scores, TN))
        dk_ref[pl.ds(start, block_k), :] = grad_key
        dv_ref[pl.ds(start, block_k), :] = grad_value
        return tuple(out)

    fresh = jnp.zeros((LANES, block_q), f32)
    done = lax.fori_loop(first, stop, visit, (fresh, fresh))
    turned = jnp.concatenate([done[0][:HD], done[1][HD:]], axis=0) * (1.0 / math.sqrt(HD))
    total = jnp.transpose(turned)
    if len(refs) > 3 + count:
        total = total + refs[0][...].astype(f32)
    dq_ref[...] = total.astype(bf16)

    @pl.when(step == span // block_q - 1)
    def leave():
        for turn, out_ref in enumerate(out_refs):
            out_ref[:, :LANES] = dk_ref[turn * span : (turn + 1) * span, :].astype(bf16)
            out_ref[:, LANES:] = dv_ref[turn * span : (turn + 1) * span, :].astype(bf16)


def attn_bwd(
    base, rows, bounds, low_first, here, low, queries, keys_values, lse, att, grads, far=()
):
    span = queries.shape[0]
    block_q, block_k = 512, 512
    reach = keys_values.shape[0]
    by_row, one_lane, two_lane, by_lane = attn_specs(block_q, rows, span)
    in_specs = [
        by_row,
        pl.BlockSpec(keys_values.shape, lambda i, s, here: (0, 0)),
        one_lane,
        two_lane,
        by_lane,
        by_row,
        by_row,
    ]
    return pl.pallas_call(
        lambda *refs: attn_bwd_kernel(base, span, rows, block_k, bounds, *refs),
        grid_spec=pltpu.PrefetchScalarGridSpec(
            num_scalar_prefetch=2,
            grid=(span // block_q,),
            in_specs=in_specs[: 6 + len(far)],
            out_specs=[by_row]
            + [pl.BlockSpec((span, 2 * LANES), lambda i, s, here: (0, 0))] * (reach // span),
            scratch_shapes=[pltpu.VMEM((reach, LANES), f32), pltpu.VMEM((reach, LANES), f32)],
        ),
        out_shape=[jax.ShapeDtypeStruct((span, LANES), bf16)]
        + [jax.ShapeDtypeStruct((span, 2 * LANES), bf16)] * (reach // span),
        compiler_params=params(32),
        cost_estimate=lasting(keys_values.shape[0] / 200),
        name="attn_bwd",
    )(low_first[::block_q], here, queries, keys_values, low[None, :], lse, att, grads, *far)


def hits(count, row):
    return lax.broadcasted_iota(jnp.int32, (count, row.shape[1]), 0) == row


def one_hot(count, row):
    return jnp.where(hits(count, row), 1.0, 0.0).astype(bf16)


def wide_hits(count, ref, top, rows):
    return [hits(count, ref[row : row + 1, :]) for row in range(top, top + rows)]


def bucket_rows(high_ref, low_ref, load_refs, places):
    batch = 8
    total = jnp.zeros((places, len(load_refs) * LANES), f32)
    for top in range(0, high_ref.shape[0], batch):
        high = [
            jnp.where(hit, 1.0, 0.0).astype(bf16) for hit in wide_hits(places, high_ref, top, batch)
        ]
        low = wide_hits(LANES, low_ref, top, batch)
        parts = [
            jnp.concatenate(
                [
                    jnp.where(low[row], load_ref[top + row : top + row + 1, :], 0.0).astype(bf16)
                    for row in range(batch)
                ],
                axis=1,
            )
            for load_ref in load_refs
        ]
        total = total + mm(jnp.concatenate(high, axis=1), jnp.concatenate(parts, axis=0), NT)
    return total


def entries_kernel(high_ref, low_ref, first_ref, second_ref, out_ref, token_ref):
    token_ref[...] = lax.broadcasted_iota(jnp.int32, token_ref.shape, 0).astype(f32)
    loads = (token_ref, first_ref, second_ref)
    out_ref[...] = bucket_rows(high_ref, low_ref, loads, out_ref.shape[0]).astype(bf16)


def make_entries(high, low, first, second, places):
    return pl.pallas_call(
        entries_kernel,
        out_shape=jax.ShapeDtypeStruct((places // LANES, 3 * LANES), bf16),
        scratch_shapes=[pltpu.VMEM(high.shape, f32)],
        compiler_params=params(16),
        cost_estimate=lasting(5),
        name="make_entries",
    )(high, low, first.astype(f32), second.astype(f32))


def weights_kernel(picked_ref, high_ref, low_ref, weight_ref, out_ref):
    parts = []
    for head in range(MH):
        picked = picked_ref[2 * head] + picked_ref[2 * head + 1]
        powers = jnp.exp(picked - jnp.max(picked, axis=0, keepdims=True))
        parts.append(powers / jnp.sum(powers, axis=0, keepdims=True))
    weight_ref[...] = jnp.transpose(jnp.concatenate(parts, axis=0))
    out_ref[...] = bucket_rows(high_ref, low_ref, (weight_ref,), out_ref.shape[0]).astype(bf16)


def make_weights(picked, high, low, places):
    return pl.pallas_call(
        weights_kernel,
        out_shape=[
            jax.ShapeDtypeStruct(high.shape, f32),
            jax.ShapeDtypeStruct((places // LANES, LANES), bf16),
        ],
        compiler_params=params(16),
        cost_estimate=lasting(3),
        name="make_weights",
    )(picked, high, low)


def grads_kernel(high_ref, low_ref, weight_ref, table_ref, out_ref, found_ref):
    turned = jnp.transpose(table_ref[...])
    main = turned.astype(bf16)
    rest = (turned - main.astype(f32)).astype(bf16)
    batch = 8
    for top in range(0, high_ref.shape[0], batch):
        high = jnp.concatenate(
            [
                jnp.where(hit, 1.0, 0.0).astype(bf16)
                for hit in wide_hits(table_ref.shape[0], high_ref, top, batch)
            ],
            axis=1,
        )
        found = mm(main, high) + mm(rest, high)
        low = jnp.concatenate(wide_hits(LANES, low_ref, top, batch), axis=1)
        line = jnp.sum(jnp.where(low, found, 0.0), axis=0, keepdims=True)
        for row in range(batch):
            found_ref[top + row : top + row + 1, :] = line[:, row * LANES : (row + 1) * LANES]
    grads = jnp.transpose(found_ref[...])
    weights = jnp.transpose(weight_ref[...])
    for head in range(MH):
        rows = slice(head * KPICK, (head + 1) * KPICK)
        coupled = jnp.sum(weights[rows] * grads[rows], axis=0, keepdims=True)
        out_ref[rows, :] = weights[rows] * (grads[rows] - coupled)


def pick_grads(high, low, weights, table):
    return pl.pallas_call(
        grads_kernel,
        out_shape=jax.ShapeDtypeStruct((high.shape[1], high.shape[0]), f32),
        scratch_shapes=[pltpu.VMEM(high.shape, f32)],
        compiler_params=params(16),
        cost_estimate=lasting(5),
        name="pick_grads",
    )(high, low, weights, table)


def place_rows(rows, subs, token_row, first_row):
    tokens = one_hot(rows, token_row)
    return jnp.concatenate(
        [tokens * jnp.where(first_row == first, 1.0, 0.0).astype(bf16) for first in range(subs)],
        axis=0,
    )


def spread_kernel(
    rows, subs, outer, here_ref, token_ref, first_ref, second_ref, weight_ref, value_ref, *refs
):
    table_ref, keep_ref, send_ref = refs[-3:]
    count = token_ref.shape[1]
    fold = rows // outer
    for block in range(count):
        left = place_rows(rows, subs, token_ref[0, block], first_ref[0, block])
        right = jnp.where(hits(NSUB, second_ref[0, block]), weight_ref[0, block], 0.0).astype(bf16)
        table = mm(left, right, NT).astype(bf16)
        for first in range(subs):
            table_ref[0, block * rows : (block + 1) * rows, first * NSUB : (first + 1) * NSUB] = (
                table[first * rows : (first + 1) * rows]
            )
    partial = mm(table_ref[0], value_ref[...]).astype(bf16)
    here = here_ref[0]
    chip = here // 2

    def store(core):
        for there in range(TP):
            target_ref = keep_ref if there % 2 == core else send_ref
            place = jnp.bitwise_xor(chip, there // 2)
            for block in range(count):
                for part in range(outer):
                    top = block * rows + part * fold
                    target_ref[place, 0, part, block] = partial[
                        top : top + fold, there * LANES : (there + 1) * LANES
                    ]

    pl.when(here % 2 == 0)(lambda: store(0))
    pl.when(here % 2 == 1)(lambda: store(1))


def spread_weights(
    rows, subs, heads, outer, turn, turns, here, token, first, second, weight, values, table
):
    blocks, capacity = token.shape[1], token.shape[3]
    width = values.shape[1]
    count = 2
    steps = blocks // turns // count
    fold = rows // outer
    row = pl.BlockSpec((1, count, 1, capacity), lambda h, i, s: (h, turn * steps + i, 0, 0))
    piece = pl.BlockSpec(
        (TP // 2, 1, outer, count, fold, LANES), lambda h, i, s: (0, h, 0, i, 0, 0)
    )
    piece_shape = jax.ShapeDtypeStruct(
        (TP // 2, heads, outer, blocks // turns, fold, LANES), bf16
    )
    operands = [here, token, first, second, weight, values]
    in_specs = [row, row, row, row, pl.BlockSpec(values.shape, lambda h, i, s: (0, 0))]
    aliases = {}
    if table is not None:
        operands.append(table)
        in_specs.append(pl.BlockSpec(memory_space=pl.ANY))
        aliases = {6: 0}
    return pl.pallas_call(
        lambda *refs: spread_kernel(rows, subs, outer, *refs),
        grid_spec=pltpu.PrefetchScalarGridSpec(
            num_scalar_prefetch=1,
            grid=(heads, steps),
            in_specs=in_specs,
            out_specs=[
                pl.BlockSpec(
                    (1, count * rows, subs * NSUB), lambda h, i, s: (h, turn * steps + i, 0)
                ),
                piece,
                piece,
            ],
        ),
        out_shape=[
            jax.ShapeDtypeStruct((heads, blocks * rows, subs * NSUB), bf16),
            piece_shape,
            piece_shape,
        ],
        input_output_aliases=aliases,
        compiler_params=params(36),
        cost_estimate=lasting(heads * blocks // turns * rows / 90),
        name="spread_weights",
    )(*operands)


def dots_kernel(
    rows, subs, outer, token_ref, first_ref, second_ref, grad_ref, value_ref, *refs
):
    out_ref, dense_ref = refs[-2:]
    count = token_ref.shape[1]
    fold = rows // outer
    for block in range(count):
        for part in range(outer):
            top = block * rows + part * fold
            for there in range(TP):
                dense_ref[0, top : top + fold, there * LANES : (there + 1) * LANES] = grad_ref[
                    0, part, there, block
                ]
    dense = dense_ref[0]
    found = [
        mm(value_ref[first * NSUB : (first + 1) * NSUB, :], dense, NT).astype(bf16)
        for first in range(subs)
    ]
    for block in range(count):
        left = place_rows(rows, subs, token_ref[0, block], first_ref[0, block])
        table = jnp.concatenate(
            [
                found[first][:, block * rows : (block + 1) * rows] for first in range(subs)
            ],
            axis=1,
        )
        spread = mm(table, left)
        out_ref[0, block] = jnp.sum(
            jnp.where(hits(NSUB, second_ref[0, block]), spread, 0.0), axis=0, keepdims=True
        )


def roomy(heads, size):
    return max(heads, 2**24 // size)


def row_dots(rows, subs, part, parts, outer, token, first, second, grads, values, dense):
    heads, blocks, capacity = token.shape[0], token.shape[1], token.shape[3]
    width = values.shape[1]
    count = 2
    fold = rows // outer
    mine = heads // parts
    top = part * mine
    row = pl.BlockSpec((1, count, 1, capacity), lambda h, i: (top + h, i, 0, 0))
    operands = [token, first, second, grads, values]
    in_specs = [
        row,
        row,
        row,
        pl.BlockSpec((1, outer, TP, count, fold, LANES), lambda h, i: (top + h, 0, 0, i, 0, 0)),
        pl.BlockSpec(values.shape, lambda h, i: (0, 0)),
    ]
    aliases = {}
    if dense is not None:
        operands.append(dense)
        in_specs.append(pl.BlockSpec(memory_space=pl.ANY))
        aliases = {5: 1}
    return pl.pallas_call(
        lambda *refs: dots_kernel(rows, subs, outer, *refs),
        grid=(mine, blocks // count),
        in_specs=in_specs,
        out_specs=[
            pl.BlockSpec((1, count, 1, capacity), lambda h, i: (h, i, 0, 0)),
            pl.BlockSpec((1, count * rows, width), lambda h, i: (top + h, i, 0)),
        ],
        out_shape=[
            jax.ShapeDtypeStruct((mine, blocks, 1, capacity), f32),
            jax.ShapeDtypeStruct((roomy(heads, blocks * rows * width), blocks * rows, width), bf16),
        ],
        input_output_aliases=aliases,
        compiler_params=params(46),
        cost_estimate=lasting(mine * blocks * rows / 90),
        name="row_dots",
    )(*operands)


def value_grads_kernel(table_ref, dense_ref, *refs):
    out_ref = refs[-1]
    out_ref[...] = mm(table_ref[...], dense_ref[...], TN)


def value_grads(turn, turns, table, dense, sums):
    tokens, own_rows = table.shape
    width = dense.shape[1]
    block = min(512, own_rows // turns)
    steps = own_rows // turns // block
    operands = [table, dense]
    in_specs = [
        pl.BlockSpec((tokens, block), lambda i: (0, turn * steps + i)),
        pl.BlockSpec((tokens, width), lambda i: (0, 0), pipeline_mode=pl.Buffered(1)),
    ]
    aliases = {}
    if sums is not None:
        operands.append(sums)
        in_specs.append(pl.BlockSpec(memory_space=pl.ANY))
        aliases = {2: 0}
    return pl.pallas_call(
        value_grads_kernel,
        grid=(steps,),
        in_specs=in_specs,
        out_specs=pl.BlockSpec((block, width), lambda i: (turn * steps + i, 0)),
        out_shape=jax.ShapeDtypeStruct((own_rows, width), f32),
        input_output_aliases=aliases,
        compiler_params=params(58),
        cost_estimate=lasting(15 * 2 / turns),
        name="value_grads",
    )(*operands)


def pick_kernel(query_ref, table_ref, index_ref, out_ref):
    scores = mm(query_ref[...], table_ref[...], NT)
    index = index_ref[...]
    place = jnp.bitwise_and(index, LANES - 1)
    low = jnp.take_along_axis(scores[:, :LANES], place, axis=1)
    high = jnp.take_along_axis(scores[:, LANES:], place, axis=1)
    out_ref[...] = jnp.transpose(jnp.where(index < LANES, low, high))[:KPICK]


def pick_scores(query, table, index):
    rows = query.shape[0]
    block = 256
    return pl.pallas_call(
        pick_kernel,
        grid=(rows // block,),
        in_specs=[
            pl.BlockSpec((block, QHALF), lambda i: (i, 0)),
            pl.BlockSpec((NSUB, QHALF), lambda i: (0, 0)),
            pl.BlockSpec((block, LANES), lambda i: (i, 0)),
        ],
        out_specs=pl.BlockSpec((KPICK, block), lambda i: (0, i)),
        out_shape=jax.ShapeDtypeStruct((KPICK, rows), f32),
        compiler_params=params(16),
        cost_estimate=lasting(rows / 600),
        name="pick_scores",
    )(query, table, index)


def unpick_kernel(grad_ref, index_ref, table_ref, sub_ref, query_ref):
    count = grad_ref.shape[1]
    place = lax.broadcasted_iota(jnp.int32, (NSUB, count), 0)
    total = jnp.zeros((NSUB, count), f32)
    for pick in range(KPICK):
        hit = place == index_ref[pick : pick + 1, :]
        total = total + jnp.where(hit, grad_ref[pick : pick + 1, :], 0.0)
    low = total.astype(bf16)
    sub_ref[...] = low
    query_ref[...] = mm(low, table_ref[...], TN).astype(bf16)


def unpick_scores(grads, index, table):
    rows = grads.shape[1]
    block = 256
    return pl.pallas_call(
        unpick_kernel,
        grid=(rows // block,),
        in_specs=[
            pl.BlockSpec((KPICK, block), lambda i: (0, i)),
            pl.BlockSpec((KPICK, block), lambda i: (0, i)),
            pl.BlockSpec((NSUB, QHALF), lambda i: (0, 0)),
        ],
        out_specs=[
            pl.BlockSpec((NSUB, block), lambda i: (0, i)),
            pl.BlockSpec((block, QHALF), lambda i: (i, 0)),
        ],
        out_shape=[
            jax.ShapeDtypeStruct((NSUB, rows), bf16),
            jax.ShapeDtypeStruct((rows, QHALF), bf16),
        ],
        compiler_params=params(16),
        cost_estimate=lasting(rows / 180),
        name="unpick_scores",
    )(grads, index, table)


def products_kernel(dims, rows, *refs):
    left_ref, right_ref, keep_ref, send_ref = refs[-4:]
    if len(refs) > 4:
        place = lax.broadcasted_iota(jnp.int32, (2 * rows, refs[0].shape[1]), 0)
        home = place + pl.program_id(0) * 2 * rows == refs[0][...]
        left = mm(jnp.where(home, 1.0, 0.0).astype(bf16), left_ref[...]).astype(bf16)
    else:
        left = left_ref[...]
    product = mm(left, right_ref[...], dims).astype(bf16)
    keep_ref[0] = product[:rows]
    send_ref[0] = product[rows:]


def two_products(left, right, dims, rows, dealt_from=None):
    width = right.shape[1] if dims == NN else right.shape[0]
    operands = [left, right]
    in_specs = [
        pl.BlockSpec((2 * rows, left.shape[1]), lambda i: (i, 0)),
        pl.BlockSpec(right.shape, lambda i: (0, 0)),
    ]
    if dealt_from is not None:
        in_specs[0] = pl.BlockSpec(left.shape, lambda i: (0, 0))
        operands.insert(0, dealt_from[None, :])
        in_specs.insert(0, pl.BlockSpec((1, dealt_from.shape[0]), lambda i: (0, 0)))
    return pl.pallas_call(
        lambda *refs: products_kernel(dims, rows, *refs),
        grid=(TP // 2,),
        in_specs=in_specs,
        out_specs=[pl.BlockSpec((1, rows, width), lambda i: (i, 0, 0))] * 2,
        out_shape=[jax.ShapeDtypeStruct((TP // 2, rows, width), bf16)] * 2,
        compiler_params=params(16),
        cost_estimate=lasting(4),
        name="two_products",
    )(*operands)


def shards_kernel(splits, sums_ref, gain_ref, weight_refs, out_refs, gain_grad_ref):
    sources = sums_ref.shape[0]
    turned = jnp.zeros(gain_grad_ref.shape, f32)
    for part in range(TP):
        total = sums_ref[part].astype(f32)
        for more in range(part + TP, sources, TP):
            total = total + sums_ref[more].astype(f32)
        start = 0
        for (width, stride, offset), weight_ref, out_ref in zip(splits, weight_refs, out_refs):
            here = slice(offset + part * stride, offset + part * stride + width)
            piece = total[:, start : start + width]
            product = piece * weight_ref[:, here].astype(f32)
            turned = turned + jnp.sum(product, axis=1, keepdims=True)
            out_ref[:, here] = piece * gain_ref[...]
            start = start + width
    gain_grad_ref[...] = turned


def shard_grads(sums, gain, splits, *weights):
    rows = gain.shape[0]
    count = len(weights)
    owners = [min(at, count - 1) for at in range(len(splits))]

    def kernel(sums_ref, gain_ref, *refs):
        weight_refs = [refs[at] for at in owners]
        out_refs = [refs[count + at] for at in owners]
        shards_kernel(splits, sums_ref, gain_ref, weight_refs, out_refs, refs[-1])

    return pl.pallas_call(
        kernel,
        out_shape=[jax.ShapeDtypeStruct(weight.shape, f32) for weight in weights]
        + [jax.ShapeDtypeStruct((rows, 1), f32)],
        compiler_params=params(16),
        cost_estimate=lasting(3),
        name="shard_grads",
    )(sums, gain, *weights)


def swap(array, axes):
    return lax.all_to_all(array, axes, split_axis=0, concat_axis=0, tiled=True)


def gather(array, axes):
    return lax.all_gather(array, axes, axis=0, tiled=True)


def across(array, distance):
    return lax.ppermute(array, "tp", [(at, at ^ distance) for at in range(TP)])


def onward(array, count, step):
    pairs = [(at, at + step) for at in range(count) if 0 <= at + step < count]
    return lax.ppermute(array, GROUP, pairs)


def gather_hop(own):
    far = across(own, 6)
    return across(own, 2), across(own, 4), far


def gather_cores(own, near):
    quad = jnp.stack([own, *near])
    both = jnp.stack([quad, across(quad, 1)], axis=1)
    return both.reshape((TP * own.shape[0],) + own.shape[1:])


def gather_tp(own):
    return gather_cores(own, gather_hop(own))


def chip_send(sums):
    return sums[0], [across(sums[turn].astype(bf16), 2 * turn) for turn in (3, 1, 2)]


def chip_hop(keep, met):
    return chip_send(keep.astype(f32) + met.astype(f32))


def chip_call_kernel(keep_ref, met_ref, own_ref, *out_refs):
    own_ref[...] = keep_ref[0].astype(f32) + met_ref[0].astype(f32)
    for turn, out_ref in enumerate(out_refs):
        total = keep_ref[turn + 1].astype(f32) + met_ref[turn + 1].astype(f32)
        out_ref[...] = total.astype(bf16)


def chip_call(keep, met):
    chips, rows, width = keep.shape
    block = width // 2
    half = pl.BlockSpec((chips, rows, block), lambda i: (0, 0, i))
    out = pl.BlockSpec((rows, block), lambda i: (0, i))
    own, *sends = pl.pallas_call(
        chip_call_kernel,
        grid=(2,),
        in_specs=[half, half],
        out_specs=[out] * chips,
        out_shape=[jax.ShapeDtypeStruct((rows, width), f32)]
        + [jax.ShapeDtypeStruct((rows, width), bf16)] * (chips - 1),
        compiler_params=params(16),
        cost_estimate=lasting(1),
        name="chip_call",
    )(keep, met)
    return own, [across(sends[turn - 1], 2 * turn) for turn in (3, 1, 2)]


def last_hop(own, got):
    return own + sum(part.astype(f32) for part in got)


def sum_back(left, right, dims, rows):
    keep, send = two_products(left, right, dims, rows)
    return last_hop(*chip_call(keep, across(send, 1)))


def chip_sums(keep_ref, met_ref, chip, half):
    size = keep_ref.shape[2] // 2
    rows = slice(half * size, (half + 1) * size)
    return keep_ref[chip, 0, rows].astype(f32) + met_ref[chip, 0, rows].astype(f32)


def leave_kernel(keep_ref, met_ref, along_ref, aside_ref):
    for turn in range(2):
        along_ref[turn, 0] = chip_sums(keep_ref, met_ref, 2 * turn + 1, 0).astype(bf16)
        aside_ref[turn, 0] = chip_sums(keep_ref, met_ref, 2 + turn, 1).astype(bf16)


def pass_kernel(keep_ref, met_ref, along_ref, aside_ref, out_along_ref, out_aside_ref):
    along = chip_sums(keep_ref, met_ref, 2, 0) + along_ref[1, 0].astype(f32)
    aside = chip_sums(keep_ref, met_ref, 1, 1) + aside_ref[1, 0].astype(f32)
    out_along_ref[0] = along.astype(bf16)
    out_aside_ref[0] = aside.astype(bf16)


def total_kernel(keep_ref, met_ref, along_ref, aside_ref, far_ref, side_ref, out_ref):
    size = keep_ref.shape[2] // 2
    along = chip_sums(keep_ref, met_ref, 0, 0) + along_ref[0, 0].astype(f32)
    aside = chip_sums(keep_ref, met_ref, 0, 1) + aside_ref[0, 0].astype(f32)
    out_ref[0, :size] = (along + far_ref[0].astype(f32)).astype(bf16)
    out_ref[0, size:] = (aside + side_ref[0].astype(f32)).astype(bf16)


def hop_call(kernel, name, keep, outs, *operands):
    groups, rows = keep.shape[1:3]
    four = pl.BlockSpec((4, 1, rows, LANES), lambda i: (0, i, 0, 0))
    two = pl.BlockSpec((2, 1, rows // 2, LANES), lambda i: (0, i, 0, 0))
    one = pl.BlockSpec((1, rows // 2, LANES), lambda i: (i, 0, 0))
    whole = pl.BlockSpec((1, rows, LANES), lambda i: (i, 0, 0))
    specs = {"two": two, "one": one, "whole": whole}
    shapes = {
        "two": (2, groups, rows // 2, LANES),
        "one": (groups, rows // 2, LANES),
        "whole": (groups, rows, LANES),
    }
    return pl.pallas_call(
        kernel,
        grid=(groups,),
        in_specs=[four, four, two, two, one, one][: len(operands) + 1],
        out_specs=[specs[out] for out in outs],
        out_shape=[jax.ShapeDtypeStruct(shapes[out], bf16) for out in outs],
        compiler_params=params(16),
        cost_estimate=lasting(keep.size / 5e5),
        name=name,
    )(keep, *operands)


def sum_groups_start(total, groups, group_index):
    parts = [lax.dynamic_index_in_dim(total, group_index, 0, keepdims=False)]
    low = total.astype(bf16)
    for away in range(1, groups):
        piece = lax.dynamic_index_in_dim(
            low, lax.rem(group_index + away, groups), 0, keepdims=False
        )
        pairs = [(at, (at + away) % groups) for at in range(groups)]
        parts.append(lax.ppermute(piece, GROUP, pairs))
    return parts


def sum_groups(total, groups, group_index):
    return sum(part.astype(f32) for part in sum_groups_start(total, groups, group_index))


def shift(own, groups, away):
    return lax.ppermute(own, GROUP, [(at, (at + away) % groups) for at in range(groups)])


def by_group(own, shifts, groups, group_index):
    result = jnp.zeros((groups,) + own.shape, own.dtype)
    result = lax.dynamic_update_index_in_dim(result, own, group_index, 0)
    for away, piece in shifts.items():
        source = lax.rem(group_index + groups - away, groups)
        result = lax.dynamic_update_index_in_dim(result, piece, source, 0)
    return result


def rows_home(attn_parts, memory_sums, pairs):
    attn_sums = sum(part.astype(f32) for part in attn_parts).astype(bf16)
    memory_sums = memory_sums.reshape((2,) + attn_sums.shape)
    return lax.ppermute(jnp.concatenate([attn_sums[None], memory_sums]), ALL, pairs)


def tie(*arrays):
    return lax.optimization_barrier(arrays)


def norm_scale(hidden):
    return lax.rsqrt(jnp.mean(hidden * hidden, axis=-1, keepdims=True) + epsilon)


def norm_back(hidden, scale, weighted):
    coupled = jnp.mean(hidden * weighted, axis=-1, keepdims=True)
    return scale * weighted - hidden * (scale * scale * scale) * coupled


def body(
    inputs,
    attn_gain,
    attn_qkv,
    attn_out,
    memory_gain,
    memory_query,
    sub_keys,
    memory_gate,
    memory_out,
    memory_values,
    doc_lengths,
    token_order,
    memory_picks,
    cotangent,
):
    rows, width = inputs.shape
    outer = lax.axis_size("outer")
    heads = lax.axis_size("head")
    groups = heads * outer
    blocks = outer * TP
    devices = groups * TP
    share = rows // blocks
    fold = TP * share
    span = TP * rows
    tokens = token_order.shape[0]
    head_index = lax.axis_index("head")
    outer_index = lax.axis_index("outer")
    here = lax.axis_index("tp")
    here_word = here.astype(jnp.int32)[None]
    group_index = head_index * outer + outer_index
    rows_w = attn_qkv.shape[0]
    subs = memory_values.shape[0] // NSUB
    picks = MH * KPICK
    capacity = 2 * rows * picks // devices
    back = min(groups - 1, -(-(tokens // 2 - 1) // span))
    base = back * span

    near = gather_hop(inputs)
    row_cut = jnp.stack([attn_out, memory_out, sub_keys.reshape(rows_w, width)])
    own_cot, row_cut, *near = tie(cotangent, row_cut, *near)
    near_cot = gather_hop(own_cot)
    to_turned = [
        (groups * part + group, group * TP + part) for group in range(groups) for part in range(TP)
    ]
    from_turned = [(there, at) for at, there in to_turned]
    row_cut = lax.ppermute(row_cut, ALL, to_turned)
    group_inputs = gather_cores(inputs, near)
    gain_one = attn_gain.astype(f32)[:, None]
    gain_two = memory_gain.astype(f32)[:, None]
    scaled_qkv = (attn_qkv.astype(f32) * gain_one).astype(bf16)
    scaled_query = (memory_query.astype(f32) * gain_two).astype(bf16)
    scaled_gate = (memory_gate.astype(f32) * gain_two).astype(bf16)
    qkv_cut = jnp.transpose(scaled_qkv.reshape(rows_w, 3, TP, LANES), (2, 0, 1, 3))
    qkv_cut = jnp.broadcast_to(
        qkv_cut.reshape(1, TP, rows_w, 3 * LANES), (groups, TP, rows_w, 3 * LANES)
    ).reshape(devices, rows_w, 3 * LANES)
    weight_qkv = swap(qkv_cut, ALL).reshape(width, 3 * LANES)

    def columns(piece):
        return jnp.moveaxis(piece.reshape(rows_w, TP, -1), 1, 0)

    by_half = jnp.transpose(memory_picks.reshape(outer, fold, MH, KPICK, 2), (0, 2, 4, 3, 1))
    by_half = by_half.reshape(blocks, KPICK, fold).astype(bf16)
    rest_cut = jnp.concatenate([columns(scaled_query), columns(scaled_gate)], axis=2)
    rest_width = rest_cut.shape[2]

    laid = token_order.reshape(heads, blocks, outer, fold)
    mine = lax.dynamic_index_in_dim(laid, head_index, 0, keepdims=False)
    mine = lax.dynamic_index_in_dim(mine, outer_index, 1, keepdims=False)
    local = jnp.bitwise_xor(mine.reshape(span) - group_index * span, here * rows)
    span_range = jnp.arange(span, dtype=jnp.int32)
    deal = (local[:, None] == span_range[None, :]).astype(bf16)

    group_wide = group_inputs.astype(f32)
    normed_one = (group_wide * norm_scale(group_wide)).astype(bf16)
    projected = mm(normed_one, weight_qkv).astype(bf16)
    queries = projected[:, :LANES] * jnp.asarray(1.0 / math.sqrt(HD), bf16)
    kv_pieces = [projected[:, LANES:]]
    own_picks, rest_cut, by_half, kv_pieces[0] = tie(
        memory_picks, rest_cut, by_half, kv_pieces[0]
    )
    if back > 0:
        kv_pieces.insert(0, onward(kv_pieces[0], groups, 1))
    if by_half.shape[:2] == rest_cut.shape[:2]:
        both = swap(jnp.concatenate([rest_cut, by_half], axis=2), "tp")
        rest_rows, by_half = both[:, :, :rest_width], both[:, :, rest_width:]
    else:
        rest_rows, by_half = swap(rest_cut, "tp"), swap(by_half, BLK)
    rest_rows = rest_rows.reshape(TP * rows_w, rest_width)
    kv_pieces[0], row_cut, *near_cot = tie(kv_pieces[0], row_cut, *near_cot)
    for away in range(1, back):
        kv_pieces.insert(0, onward(kv_pieces[0], groups, 1))
    group_cot = gather_cores(own_cot, near_cot)

    first_pick = own_picks[:, :, :, 0].reshape(rows, picks)
    second_pick = own_picks[:, :, :, 1].reshape(rows, picks)
    owner = first_pick // subs
    device_range = jnp.arange(devices, dtype=jnp.int32)
    owned = (owner[None] == device_range[:, None, None]).astype(bf16)
    before = (
        jnp.arange(picks, dtype=jnp.int32)[:, None] < jnp.arange(picks, dtype=jnp.int32)[None, :]
    ).astype(bf16)
    before_rows = (
        jnp.arange(rows, dtype=jnp.int32)[:, None] < jnp.arange(rows, dtype=jnp.int32)[None, :]
    ).astype(bf16)
    in_row = jnp.einsum("dtk,kj->dtj", owned, before, preferred_element_type=f32)
    row_counts = jnp.sum(owned.astype(f32), axis=2)
    of_rows = jnp.dot(row_counts.astype(bf16), before_rows, preferred_element_type=f32)
    rank = jnp.sum(owned.astype(f32) * (in_row + of_rows[:, :, None]), axis=0).astype(jnp.int32)
    target = owner * capacity + rank
    target_high = target // LANES
    target_low = target % LANES
    places = devices * capacity
    entries = make_entries(target_high, target_low, first_pick % subs, second_pick, places)

    turned_one, unused = tie(jnp.transpose(normed_one), kv_pieces[0])
    keys_values, rest_rows, by_half, entries, turned_one, row_cut = tie(
        jnp.concatenate(kv_pieces, axis=0),
        rest_rows,
        by_half,
        entries,
        turned_one,
        row_cut,
    )
    half_index = jnp.moveaxis(by_half, 1, 0).reshape(KPICK, span).astype(jnp.int32)
    wide_index = jnp.pad(jnp.transpose(half_index), ((0, 0), (0, LANES - KPICK)))
    rest_shifts = {away: shift(rest_rows, groups, away) for away in range(1, groups, 2)}
    doc_ends = jnp.cumsum(doc_lengths)

    def lowest(inside):
        positions = group_index * span + inside
        starts = jnp.where(positions[:, None] >= doc_ends[None, :], doc_ends[None, :], 0)
        return jnp.max(starts, axis=1) - (group_index - back) * span

    low_first = lowest(span_range)
    low = lowest(jnp.bitwise_xor(span_range, here * rows))
    attended, lse, attended_low = attn_fwd(
        base, rows, (0, back + 1), low_first, here_word, low, queries, keys_values
    )
    split = back > 1
    near_bounds = (1 if split else 0, back + 1)
    far_kv = keys_values[:span]
    near_kv = keys_values[near_bounds[0] * span :]
    attn_shifts = {away: shift(row_cut[0], groups, away) for away in range(1, groups)}
    attended_low, group_cot, rest_rows, *shifted = tie(
        attended_low, group_cot, rest_rows, *attn_shifts.values(), *rest_shifts.values()
    )
    attn_shifts = dict(zip(attn_shifts, shifted))
    rest_shifts = dict(zip(rest_shifts, shifted[len(attn_shifts) :]))
    weight_attn = by_group(row_cut[0], attn_shifts, groups, group_index).reshape(LANES, width)
    even_shifts = {away: shift(rest_rows, groups, away) for away in range(2, groups, 2)}
    inputs_wide = inputs.astype(f32)
    hidden_one = inputs_wide + sum_back(attended_low, weight_attn, NN, rows)
    hidden_one, row_cut, *shifted = tie(hidden_one, row_cut, *even_shifts.values())
    rest_shifts.update(zip(even_shifts, shifted))
    weight_rest = by_group(rest_rows, rest_shifts, groups, group_index).reshape(width, rest_width)
    row_shifts = {away: shift(row_cut[1:], groups, away) for away in range(1, groups)}
    row_all = by_group(row_cut[1:], row_shifts, groups, group_index)
    row_all = jnp.moveaxis(row_all, 0, 1).reshape(2, LANES, width)
    weight_mixed = row_all[0]
    key_table = row_all[1].reshape(NSUB, QHALF)
    scale_two = norm_scale(hidden_one)
    dealt_cot = mm(deal, group_cot).astype(bf16)
    grad_mixed = mm(dealt_cot, weight_mixed, NT)
    normed_two = mm(deal, gather_tp((hidden_one * scale_two).astype(bf16))).astype(bf16)

    pre = mm(normed_two, weight_rest)
    query_mem = pre[:, :QHALF].astype(bf16)
    gate_pre = pre[:, QHALF:]
    gate_sig = jax.nn.sigmoid(gate_pre)
    grad_memory = (grad_mixed * gate_pre * gate_sig).astype(bf16)
    query_mem, grad_memory = tie(query_mem, grad_memory)
    every_grad = gather(grad_memory, ALL).reshape(heads, outer, TP, blocks, fold, LANES)
    picked_half = pick_scores(query_mem, key_table, wide_index).reshape(KPICK, blocks, fold)
    picked = swap(jnp.moveaxis(picked_half, 1, 0), BLK)
    turned_two, unused = tie(jnp.transpose(normed_two), picked_half)
    picked, turned_two = tie(picked, turned_two)
    picked = jnp.moveaxis(picked.reshape(outer, TP, KPICK, fold), 0, 2).reshape(TP, KPICK, rows)
    pick_weights, sent_weights = make_weights(picked, target_high, target_low, places)
    sent = jnp.concatenate([entries, sent_weights], axis=1)
    sent = jnp.moveaxis(sent.reshape(devices, capacity // LANES, 4, LANES), 2, 1)
    entries = swap(sent.reshape(devices, 4, capacity), ALL).astype(f32)
    entries = entries.reshape(heads, blocks, 4, 1, capacity)
    entry_token = entries[:, :, 0].astype(jnp.int32)
    entry_first = entries[:, :, 1].astype(jnp.int32)
    entry_second = entries[:, :, 2].astype(jnp.int32)
    entry_weight = entries[:, :, 3]

    turns = 2
    table = None
    leaving = []
    flat = (TP // 2, groups, span // turns, LANES)
    for turn in range(turns):
        table, keep, send = spread_weights(
            rows,
            subs,
            heads,
            outer,
            turn,
            turns,
            here_word,
            entry_token,
            entry_first,
            entry_second,
            entry_weight,
            memory_values,
            table,
        )
        leaving.append((keep.reshape(flat), across(send.reshape(flat), 1)))
    dots = []
    dense = None

    def more_dots(dense, *moved):
        if len(dots) == heads:
            return dense, moved
        part, dense = row_dots(
            rows,
            subs,
            len(dots),
            heads,
            outer,
            entry_token,
            entry_first,
            entry_second,
            every_grad,
            memory_values,
            dense,
        )
        part, dense, *moved = tie(part, dense, *moved)
        dots.append(part)
        return dense, moved

    def sums_call(kernel, name, outs, half, *operands):
        keep, met = leaving[half]
        return hop_call(kernel, name, keep, outs, met, *operands)

    leaves = sums_call(leave_kernel, "sums_first", ("two", "two"), 0)
    every_grad, *leaves = tie(every_grad, *leaves)
    first = [[across(leaves[0], 2), across(leaves[1], 4)]]
    dense, leaving[1] = more_dots(dense, *leaving[1])
    leaves = sums_call(leave_kernel, "sums_first", ("two", "two"), 1)
    dense, *leaves = tie(dense, *leaves)
    first.append([across(leaves[0], 2), across(leaves[1], 4)])
    dense, first[0] = more_dots(dense, *first[0])
    leaves = sums_call(pass_kernel, "sums_second", ("one", "one"), 0, *first[0])
    dense, *leaves = tie(dense, *leaves)
    second = [[across(leaves[0], 4), across(leaves[1], 2)]]
    dense, moved = more_dots(dense, *first[1], *second[0])
    first[1], second[0] = moved[:2], moved[2:]
    leaves = sums_call(pass_kernel, "sums_second", ("one", "one"), 1, *first[1])
    total = sums_call(total_kernel, "sums_last", ("whole",), 0, *first[0], *second[0])
    dense, *leaves = tie(dense, *leaves)
    second.append([across(leaves[0], 4), across(leaves[1], 2)])
    dense, second[1] = more_dots(dense, *second[1])
    while len(dots) < heads:
        dense, unused = more_dots(dense)
    total += sums_call(total_kernel, "sums_last", ("whole",), 1, *first[1], *second[1])
    total = jnp.concatenate(total, axis=1)
    memory = sum_groups(total, groups, group_index)

    entry_dots = jnp.concatenate(dots, axis=0).reshape(devices, capacity)
    returned = swap(entry_dots, ALL).reshape(places // LANES, LANES)
    table = table.reshape(tokens, subs * NSUB)
    dense = dense.reshape(-1, width)
    grad_values = value_grads(0, turns, table, dense, None)
    returned, grad_values = tie(returned, grad_values)
    grad_picked = pick_grads(target_high, target_low, pick_weights, returned)
    to_half = jnp.moveaxis(grad_picked.reshape(MH, KPICK, outer, fold), 2, 0)
    to_half = jnp.broadcast_to(to_half[:, :, None], (outer, MH, 2, KPICK, fold))
    grad_half = swap(to_half.reshape(blocks, KPICK, fold), BLK)
    grad_half = jnp.moveaxis(grad_half, 1, 0).reshape(KPICK, span)
    grad_sub, grad_query = unpick_scores(grad_half, half_index, key_table)

    mixed_low = (memory * gate_pre * gate_sig).astype(bf16)
    grad_gate = (grad_mixed * memory * gate_sig * (1.0 + gate_pre * (1.0 - gate_sig))).astype(bf16)
    grad_pre = jnp.concatenate([grad_query, grad_gate], axis=1)
    keep, send = two_products(grad_pre, weight_rest, NT, rows, local)
    met = across(send, 1)

    met, grad_pre, mixed_low, grad_sub = tie(met, grad_pre, mixed_low, grad_sub)
    own, got = chip_hop(keep, met)
    rest_grads = mm(turned_two, grad_pre).astype(bf16)
    row_grads = [mm(mixed_low, dealt_cot, TN), mm(grad_sub, query_mem).reshape(LANES, width)]
    row_grads = jnp.stack(row_grads).astype(bf16).reshape(2, groups, rows_w, width)
    row_grads = jnp.moveaxis(row_grads, 0, 1).reshape(groups * TP * rows_w, -1)
    memory_grads = jnp.concatenate([rest_grads, row_grads], axis=1)
    memory_grads, mixed_low, *got = tie(memory_grads, mixed_low, *got)
    memory_grads = lax.psum_scatter(memory_grads, GROUP, scatter_dimension=0, tiled=True)
    weighted_two = last_hop(own, got)
    grad_hidden = cotangent.astype(f32) + norm_back(hidden_one, scale_two, weighted_two)

    output_keep, output_met = two_products(mixed_low, weight_mixed, NN, rows, local)
    own_branch = grad_hidden.astype(bf16)
    near_branch = gather_hop(own_branch)
    output_keep, output_met, *near_branch = tie(output_keep, output_met, *near_branch)
    output_met = across(output_met, 1)
    grad_branch = gather_cores(own_branch, near_branch)
    grad_attended = mm(grad_branch, weight_attn, NT).astype(bf16)
    through = (low_first, here_word, low, queries)
    results = (lse, attended, grad_attended)
    far = far_grads = ()
    if split:
        far_grad_q, *far_grads = attn_bwd(base, rows, (0, 1), *through, far_kv, *results)
        far = (far_grad_q,)
        output_keep, output_met, far_grads[0] = tie(output_keep, output_met, far_grads[0])
        output_own, output_got = chip_hop(output_keep, output_met)
        attended_low, far_grads[0] = tie(attended_low, far_grads[0])
    attn_rows = mm(attended_low, grad_branch, TN).astype(bf16).reshape(groups, rows_w, width)
    attn_rows = sum_groups_start(attn_rows, groups, group_index)
    grad_q, *grad_kv = attn_bwd(base, rows, near_bounds, *through, near_kv, *results, far)
    grad_kv = [*far_grads, *grad_kv]
    if not split:
        output_own, output_got = chip_hop(output_keep, output_met)
    output_own, table, memory_grads, *near_grads = tie(
        output_own, table, memory_grads, *grad_kv[len(far_grads) :]
    )
    grad_kv = [*far_grads, *near_grads]

    row_home = None
    carry = grad_kv[0]
    for away in range(back):
        met = onward(carry, groups, -1)
        if away == back - 1:
            rest_home = swap(memory_grads[:, :rest_width].reshape(TP, rows_w, -1), "tp")
            grad_values = value_grads(1, turns, table, dense, grad_values)
            row_home = rows_home(attn_rows, memory_grads[:, rest_width:], from_turned)
            met, rest_home, row_home, grad_values, *output_got = tie(
                met, rest_home, row_home, grad_values, *output_got
            )
        if away == 0:
            met, memory_grads, table, *attn_rows = tie(met, memory_grads, table, *attn_rows)
        carry = (grad_kv[away + 1].astype(f32) + met.astype(f32)).astype(bf16)
    if back == 0:
        rest_home = swap(memory_grads[:, :rest_width].reshape(TP, rows_w, -1), "tp")
        row_home = rows_home(attn_rows, memory_grads[:, rest_width:], from_turned)
        grad_values = value_grads(1, turns, table, dense, grad_values)
    grad_projected = jnp.concatenate([grad_q, carry], axis=1)

    late_grads = mm(turned_one, grad_projected).astype(bf16)
    grad_projected, late_grads = tie(grad_projected, late_grads)
    qkv_home = swap(late_grads.reshape(devices, rows_w, 3 * LANES), ALL)
    keep, send = two_products(grad_projected, weight_qkv, NT, rows)
    sums = keep.astype(f32) + across(send, 1).astype(f32)
    own, got = chip_send(sums)
    weighted_one = last_hop(own, got)
    grad_inputs = grad_hidden + norm_back(inputs_wide, norm_scale(inputs_wide), weighted_one)
    output = (hidden_one + last_hop(output_own, output_got)).astype(bf16)
    row_home = row_home.astype(f32)
    splits = ((QHALF, QHALF, 0), (LANES, LANES, 0))
    grad_query_home, grad_gate_home, grad_memory_gain = shard_grads(
        rest_home, gain_two, splits, memory_query, memory_gate
    )
    splits = tuple((LANES, LANES, part * width) for part in range(3))
    grad_qkv_home, grad_attn_gain = shard_grads(qkv_home, gain_one, splits, attn_qkv)
    return (
        output,
        grad_inputs,
        grad_attn_gain.reshape(-1),
        grad_qkv_home,
        row_home[0],
        grad_memory_gain.reshape(-1),
        grad_query_home,
        row_home[2].reshape(sub_keys.shape),
        grad_gate_home,
        row_home[1],
        grad_values,
    )


def solution(mesh):
    heads, blocks = mesh.devices.shape
    cut_mesh = Mesh(mesh.devices.reshape(heads, blocks // TP, TP), ALL)
    matrix = P(ALL, None)
    in_specs = (
        matrix,
        P(ALL),
        matrix,
        matrix,
        P(ALL),
        matrix,
        matrix,
        matrix,
        matrix,
        matrix,
        P(),
        P(),
        P(ALL, None, None, None),
        matrix,
    )
    out_specs = (
        matrix,
        matrix,
        P(ALL),
        matrix,
        matrix,
        P(ALL),
        matrix,
        matrix,
        matrix,
        matrix,
        matrix,
    )
    return jax.shard_map(
        body, mesh=cut_mesh, in_specs=in_specs, out_specs=out_specs, check_vma=False
    )
```
